256 devices in a mesh: seq: 64 (over z, y, core), mp: 4 (over x).
Axes of the slice: x: 4, y: 4, z: 8, core: 2. Of those that a mesh axis runs over, the one named last changes fastest.
Arguments:
- latents: bfloat16 [128, 128, 256], P('seq'), may hold values from -6 to 6
- conv_w: bfloat16 [3, 3, 256, 256], P(None, None, None, 'mp'), may hold values from -0.125 to 0.125
- embed_w: bfloat16 [4, 256, 4096], P(None, 'mp', 'seq'), may hold values from -0.1875 to 0.1875
- text_emb: bfloat16 [8192, 4096], P('seq', 'mp'), may hold values from -6 to 6
- wqkv: bfloat16 [4096, 3, 2048], P(None, None, 'mp'), may hold values from -2 to 2
- seg_ids: int32 [8192], replicated, may hold values from 0 to 1, as said below
Outputs:
- attn: bfloat16 [8192, 2048], P('seq', 'mp')
The draws below stay inside these ranges and needn't reach their ends.
Inputs may be any that keep to these rules, and one draw needn't show every extreme that they name: `seg_ids`: image n occupies one run of 4096 positions that starts at a multiple of 64; runs come in the order of n and every image is present; 0 marks text.
All inputs are finite; a program needn't handle non-finite values.
Results may differ from the reference program's by a relative error of at most 0.015.
The reference program's roundings to bfloat16 on the way count: a program that leaves them out, or rounds other values in their place, can miss the bound.
Values may be sent and summed in bfloat16 or wider, within the bound.
No kernel may reach another device: no remote copies, remote signals or barrier semaphores. Data moves between devices by JAX's collectives and lax.ppermute only.
A program may use at most 128 MiB of HBM per device.

```python
import math
import jax
import jax.numpy as jnp
from jax import lax

D = 4096
HEADS = 16
HD = 128
C = 256
PCOLS = 64
IMG_ROWS = 64
SEQLEN = 8192
NIMG = 1


def draw_seg_ids(key, part):
    key = jax.random.fold_in(key, 11)
    units = SEQLEN // PCOLS
    spare = units - NIMG * IMG_ROWS
    offsets = jnp.sort(jax.random.randint(key, (NIMG,), 0, spare + 1))
    starts = offsets * PCOLS + jnp.arange(NIMG, dtype=jnp.int32) * (IMG_ROWS * PCOLS)
    positions = jnp.arange(SEQLEN, dtype=jnp.int32)
    inside = (positions[None, :] >= starts[:, None]) & (positions[None, :] < starts[:, None] + IMG_ROWS * PCOLS)
    labels = jnp.arange(1, NIMG + 1, dtype=jnp.int32)
    return jnp.sum(jnp.where(inside, labels[:, None], 0), axis=0).astype(jnp.int32)


def shared_basis(key):
    basis_key = jax.random.fold_in(key, 29)
    first_key, second_key, third_key = jax.random.split(basis_key, 3)
    query_sign = (2 * jax.random.randint(first_key, (D,), 0, 2) - 1).astype(jnp.float32)
    key_sign = (2 * jax.random.randint(second_key, (D,), 0, 2) - 1).astype(jnp.float32)
    head_dirs = jnp.clip(jax.random.normal(third_key, (HEADS, HD), jnp.float32), -3.0, 3.0)
    return (query_sign, key_sign, head_dirs)


def chosen_rows(key, part):
    segments = draw_seg_ids(key, part)
    row_key = jax.random.fold_in(key, 31)
    positions = jnp.arange(SEQLEN, dtype=jnp.int32)
    ranks = jax.random.randint(row_key, (SEQLEN,), 0, 1024)
    marks = jnp.where(segments == 0, ranks * SEQLEN + positions, -1)
    picked = lax_top(marks)
    return picked


def lax_top(marks):
    return jax.lax.top_k(marks, 20)[1].astype(jnp.int32)


def draw_text_emb(key, part):
    query_sign, key_sign, head_dirs = shared_basis(key)
    picked = chosen_rows(key, part)
    key = jax.random.fold_in(key, 17)
    drawn_key, strength_key, query_key = jax.random.split(key, 3)
    drawn = jnp.clip(jax.random.normal(drawn_key, (SEQLEN, D), jnp.float32), -6.0, 6.0)
    key_strength = jax.random.uniform(strength_key, (16,), jnp.float32, 0.9, 1.1)
    query_strength = jax.random.uniform(query_key, (4,), jnp.float32, 2.5, 3.5)
    positions = jnp.arange(SEQLEN, dtype=jnp.int32)
    key_hit = positions[:, None] == picked[None, :16]
    query_hit = positions[:, None] == picked[None, 16:]
    key_scale = jnp.sum(jnp.where(key_hit, key_strength[None, :], 0.0), axis=1)
    query_scale = jnp.sum(jnp.where(query_hit, query_strength[None, :], 0.0), axis=1)
    is_key = jnp.any(key_hit, axis=1)
    is_query = jnp.any(query_hit, axis=1)
    rows = jnp.where(is_key[:, None], key_scale[:, None] * key_sign[None, :] + 0.3 * drawn, drawn)
    rows = jnp.where(is_query[:, None], query_scale[:, None] * query_sign[None, :], rows)
    return rows.astype(jnp.bfloat16)


def draw_wqkv(key, part):
    query_sign, key_sign, head_dirs = shared_basis(key)
    key = jax.random.fold_in(key, 23)
    base = jnp.clip(jax.random.normal(key, (D, 3, HEADS * HD), jnp.float32), -6.0, 6.0) * D ** (-0.5)
    part_gain = jnp.array([1.7, 1.7, 1.0], jnp.float32)
    base = base * part_gain[None, :, None]
    query_gain = 0.115 * math.sqrt(D)
    key_gain = 1.0
    flat_dirs = head_dirs.reshape(HEADS * HD)
    query_part = query_gain / D * query_sign[:, None] * flat_dirs[None, :]
    key_part = key_gain / D * key_sign[:, None] * flat_dirs[None, :]
    planted = jnp.stack([query_part, key_part, jnp.zeros_like(query_part)], axis=1)
    return (base + planted).astype(jnp.bfloat16)


def block_levels(key, dims, cuts, low, high):
    gain = 1.0
    for axis_at, parts in cuts:
        steps = jax.random.uniform(jax.random.fold_in(jax.random.fold_in(key, 6), axis_at), (parts,), jnp.float32, low / len(cuts), high / len(cuts))
        gain = gain * jnp.repeat(jnp.exp(steps), dims[axis_at] // parts).reshape((-1,) + (1,) * (len(dims) - 1 - axis_at))
    return gain


def centred(stream_key, dims, deviation, limit, cuts=(), kind=jnp.bfloat16):
    factor_of = block_levels(stream_key, dims, cuts, -0.22, 0.18) if cuts else 1.0
    values = jax.random.normal(stream_key, dims, jnp.float32) * deviation * factor_of
    return jnp.minimum(jnp.maximum(values, -limit), limit).astype(kind)


def setup_inputs(seed: int = 0) -> dict:
    streams_of = jax.random.split(jax.random.key(seed), 7)
    return {
        "latents": centred(streams_of[0], (NIMG * 2 * IMG_ROWS, 2 * PCOLS, C), 1.0, 6.0, ((0, 64),)),
        "conv_w": centred(streams_of[1], (3, 3, C, C), (9 * C) ** -0.5, 0.125, ((3, 4),)),
        "embed_w": centred(streams_of[2], (4, C, D), (4 * C) ** -0.5, 0.1875, ((1, 4), (2, 64))),
        "text_emb": draw_text_emb(jax.random.fold_in(streams_of[6], 71), 0),
        "wqkv": draw_wqkv(jax.random.fold_in(streams_of[6], 71), 0),
        "seg_ids": draw_seg_ids(jax.random.fold_in(streams_of[6], 71), 0),
    }


def image_starts(seg_ids):
    positions = jnp.arange(SEQLEN, dtype=jnp.int32)
    labels = jnp.arange(1, NIMG + 1, dtype=jnp.int32)
    marks = seg_ids[None, :] == labels[:, None]
    return jnp.min(jnp.where(marks, positions[None, :], SEQLEN), axis=1).astype(jnp.int32)


def down_block(latents, conv_w):
    images = latents.reshape(NIMG, 2 * IMG_ROWS, 2 * PCOLS, C)
    padded = jnp.pad(images, ((0, 0), (1, 1), (1, 1), (0, 0)))
    summed = jnp.zeros((NIMG, 2 * IMG_ROWS, 2 * PCOLS, C), jnp.float32)
    for row_step in range(3):
        for col_step in range(3):
            window = padded[:, row_step:row_step + 2 * IMG_ROWS, col_step:col_step + 2 * PCOLS, :]
            summed = summed + jnp.einsum("nhwc,cd->nhwd", window.astype(jnp.float32), conv_w[row_step, col_step].astype(jnp.float32))
    return (images.astype(jnp.float32) + jax.nn.silu(summed)).astype(jnp.bfloat16)


def reference(latents, conv_w, embed_w, text_emb, wqkv, seg_ids):
    mixed = down_block(latents, conv_w)
    tiles = mixed.reshape(NIMG, IMG_ROWS, 2, PCOLS, 2, C).transpose(0, 1, 3, 2, 4, 5).reshape(NIMG * IMG_ROWS * PCOLS, 4 * C)
    embedded = jnp.dot(tiles, embed_w.reshape(4 * C, D), preferred_element_type=jnp.float32).astype(jnp.bfloat16)
    starts = image_starts(seg_ids)
    inner = jnp.arange(IMG_ROWS * PCOLS, dtype=jnp.int32)
    targets = (starts[:, None] + inner[None, :]).reshape(-1)
    hidden = text_emb.at[targets].set(embedded)
    qkv = jnp.dot(hidden, wqkv.reshape(D, 3 * HEADS * HD), preferred_element_type=jnp.float32).astype(jnp.bfloat16)
    qkv = qkv.reshape(SEQLEN, 3, HEADS, HD)
    queries = qkv[:, 0].astype(jnp.float32)
    keys = qkv[:, 1].astype(jnp.float32)
    values = qkv[:, 2].astype(jnp.float32)
    block_rows = 512 if SEQLEN % 512 == 0 else SEQLEN
    key_pos = jnp.arange(SEQLEN, dtype=jnp.int32)
    scale = HD ** -0.5

    def attend(block):
        first = (block * block_rows).astype(jnp.int32)
        query_blk = lax.dynamic_slice_in_dim(queries, first, block_rows, 0)
        query_pos = first + jnp.arange(block_rows, dtype=jnp.int32)
        query_seg = lax.dynamic_slice_in_dim(seg_ids, first, block_rows, 0)
        allowed = (key_pos[None, :] <= query_pos[:, None]) | ((query_seg[:, None] == seg_ids[None, :]) & (query_seg[:, None] > 0))
        scores = jnp.einsum("qhd,khd->hqk", query_blk, keys) * scale
        scores = jnp.where(allowed[None], scores, -1e30)
        highest = jnp.max(scores, axis=-1)
        weights = jnp.where(allowed[None], jnp.exp(scores - highest[..., None]), 0.0)
        totals = jnp.sum(weights, axis=-1)
        probs = lax.optimization_barrier(weights.astype(jnp.bfloat16)).astype(jnp.float32)
        result = jnp.einsum("hqk,khd->hqd", probs, values) / totals[..., None]
        return result.transpose(1, 0, 2).reshape(block_rows, HEADS * HD).astype(jnp.bfloat16)

    blocks = lax.map(attend, jnp.arange(SEQLEN // block_rows, dtype=jnp.int32))
    return blocks.reshape(SEQLEN, HEADS * HD)
```

```python
import math

import jax
import jax.numpy as jnp
from jax import lax
from jax.experimental import pallas as pl
from jax.experimental.pallas import tpu as pltpu
from jax.sharding import Mesh
from jax.sharding import PartitionSpec as P

NZ, NY, NC, NX = 8, 4, 2, 4
HD = 128
TOK = 128
IMG = 4096
SEQ = ("z", "y", "c")
SIZES = {"z": NZ, "y": NY, "c": NC, "mp": NX}
BF = jnp.bfloat16
F32 = jnp.float32


def shift(value, axis, step):
    count = SIZES[axis]
    return lax.ppermute(value, axis, [(i, (i + step) % count) for i in range(count)])


def ordered(pieces, first):
    count = len(pieces)
    twice = jnp.stack(pieces + pieces)
    return lax.dynamic_slice_in_dim(twice, (count - first) % count, count, 0)


def gather_z(block):
    half = block.shape[0] // 2
    below, above = shift(block, "z", 1), shift(block, "z", -1)
    below_2, above_2 = shift(block, "z", 2), shift(block, "z", -2)
    first = [(0, block), (-1, below), (1, above), (-2, below_2), (2, above_2)]
    below_3, above_3 = shift(below_2, "z", 1), shift(above_2, "z", -1)
    far = jnp.concatenate(
        [shift(below_2[:half], "z", 2), shift(above_2[half:], "z", -2)], axis=0
    )
    return first, [(-3, below_3), (3, above_3), (4, far)]


def embed_weight(embed_w, y):
    cells = embed_w.reshape(2, 128, 64)
    packed = jnp.concatenate([cells[0], cells[1]], axis=1)
    pieces = []
    for t in range(4):
        perm = []
        for src_y in range(NY):
            for src_c in range(NC):
                for src_x in range(NX):
                    dst_y = (2 * (src_x % 2) + src_c - t) % 4
                    perm.append(
                        (src_y * 8 + src_c * 4 + src_x, dst_y * 8 + (src_x // 2) * 4 + src_y)
                    )
        pieces.append(lax.ppermute(packed, ("y", "c", "mp"), perm))
    pieces = ordered(pieces, y)
    block = pieces.reshape(2, 2, 128, 2, 64).transpose(0, 3, 2, 1, 4).reshape(512, 128)
    return gather_z(block)


def placed_patches(patches, unit):
    low = (unit // 2) % 4
    odd = unit % 2

    def spread(low_shift, parity):
        def branch(rows):
            even = lax.ppermute(rows, SEQ, [(s, low_shift + s // 2) for s in range(0, 64, 2)])
            other = lax.ppermute(
                rows, SEQ, [(s, low_shift + parity + s // 2) for s in range(1, 64, 2)]
            )
            return jnp.concatenate([other, even] if parity else [even, other], axis=0)

        return branch

    rows = lax.switch(low * 2 + odd, [spread(i // 2, i % 2) for i in range(8)], patches)

    def moved(high):
        def branch(rows):
            if high == 0:
                return rows
            return lax.ppermute(rows, SEQ, [(s, (s + 4 * high) % 64) for s in range(64)])

        return branch

    return lax.switch(unit // 8, [moved(i) for i in range(9)], rows)


def attend_kernel(groups, first_call, last_call, *refs):
    info = refs[0]
    z, y, c, start = info[0], info[1], info[2], info[3]
    q_ref = refs[1]
    kv_refs = refs[2 : 2 + len(groups)]
    rest = refs[2 + len(groups) :]
    count = q_ref.shape[0]
    factor = HD**-0.5 * math.log2(math.e)
    if first_call:
        top = jnp.full((1, count), -1e30, F32)
        total = jnp.zeros((1, count), F32)
        acc = jnp.zeros((HD, count), F32)
    else:
        top, total, acc = rest[0][0:1, :], rest[0][8:9, :], rest[0][16:, :]
        rest = rest[1:]
    lanes = lax.broadcasted_iota(jnp.int32, (1, TOK), 1)
    limits = []
    for j in range(NY):
        pos = z * 1024 + lax.rem(y - j + NY, NY) * 256 + c * TOK + lanes
        inside = (pos >= start) & (pos < start + IMG)
        limits.append(jnp.where(inside, start + (IMG - 1), pos))
    limit = jnp.concatenate(limits, axis=1)
    rows = lax.broadcasted_iota(jnp.int32, (TOK, count), 0)
    queries = q_ref[...]
    for kv_ref, (offsets, own_core) in zip(kv_refs, groups):
        core = c if own_core else 1 - c
        for at, offset in enumerate(offsets):
            zone = lax.rem(z + offset + NZ, NZ)
            block = kv_ref[at * 512 : (at + 1) * 512, :]
            scores = lax.dot_general(
                block[:, :HD], queries, (((1,), (1,)), ((), ())), preferred_element_type=F32
            )
            parts = []
            for j in range(NY):
                base = zone * 1024 + lax.rem(y - j + NY, NY) * 256 + core * TOK
                visible = rows <= limit - base
                parts.append(jnp.where(visible, scores[j * TOK : (j + 1) * TOK], -1e30))
            scores = jnp.concatenate(parts, axis=0)
            higher = jnp.maximum(top, jnp.max(scores, axis=0, keepdims=True))
            fade = jnp.exp2((top - higher) * factor)
            weights = jnp.exp2((scores - higher) * factor)
            total = total * fade + jnp.sum(weights, axis=0, keepdims=True)
            acc = acc * fade + lax.dot_general(
                block[:, HD:],
                weights.astype(BF),
                (((0,), (0,)), ((), ())),
                preferred_element_type=F32,
            )
            top = higher
    out_ref = rest[0]
    if last_call:
        out_ref[...] = (acc / total).T.astype(BF)
    else:
        out_ref[0:8, :] = jnp.broadcast_to(top, (8, count))
        out_ref[8:16, :] = jnp.broadcast_to(total, (8, count))
        out_ref[16:, :] = acc


def attend(info, queries, groups, carry, last_call):
    import functools

    arrays = [array for array, _, _ in groups]
    shape = [(offsets, own) for _, offsets, own in groups]
    operands = [info, queries] + arrays + ([] if carry is None else [carry])
    vmem = pl.BlockSpec(memory_space=pltpu.VMEM)
    count = queries.shape[0]
    keys = sum(a.shape[0] for a in arrays)
    if last_call:
        out = jax.ShapeDtypeStruct((count, HD), BF)
    else:
        out = jax.ShapeDtypeStruct((HD + 16, count), F32)
    return pl.pallas_call(
        functools.partial(attend_kernel, shape, carry is None, last_call),
        out_shape=out,
        in_specs=[pl.BlockSpec(memory_space=pltpu.SMEM)] + [vmem] * (len(operands) - 1),
        out_specs=vmem,
        compiler_params=pltpu.CompilerParams(vmem_limit_bytes=40 * 1024 * 1024),
        cost_estimate=pl.CostEstimate(
            flops=4 * count * keys * HD,
            bytes_accessed=keys * 512,
            transcendentals=count * keys,
        ),
    )(*operands)


def shards(latents, conv_w, embed_w, text_emb, wqkv, seg_ids):
    z, y, c, x = (lax.axis_index(a) for a in ("z", "y", "c", "mp"))
    place = z * 8 + y * 2 + c
    positions = jnp.arange(seg_ids.shape[0], dtype=jnp.int32)
    start = jnp.min(jnp.where(seg_ids == 1, positions, seg_ids.shape[0])).astype(jnp.int32)

    near_w, far_w = embed_weight(embed_w, y)

    top = lax.ppermute(latents[1:], SEQ, [(i, i + 1) for i in range(63)])
    bottom = lax.ppermute(latents[:1], SEQ, [(i + 1, i) for i in range(63)])
    rows = jnp.concatenate([top, latents, bottom], axis=0)
    conv = lax.conv_general_dilated(
        rows[None],
        conv_w,
        (1, 1),
        ((0, 0), (1, 1)),
        dimension_numbers=("NHWC", "HWIO", "NHWC"),
        preferred_element_type=F32,
    )[0]
    own = lax.dynamic_slice_in_dim(latents, x * 64, 64, 2)
    mixed = (own.astype(F32) + jax.nn.silu(conv)).astype(BF)
    patches = mixed.reshape(2, 64, 2, 64).transpose(1, 0, 2, 3).reshape(64, 256)
    patches = placed_patches(patches, start // 64)
    patches = ordered([patches] + [shift(patches, "mp", -t) for t in (1, 2, 3)], x)
    patches = patches.transpose(1, 0, 2).reshape(TOK, 1024)

    texts = ordered([text_emb] + [shift(text_emb, "mp", -t) for t in (1, 2, 3)], x)
    texts = texts.transpose(1, 0, 2).reshape(TOK, 4096)

    blocks = []
    for group in (near_w, far_w):
        mine = jnp.concatenate([w for _, w in group], axis=1)
        other = shift(mine, "c", 1)
        lower = jnp.where(c == 0, mine, other)
        upper = jnp.where(c == 0, other, mine)
        part = jnp.dot(patches[:, :512], lower, preferred_element_type=F32)
        part = part + jnp.dot(patches[:, 512:], upper, preferred_element_type=F32)
        part = part.astype(BF)
        for i, (offset, _) in enumerate(group):
            blocks.append((offset % NZ, part[:, i * 128 : (i + 1) * 128]))
    blocks = [b for _, b in sorted(blocks, key=lambda pair: pair[0])]
    twice = jnp.concatenate(blocks + blocks, axis=1)
    columns = lax.dynamic_slice_in_dim(twice, ((NZ - z) % NZ) * 128, 1024, 1)
    embedded = ordered([columns] + [shift(columns, "mp", -t) for t in (1, 2, 3)], x)
    embedded = embedded.reshape(NX, TOK, NZ, 128).transpose(1, 2, 0, 3).reshape(TOK, 4096)

    my_pos = place * TOK + jnp.arange(TOK, dtype=jnp.int32)
    is_text = (my_pos < start) | (my_pos >= start + IMG)
    hidden = jnp.where(is_text[:, None], texts, embedded)

    qkv = jnp.dot(hidden, wqkv.reshape(4096, 1536), preferred_element_type=F32).astype(BF)
    by_head = qkv.reshape(TOK, 3, 4, HD).transpose(2, 0, 1, 3).reshape(4, TOK, 3 * HD)
    parts = []
    for t in range(NY):
        part = lax.dynamic_index_in_dim(by_head, (y + t) % NY, 0, keepdims=False)
        parts.append(part if t == 0 else shift(part, "y", t))
    head = jnp.concatenate(parts, axis=0)
    queries, keys_values = head[:, :HD], head[:, HD:]

    info = jnp.stack([z, y, c, start]).astype(jnp.int32)
    carry = None
    near, far = gather_z(keys_values)
    for group, last in ((near, False), (far, True)):
        mine = jnp.concatenate([b for _, b in group], axis=0)
        other = shift(mine, "c", 1)
        offsets = tuple(o for o, _ in group)
        carry = attend(info, queries, [(mine, offsets, True), (other, offsets, False)], carry, last)
    back = [carry[:TOK]]
    for t in range(1, NY):
        back.append(shift(carry[t * TOK : (t + 1) * TOK], "y", -t))
    return ordered(back, y).transpose(1, 0, 2).reshape(TOK, 4 * HD)


def solution(mesh):
    inner = Mesh(mesh.devices.reshape(NZ, NY, NC, NX), ("z", "y", "c", "mp"))
    return jax.shard_map(
        shards,
        mesh=inner,
        in_specs=(
            P(SEQ, None, None),
            P(None, None, None, "mp"),
            P(None, "mp", SEQ),
            P(SEQ, "mp"),
            P(None, None, "mp"),
            P(),
        ),
        out_specs=P(SEQ, "mp"),
        check_vma=False,
    )
```

```python
import math

import jax
import jax.numpy as jnp
from jax import lax
from jax.experimental import pallas as pl
from jax.experimental.pallas import tpu as pltpu
from jax.sharding import Mesh
from jax.sharding import PartitionSpec as P

NZ, NY, NC, NX = 8, 4, 2, 4
HD = 128
TOK = 128
IMG = 4096
SEQ = ("z", "y", "c")
SIZES = {"z": NZ, "y": NY, "c": NC, "mp": NX}
BF = jnp.bfloat16
F32 = jnp.float32


def shift(value, axis, step):
    count = SIZES[axis]
    return lax.ppermute(value, axis, [(i, (i + step) % count) for i in range(count)])


def ordered(pieces, first):
    count = len(pieces)
    twice = jnp.stack(pieces + pieces)
    return lax.dynamic_slice_in_dim(twice, (count - first) % count, count, 0)


def gather_z(block):
    half = block.shape[0] // 2
    below, above = shift(block, "z", 1), shift(block, "z", -1)
    below_2, above_2 = shift(block, "z", 2), shift(block, "z", -2)
    first = [(0, block), (-1, below), (1, above), (-2, below_2), (2, above_2)]
    below_3, above_3 = shift(below_2, "z", 1), shift(above_2, "z", -1)
    far = jnp.concatenate(
        [shift(below_2[:half], "z", 2), shift(above_2[half:], "z", -2)], axis=0
    )
    return first, [(-3, below_3), (3, above_3), (4, far)]


def embed_weight(embed_w, y):
    cells = embed_w.reshape(2, 128, 64)
    packed = jnp.concatenate([cells[0], cells[1]], axis=1)
    pieces = []
    for t in range(4):
        perm = []
        for src_y in range(NY):
            for src_c in range(NC):
                for src_x in range(NX):
                    dst_y = (2 * (src_x % 2) + src_c - t) % 4
                    perm.append(
                        (src_y * 8 + src_c * 4 + src_x, dst_y * 8 + (src_x // 2) * 4 + src_y)
                    )
        pieces.append(lax.ppermute(packed, ("y", "c", "mp"), perm))
    pieces = ordered(pieces, y)
    block = pieces.reshape(2, 2, 128, 2, 64).transpose(0, 3, 2, 1, 4).reshape(512, 128)
    return gather_z(block)


def placed_patches(pair, unit):
    low = (unit // 2) % 4
    odd = unit % 2

    def spread(low_shift, parity):
        moves = [(s, low_shift + (s + parity) // 2) for s in range(parity, 64, 2)]
        if parity:
            moves.append((0, low_shift))
        return lambda rows: lax.ppermute(rows, SEQ, moves)

    rows = lax.switch(low * 2 + odd, [spread(i // 2, i % 2) for i in range(8)], pair)

    def moved(high):
        if high == 0:
            return lambda rows: rows
        if high % 2 == 0:
            return lambda rows: shift(rows, "z", high // 2)
        return lambda rows: lax.ppermute(rows, SEQ, [(s, (s + 4 * high) % 64) for s in range(64)])

    return lax.switch(unit // 8, [moved(i) for i in range(9)], rows)


def attend_kernel(groups, first_call, last_call, *refs):
    info = refs[0]
    z, y, c, start = info[0], info[1], info[2], info[3]
    q_ref = refs[1]
    kv_refs = refs[2 : 2 + len(groups)]
    rest = refs[2 + len(groups) :]
    count = q_ref.shape[0]
    factor = HD**-0.5 * math.log2(math.e)
    if first_call:
        top = jnp.full((1, count), -1e30, F32)
        total = jnp.zeros((1, count), F32)
        acc = jnp.zeros((HD, count), F32)
    else:
        top, total, acc = rest[0][0:1, :], rest[0][8:9, :], rest[0][16:, :]
        rest = rest[1:]
    lanes = lax.broadcasted_iota(jnp.int32, (1, TOK), 1)
    limits = []
    for j in range(NY):
        pos = z * 1024 + lax.rem(y - j + NY, NY) * 256 + c * TOK + lanes
        inside = (pos >= start) & (pos < start + IMG)
        limits.append(jnp.where(inside, start + (IMG - 1), pos))
    limit = jnp.concatenate(limits, axis=1)
    rows = lax.broadcasted_iota(jnp.int32, (TOK, count), 0)
    queries = q_ref[...]
    for kv_ref, (offsets, own_core) in zip(kv_refs, groups):
        core = c if own_core else 1 - c
        for at, offset in enumerate(offsets):
            zone = lax.rem(z + offset + NZ, NZ)
            block = kv_ref[at * 512 : (at + 1) * 512, :]
            scores = lax.dot_general(
                block[:, :HD], queries, (((1,), (1,)), ((), ())), preferred_element_type=F32
            )
            parts = []
            for j in range(NY):
                base = zone * 1024 + lax.rem(y - j + NY, NY) * 256 + core * TOK
                visible = rows <= limit - base
                parts.append(jnp.where(visible, scores[j * TOK : (j + 1) * TOK], -1e30))
            scores = jnp.concatenate(parts, axis=0)
            higher = jnp.maximum(top, jnp.max(scores, axis=0, keepdims=True))
            fade = jnp.exp2((top - higher) * factor)
            weights = jnp.exp2((scores - higher) * factor)
            total = total * fade + jnp.sum(weights, axis=0, keepdims=True)
            acc = acc * fade + lax.dot_general(
                block[:, HD:],
                weights.astype(BF),
                (((0,), (0,)), ((), ())),
                preferred_element_type=F32,
            )
            top = higher
    out_ref = rest[0]
    if last_call:
        out_ref[...] = (acc / total).T.astype(BF)
    else:
        out_ref[0:8, :] = jnp.broadcast_to(top, (8, count))
        out_ref[8:16, :] = jnp.broadcast_to(total, (8, count))
        out_ref[16:, :] = acc


def attend(info, queries, groups, carry, last_call):
    import functools

    arrays = [array for array, _, _ in groups]
    shape = [(offsets, own) for _, offsets, own in groups]
    operands = [info, queries] + arrays + ([] if carry is None else [carry])
    vmem = pl.BlockSpec(memory_space=pltpu.VMEM)
    count = queries.shape[0]
    keys = sum(a.shape[0] for a in arrays)
    if last_call:
        out = jax.ShapeDtypeStruct((count, HD), BF)
    else:
        out = jax.ShapeDtypeStruct((HD + 16, count), F32)
    return pl.pallas_call(
        functools.partial(attend_kernel, shape, carry is None, last_call),
        out_shape=out,
        in_specs=[pl.BlockSpec(memory_space=pltpu.SMEM)] + [vmem] * (len(operands) - 1),
        out_specs=vmem,
        compiler_params=pltpu.CompilerParams(vmem_limit_bytes=40 * 1024 * 1024),
        cost_estimate=pl.CostEstimate(
            flops=4 * count * keys * HD,
            bytes_accessed=keys * 512,
            transcendentals=count * keys,
        ),
    )(*operands)


def shards(latents, conv_w, embed_w, text_emb, wqkv, seg_ids):
    z, y, c, x = (lax.axis_index(a) for a in ("z", "y", "c", "mp"))
    place = z * 8 + y * 2 + c
    positions = jnp.arange(seg_ids.shape[0], dtype=jnp.int32)
    start = jnp.min(jnp.where(seg_ids == 1, positions, seg_ids.shape[0])).astype(jnp.int32)

    top = lax.ppermute(latents[1:], SEQ, [(i, i + 1) for i in range(63)])
    below = lax.ppermute(latents, SEQ, [(i + 1, i) for i in range(63)])
    below_2 = lax.ppermute(latents[:1], SEQ, [(i + 2, i) for i in range(62)])

    near_w, far_w = embed_weight(embed_w, y)

    rows = jnp.concatenate([top, latents, below, below_2], axis=0)
    conv = lax.conv_general_dilated(
        rows[None],
        conv_w,
        (1, 1),
        ((0, 0), (1, 1)),
        dimension_numbers=("NHWC", "HWIO", "NHWC"),
        preferred_element_type=F32,
    )[0]
    own = lax.dynamic_slice_in_dim(rows[1:5], x * 64, 64, 2)
    mixed = (own.astype(F32) + jax.nn.silu(conv)).astype(BF)
    pair = mixed.reshape(2, 2, 64, 2, 64).transpose(0, 2, 1, 3, 4).reshape(TOK, 256)
    unit = start // 64
    placed = placed_patches(pair, unit)
    placed = jnp.where(2 * place - unit == -1, jnp.roll(placed, 64, axis=0), placed)
    placed, wqkv, text_emb = lax.optimization_barrier((placed, wqkv, text_emb))
    patches = ordered([placed] + [shift(placed, "mp", -t) for t in (1, 2, 3)], x)
    patches = patches.transpose(1, 0, 2).reshape(TOK, 1024)

    texts = ordered([text_emb] + [shift(text_emb, "mp", -t) for t in (1, 2, 3)], x)
    texts = texts.transpose(1, 0, 2).reshape(TOK, NZ, NX, 128).transpose(2, 0, 1, 3)
    texts = texts.reshape(NX, TOK, 1024)

    blocks = []
    for group in (near_w, far_w):
        mine = jnp.concatenate([w for _, w in group], axis=1)
        other = shift(mine, "c", 1)
        lower = jnp.where(c == 0, mine, other)
        upper = jnp.where(c == 0, other, mine)
        part = jnp.dot(patches[:, :512], lower, preferred_element_type=F32)
        part = part + jnp.dot(patches[:, 512:], upper, preferred_element_type=F32)
        part = part.astype(BF)
        for i, (offset, _) in enumerate(group):
            blocks.append((offset % NZ, part[:, i * 128 : (i + 1) * 128]))
    blocks = [b for _, b in sorted(blocks, key=lambda pair: pair[0])]
    twice = jnp.concatenate(blocks + blocks, axis=1)
    columns = lax.dynamic_slice_in_dim(twice, ((NZ - z) % NZ) * 128, 1024, 1)

    my_pos = place * TOK + jnp.arange(TOK, dtype=jnp.int32)
    is_text = (my_pos < start) | (my_pos >= start + IMG)
    by_group = wqkv.reshape(NZ, NX, 128, 3, 512)
    qkv = jnp.zeros((TOK, 1536), F32)
    arrived = [columns] + [shift(columns, "mp", -t) for t in (1, 3, 2)]
    for t, piece in zip((0, 1, 3, 2), arrived):
        group = (x + t) % NX
        weight = lax.dynamic_index_in_dim(by_group, group, 1, keepdims=False).reshape(1024, 1536)
        weight = lax.optimization_barrier(weight)
        text = lax.dynamic_index_in_dim(texts, group, 0, keepdims=False)
        hidden = jnp.where(is_text[:, None], text, piece)
        qkv = qkv + jnp.dot(hidden, weight, preferred_element_type=F32)
    qkv = qkv.astype(BF)
    by_head = qkv.reshape(TOK, 3, 4, HD).transpose(2, 0, 1, 3).reshape(4, TOK, 3 * HD)
    parts = []
    for t in range(NY):
        part = lax.dynamic_index_in_dim(by_head, (y + t) % NY, 0, keepdims=False)
        parts.append(part if t == 0 else shift(part, "y", t))
    head = jnp.concatenate(parts, axis=0)
    queries, keys_values = head[:, :HD], head[:, HD:]

    info = jnp.stack([z, y, c, start]).astype(jnp.int32)
    carry = None
    near, far = gather_z(keys_values)
    for group, last in ((near, False), (far, True)):
        if last:
            group = list(zip([o for o, _ in group], lax.optimization_barrier(([b for _, b in group], carry))[0]))
        mine = jnp.concatenate([b for _, b in group], axis=0)
        other = shift(mine, "c", 1)
        offsets = tuple(o for o, _ in group)
        carry = attend(info, queries, [(mine, offsets, True), (other, offsets, False)], carry, last)
    back = [carry[:TOK]]
    for t in range(1, NY):
        back.append(shift(carry[t * TOK : (t + 1) * TOK], "y", -t))
    return ordered(back, y).transpose(1, 0, 2).reshape(TOK, 4 * HD)


def solution(mesh):
    inner = Mesh(mesh.devices.reshape(NZ, NY, NC, NX), ("z", "y", "c", "mp"))
    return jax.shard_map(
        shards,
        mesh=inner,
        in_specs=(
            P(SEQ, None, None),
            P(None, None, None, "mp"),
            P(None, "mp", SEQ),
            P(SEQ, "mp"),
            P(None, None, "mp"),
            P(),
        ),
        out_specs=P(SEQ, "mp"),
        check_vma=False,
    )
```

```python
import functools
import math

import jax
import jax.numpy as jnp
from jax import lax
from jax.experimental import pallas as pl
from jax.experimental.pallas import tpu as pltpu
from jax.sharding import Mesh
from jax.sharding import PartitionSpec as P

NZ, NY, NC, NX = 8, 4, 2, 4
HD = 128
TOK = 128
IMG = 4096
SEQ = ("z", "y", "c")
SIZES = {"z": NZ, "y": NY, "c": NC, "mp": NX}
BF = jnp.bfloat16
F32 = jnp.float32


def shift(value, axis, step):
    count = SIZES[axis]
    return lax.ppermute(value, axis, [(i, (i + step) % count) for i in range(count)])


def ordered(pieces, first):
    count = len(pieces)
    twice = jnp.stack(pieces + pieces)
    return lax.dynamic_slice_in_dim(twice, (count - first) % count, count, 0)


def tied(info, other):
    return lax.optimization_barrier((info, other))[0]


def gather_z(block):
    half = block.shape[0] // 2
    below, above = shift(block, "z", 1), shift(block, "z", -1)
    below_2, above_2 = shift(block, "z", 2), shift(block, "z", -2)
    first = [(0, block), (-1, below), (1, above), (-2, below_2), (2, above_2)]
    below_3, above_3 = shift(below_2, "z", 1), shift(above_2, "z", -1)
    far = jnp.concatenate(
        [shift(below_2[:half], "z", 2), shift(above_2[half:], "z", -2)], axis=0
    )
    return first, [(-3, below_3), (3, above_3), (4, far)]


def call(kernel, out_shape, operands, flops=0, limit=40):
    vmem = pl.BlockSpec(memory_space=pltpu.VMEM)
    size = sum(a.size * a.dtype.itemsize for a in operands)
    return pl.pallas_call(
        kernel,
        out_shape=out_shape,
        in_specs=[pl.BlockSpec(memory_space=pltpu.SMEM)] + [vmem] * (len(operands) - 1),
        out_specs=jax.tree.map(lambda _: vmem, out_shape),
        compiler_params=pltpu.CompilerParams(vmem_limit_bytes=limit * 1024 * 1024),
        cost_estimate=pl.CostEstimate(flops=flops, bytes_accessed=size, transcendentals=0),
    )(*operands)


def block_kernel(info, p0, p1, p2, p3, out):
    y = info[1]
    pieces = [p0[...], p1[...], p2[...], p3[...]]
    placed = []
    for q in range(4):
        t = lax.rem(q - y + 4, 4)
        value = pieces[0]
        for i in range(1, 4):
            value = jnp.where(t == i, pieces[i], value)
        placed.append(value)
    for a in range(2):
        for half in range(2):
            lanes = slice(half * 64, half * 64 + 64)
            row = a * 256 + half * 128
            out[row : row + 128, :] = jnp.concatenate(
                [placed[2 * a][:, lanes], placed[2 * a + 1][:, lanes]], axis=1
            )


def embed_weight(info, embed_w):
    cells = embed_w.reshape(2, 128, 64)
    packed = jnp.concatenate([cells[0], cells[1]], axis=1)
    pieces = []
    for t in range(4):
        perm = []
        for src_y in range(NY):
            for src_c in range(NC):
                for src_x in range(NX):
                    dst_y = (2 * (src_x % 2) + src_c - t) % 4
                    perm.append(
                        (src_y * 8 + src_c * 4 + src_x, dst_y * 8 + (src_x // 2) * 4 + src_y)
                    )
        pieces.append(lax.ppermute(packed, ("y", "c", "mp"), perm))
    return call(block_kernel, jax.ShapeDtypeStruct((512, 128), BF), [info] + pieces)


OFFSETS = (0, -1, 1, -2, 2, -3, 3, 4)


def embed_kernel(info, p0, p1, p2, p3, near, near_other, far, far_other, out):
    c, x = info[2], info[3]
    pieces = [p0[...], p1[...], p2[...], p3[...]]

    def features(m):
        t = lax.rem(m - x + NX, NX)
        value = pieces[0]
        for i in range(1, NX):
            value = jnp.where(t == i, pieces[i], value)
        return value

    mine = jnp.concatenate([features(2 * c), features(2 * c + 1)], axis=1)
    other = jnp.concatenate([features(2 - 2 * c), features(3 - 2 * c)], axis=1)
    at = 0
    for own_ref, other_ref in ((near, near_other), (far, far_other)):
        width = own_ref.shape[1]
        part = jnp.dot(mine, own_ref[...], preferred_element_type=F32)
        part = part + jnp.dot(other, other_ref[...], preferred_element_type=F32)
        out[:, at : at + width] = part.astype(BF)
        at += width


def relayout_kernel(info, w_ref, out_ref):
    out_ref[...] = jnp.swapaxes(w_ref[...], 0, 1)


def relayout(info, wqkv, t):
    def rows(i, info):
        x = info[3]
        zone = 2 * lax.rem(x + i // 2, NX) + lax.rem(i, 2)
        return (zone * NX + lax.rem(x + t, NX), 0, 0)

    return pl.pallas_call(
        relayout_kernel,
        grid_spec=pltpu.PrefetchScalarGridSpec(
            num_scalar_prefetch=1,
            grid=(8,),
            in_specs=[pl.BlockSpec((128, 3, 512), rows)],
            out_specs=pl.BlockSpec((3, 128, 512), lambda i, info: (0, i, 0)),
        ),
        out_shape=jax.ShapeDtypeStruct((3, 1024, 512), BF),
        compiler_params=pltpu.CompilerParams(vmem_limit_bytes=16 * 1024 * 1024),
        cost_estimate=pl.CostEstimate(flops=0, bytes_accessed=7 << 20, transcendentals=0),
    )(info, wqkv)


def qkv_kernel(t, first_call, last_call, info, t0, t1, t2, t3, emb, weight, *refs):
    z, y, c, x, start = info[0], info[1], info[2], info[3], info[4]
    hidden = refs[-2]
    total = refs[-1]
    base = (z * 8 + y * 2 + c) * TOK
    pos = base + lax.broadcasted_iota(jnp.int32, (TOK, 128), 0)
    is_text = (pos < start) | (pos >= start + IMG)
    group = lax.rem(x + t, NX)
    for r, text in enumerate((t0, t1, t2, t3)):
        for h in range(2):
            zone = 2 * lax.rem(x + r, NX) + h
            offset = lax.rem(zone - z + NZ, NZ)
            at = jnp.where(offset < 4, 2 * offset, 15 - 2 * offset)
            part = emb[:, pl.ds(pl.multiple_of(at * 128, 128), 128)]
            word = text[:, pl.ds(pl.multiple_of((h * 4 + group) * 128, 128), 128)]
            col = (2 * r + h) * 128
            hidden[:, col : col + 128] = jnp.where(is_text, word, part)
    for j in range(3):
        cols = slice(j * 512, (j + 1) * 512)
        part = jnp.dot(hidden[...], weight[j], preferred_element_type=F32)
        if not first_call:
            part = part + refs[0][:, cols]
        total[:, cols] = part
    if last_call:
        for k in range(NY):
            head = lax.rem(y + k, NY)
            for j in range(3):
                value = total[:, pl.ds(pl.multiple_of(j * 512 + head * 128, 128), 128)]
                refs[1 + k][:, j * 128 : (j + 1) * 128] = value.astype(BF)
    else:
        refs[-3][...] = total[...]


def qkv_part(info, t, texts, emb, weight, carry, last_call):
    operands = [info, *texts, emb, weight] + ([] if carry is None else [carry])
    vmem = pl.BlockSpec(memory_space=pltpu.VMEM)
    if last_call:
        out = [jax.ShapeDtypeStruct((TOK, 3 * HD), BF)] * NY
    else:
        out = jax.ShapeDtypeStruct((TOK, 1536), F32)
    return pl.pallas_call(
        functools.partial(qkv_kernel, t, carry is None, last_call),
        out_shape=out,
        in_specs=[pl.BlockSpec(memory_space=pltpu.SMEM)] + [vmem] * (len(operands) - 1),
        out_specs=jax.tree.map(lambda _: vmem, out),
        scratch_shapes=[pltpu.VMEM((TOK, 1024), BF), pltpu.VMEM((TOK, 1536), F32)],
        compiler_params=pltpu.CompilerParams(vmem_limit_bytes=24 * 1024 * 1024),
        cost_estimate=pl.CostEstimate(
            flops=2 * TOK * 1024 * 1536, bytes_accessed=5 << 20, transcendentals=0
        ),
    )(*operands)


def placed_patches(pair, unit):
    low = (unit // 2) % 4
    odd = unit % 2

    def spread(low_shift, parity):
        moves = [(s, low_shift + (s + parity) // 2) for s in range(parity, 64, 2)]
        if parity:
            moves.append((0, low_shift))
        return lambda rows: lax.ppermute(rows, SEQ, moves)

    rows = lax.switch(low * 2 + odd, [spread(i // 2, i % 2) for i in range(8)], pair)

    def moved(high):
        if high == 0:
            return lambda rows: rows
        if high % 2 == 0:
            return lambda rows: shift(rows, "z", high // 2)
        return lambda rows: lax.ppermute(rows, SEQ, [(s, (s + 4 * high) % 64) for s in range(64)])

    return lax.switch(unit // 8, [moved(i) for i in range(9)], rows)


def attend_kernel(groups, first_call, last_call, *refs):
    info = refs[0]
    z, y, c, start = info[0], info[1], info[2], info[4]
    q_ref = refs[1]
    kv_refs = refs[2 : 2 + len(groups)]
    rest = refs[2 + len(groups) :]
    count = q_ref.shape[0]
    factor = HD**-0.5 * math.log2(math.e)
    if first_call:
        top = jnp.full((1, count), -1e30, F32)
        total = jnp.zeros((1, count), F32)
        acc = jnp.zeros((HD, count), F32)
    else:
        top, total, acc = rest[0][0:1, :], rest[0][8:9, :], rest[0][16:, :]
        rest = rest[1:]
    lanes = lax.broadcasted_iota(jnp.int32, (1, TOK), 1)
    limits = []
    for j in range(NY):
        pos = z * 1024 + lax.rem(y - j + NY, NY) * 256 + c * TOK + lanes
        inside = (pos >= start) & (pos < start + IMG)
        limits.append(jnp.where(inside, start + (IMG - 1), pos))
    limit = jnp.concatenate(limits, axis=1)
    rows = lax.broadcasted_iota(jnp.int32, (TOK, count), 0)
    queries = q_ref[...]
    for kv_ref, (offsets, own_core) in zip(kv_refs, groups):
        core = c if own_core else 1 - c
        for at, offset in enumerate(offsets):
            zone = lax.rem(z + offset + NZ, NZ)
            block = kv_ref[at * 512 : (at + 1) * 512, :]
            scores = lax.dot_general(
                block[:, :HD], queries, (((1,), (1,)), ((), ())), preferred_element_type=F32
            )
            parts = []
            for j in range(NY):
                base = zone * 1024 + lax.rem(y - j + NY, NY) * 256 + core * TOK
                visible = rows <= limit - base
                parts.append(jnp.where(visible, scores[j * TOK : (j + 1) * TOK], -1e30))
            scores = jnp.concatenate(parts, axis=0)
            higher = jnp.maximum(top, jnp.max(scores, axis=0, keepdims=True))
            fade = jnp.exp2((top - higher) * factor)
            weights = jnp.exp2((scores - higher) * factor)
            total = total * fade + jnp.sum(weights, axis=0, keepdims=True)
            acc = acc * fade + lax.dot_general(
                block[:, HD:],
                weights.astype(BF),
                (((0,), (0,)), ((), ())),
                preferred_element_type=F32,
            )
            top = higher
    out_ref = rest[0]
    if last_call:
        out_ref[...] = (acc / total).T.astype(BF)
    else:
        out_ref[0:8, :] = jnp.broadcast_to(top, (8, count))
        out_ref[8:16, :] = jnp.broadcast_to(total, (8, count))
        out_ref[16:, :] = acc


def attend(info, queries, groups, carry, last_call):
    arrays = [array for array, _, _ in groups]
    shape = [(offsets, own) for _, offsets, own in groups]
    operands = [info, queries] + arrays + ([] if carry is None else [carry])
    vmem = pl.BlockSpec(memory_space=pltpu.VMEM)
    count = queries.shape[0]
    keys = sum(a.shape[0] for a in arrays)
    if last_call:
        out = jax.ShapeDtypeStruct((count, HD), BF)
    else:
        out = jax.ShapeDtypeStruct((HD + 16, count), F32)
    return pl.pallas_call(
        functools.partial(attend_kernel, shape, carry is None, last_call),
        out_shape=out,
        in_specs=[pl.BlockSpec(memory_space=pltpu.SMEM)] + [vmem] * (len(operands) - 1),
        out_specs=vmem,
        compiler_params=pltpu.CompilerParams(vmem_limit_bytes=40 * 1024 * 1024),
        cost_estimate=pl.CostEstimate(
            flops=4 * count * keys * HD,
            bytes_accessed=keys * 512,
            transcendentals=count * keys,
        ),
    )(*operands)


def shards(latents, conv_w, embed_w, text_emb, wqkv, seg_ids):
    z, y, c, x = (lax.axis_index(a) for a in ("z", "y", "c", "mp"))
    place = z * 8 + y * 2 + c
    positions = jnp.arange(seg_ids.shape[0], dtype=jnp.int32)
    start = jnp.min(jnp.where(seg_ids == 1, positions, seg_ids.shape[0])).astype(jnp.int32)

    info = jnp.stack([z, y, c, x, start]).astype(jnp.int32)

    top = lax.ppermute(latents[1:], SEQ, [(i, i + 1) for i in range(63)])
    below = lax.ppermute(latents, SEQ, [(i + 1, i) for i in range(63)])
    below_2 = lax.ppermute(latents[:1], SEQ, [(i + 2, i) for i in range(62)])

    rows = jnp.concatenate([top, latents, below, below_2], axis=0)
    conv = lax.conv_general_dilated(
        rows[None],
        conv_w,
        (1, 1),
        ((0, 0), (1, 1)),
        dimension_numbers=("NHWC", "HWIO", "NHWC"),
        preferred_element_type=F32,
    )[0]
    own = lax.dynamic_slice_in_dim(rows[1:5], x * 64, 64, 2)
    mixed = (own.astype(F32) + jax.nn.silu(conv)).astype(BF)
    pair = mixed.reshape(2, 2, 64, 2, 64).transpose(0, 2, 1, 3, 4).reshape(TOK, 256)
    unit = start // 64
    placed = placed_patches(pair, unit)
    placed = jnp.where(2 * place - unit == -1, jnp.roll(placed, 64, axis=0), placed)
    near_w, far_w = gather_z(embed_weight(tied(info, pair), embed_w))

    text_emb, _ = lax.optimization_barrier((text_emb, pair))
    texts = [text_emb] + [shift(text_emb, "mp", -t) for t in (1, 2, 3)]
    patches = [placed] + [shift(placed, "mp", -t) for t in (1, 2, 3)]

    operands = [info, *patches]
    for group in (near_w, far_w):
        mine = jnp.concatenate([w for _, w in group], axis=1)
        operands += [mine, shift(mine, "c", 1)]
    columns = call(embed_kernel, jax.ShapeDtypeStruct((TOK, 1024), BF), operands, 2 * TOK * 1024 * 1024)

    early, late = tied(info, placed), tied(info, columns)
    weights = {t: relayout(early if t in (0, 1) else late, wqkv, t) for t in range(NX)}
    carry = None
    for t in (0, 1, 3, 2):
        piece = columns if t == 0 else shift(columns, "mp", -t)
        carry = qkv_part(info, t, texts, piece, weights[t], carry, t == 2)
    parts = [carry[0]] + [shift(carry[t], "y", t) for t in (1, 2, 3)]
    head = jnp.concatenate(parts, axis=0)
    queries, keys_values = head[:, :HD], head[:, HD:]

    carry = None
    near, far = gather_z(keys_values)
    for group, last in ((near, False), (far, True)):
        if last:
            group = list(zip([o for o, _ in group], lax.optimization_barrier(([b for _, b in group], carry))[0]))
        mine = jnp.concatenate([b for _, b in group], axis=0)
        other = shift(mine, "c", 1)
        offsets = tuple(o for o, _ in group)
        carry = attend(info, queries, [(mine, offsets, True), (other, offsets, False)], carry, last)
    back = [carry[:TOK]]
    for t in range(1, NY):
        back.append(shift(carry[t * TOK : (t + 1) * TOK], "y", -t))
    return ordered(back, y).transpose(1, 0, 2).reshape(TOK, 4 * HD)


def solution(mesh):
    inner = Mesh(mesh.devices.reshape(NZ, NY, NC, NX), ("z", "y", "c", "mp"))
    return jax.shard_map(
        shards,
        mesh=inner,
        in_specs=(
            P(SEQ, None, None),
            P(None, None, None, "mp"),
            P(None, "mp", SEQ),
            P(SEQ, "mp"),
            P(None, None, "mp"),
            P(),
        ),
        out_specs=P(SEQ, "mp"),
        check_vma=False,
    )
```

```python
import functools
import math

import jax
import jax.numpy as jnp
from jax import lax
from jax.experimental import pallas as pl
from jax.experimental.pallas import tpu as pltpu
from jax.sharding import Mesh
from jax.sharding import PartitionSpec as P

NZ, NY, NC, NX = 8, 4, 2, 4
HD = 128
TOK = 128
IMG = 4096
SEQ = ("z", "y", "c")
SIZES = {"z": NZ, "y": NY, "c": NC, "mp": NX}
BF = jnp.bfloat16
F32 = jnp.float32


def shift(value, axis, step):
    count = SIZES[axis]
    return lax.ppermute(value, axis, [(i, (i + step) % count) for i in range(count)])


def ordered(pieces, first):
    count = len(pieces)
    twice = jnp.stack(pieces + pieces)
    return lax.dynamic_slice_in_dim(twice, (count - first) % count, count, 0)


def tied(info, other):
    return lax.optimization_barrier((info, other))[0]


def along(value, step):
    perm = []
    for z in range(NZ):
        perm.append((z * 2, (z + step) % NZ * 2))
        perm.append((z * 2 + 1, (z - step) % NZ * 2 + 1))
    return lax.ppermute(value, ("z", "c"), perm)


def swap(value):
    return shift(value, "c", 1)


def call(kernel, out_shape, operands, flops=0, limit=40):
    vmem = pl.BlockSpec(memory_space=pltpu.VMEM)
    size = sum(a.size * a.dtype.itemsize for a in operands)
    return pl.pallas_call(
        kernel,
        out_shape=out_shape,
        in_specs=[pl.BlockSpec(memory_space=pltpu.SMEM)] + [vmem] * (len(operands) - 1),
        out_specs=jax.tree.map(lambda _: vmem, out_shape),
        compiler_params=pltpu.CompilerParams(vmem_limit_bytes=limit * 1024 * 1024),
        cost_estimate=pl.CostEstimate(flops=flops, bytes_accessed=size, transcendentals=0),
    )(*operands)


def block_kernel(info, p0, p1, out):
    odd = lax.rem(info[1], 2)
    first = jnp.where(odd == 0, p0[...], p1[...])
    second = jnp.where(odd == 0, p1[...], p0[...])
    for a, value in enumerate((first, second)):
        for half in range(2):
            row = a * 256 + half * 128
            low = half * 64
            out[row : row + 128, :] = jnp.concatenate(
                [value[:, low : low + 64], value[:, 128 + low : 192 + low]], axis=1
            )


def embed_pieces(embed_w, c):
    cells = embed_w.reshape(2, 128, 64)
    packed = jnp.concatenate([cells[0], cells[1]], axis=1)
    other = swap(packed)
    both = jnp.concatenate(
        [jnp.where(c == 0, packed, other), jnp.where(c == 0, other, packed)], axis=1
    )
    pieces = []
    for k in range(2):
        perm = []
        for src_y in range(NY):
            for src_c in range(NC):
                for src_x in range(NX):
                    dst_y = (2 * src_c + k + src_x % 2) % NY
                    perm.append(
                        (src_y * 8 + src_c * 4 + src_x, dst_y * 8 + (src_x // 2) * 4 + src_y)
                    )
        pieces.append(lax.ppermute(both, ("y", "c", "mp"), perm))
    return pieces


def embed_kernel(info, p0, p1, p2, p3, own, own_x, d1, x1, d2, x2, d3, x3, d4, x4, out):
    c, x = info[2], info[3]
    pieces = [p0[...], p1[...], p2[...], p3[...]]

    def features(m):
        t = lax.rem(m - x + NX, NX)
        value = pieces[0]
        for i in range(1, NX):
            value = jnp.where(t == i, pieces[i], value)
        return value

    mine = jnp.concatenate([features(2 * c), features(2 * c + 1)], axis=1)
    other = jnp.concatenate([features(2 - 2 * c), features(3 - 2 * c)], axis=1)
    pairs = [
        (own[...], own_x[...]),
        (d1[:512, :], d1[512:, :]),
        (x1[512:, :], x1[:512, :]),
        (d2[:512, :], d2[512:, :]),
        (x2[512:, :], x2[:512, :]),
        (d3[:512, :], d3[512:, :]),
        (x3[512:, :], x3[:512, :]),
        (d4[...], x4[...]),
    ]
    for at, (first, second) in enumerate(pairs):
        part = jnp.dot(mine, first, preferred_element_type=F32)
        part = part + jnp.dot(other, second, preferred_element_type=F32)
        out[:, at * 128 : (at + 1) * 128] = part.astype(BF)


def qkv_kernel(t, first_call, last_call, info, t0, t1, t2, t3, emb, w0, w1, *refs):
    z, y, c, x, start = info[0], info[1], info[2], info[3], info[4]
    step = pl.program_id(0)
    hidden = refs[-2]
    total = refs[-1]

    @pl.when(step == 0)
    def _():
        base = (z * 8 + y * 2 + c) * TOK
        pos = base + lax.broadcasted_iota(jnp.int32, (TOK, 128), 0)
        is_text = (pos < start) | (pos >= start + IMG)
        group = lax.rem(x + t, NX)
        for r, text in enumerate((t0, t1, t2, t3)):
            for h in range(2):
                zone = 2 * lax.rem(x + r, NX) + h
                offset = lax.rem(zone - z + NZ, NZ)
                offset = jnp.where(c == 0, offset, lax.rem(NZ - offset, NZ))
                at = jnp.where(offset < 4, 2 * offset, 15 - 2 * offset)
                part = emb[:, pl.ds(pl.multiple_of(at * 128, 128), 128)]
                word = text[:, pl.ds(pl.multiple_of((h * 4 + group) * 128, 128), 128)]
                hidden[r, :, h * 128 : (h + 1) * 128] = jnp.where(is_text, word, part)
        if first_call:
            total[...] = jnp.zeros_like(total)
        else:
            total[...] = refs[0][...]

    here = hidden[step]
    for j in range(3):
        cols = slice(j * 512, (j + 1) * 512)
        part = jnp.dot(here[:, :128], w0[j], preferred_element_type=F32)
        part = part + jnp.dot(here[:, 128:], w1[j], preferred_element_type=F32)
        total[:, cols] = total[:, cols] + part

    @pl.when(step == NX - 1)
    def _():
        if last_call:
            for k in range(NY):
                head = lax.rem(y + k, NY)
                for j in range(3):
                    value = total[:, pl.ds(pl.multiple_of(j * 512 + head * 128, 128), 128)]
                    refs[1 + k][:, j * 128 : (j + 1) * 128] = value.astype(BF)
        else:
            refs[-3][...] = total[...]


def qkv_part(info, t, texts, emb, weight, carry, last_call):
    def rows(h):
        def index(i, info):
            zone = 2 * lax.rem(info[3] + i, NX) + h
            return (0, zone * NX + lax.rem(info[3] + t, NX), 0)

        return index

    def whole(array):
        return pl.BlockSpec(array.shape, lambda i, info: (0, 0))

    operands = [*texts, emb, weight, weight] + ([] if carry is None else [carry])
    if last_call:
        out = [jax.ShapeDtypeStruct((TOK, 3 * HD), BF)] * NY
    else:
        out = jax.ShapeDtypeStruct((TOK, 1536), F32)
    specs = [whole(a) for a in (*texts, emb)]
    specs += [pl.BlockSpec((3, 128, 512), rows(0)), pl.BlockSpec((3, 128, 512), rows(1))]
    specs += [] if carry is None else [whole(carry)]
    return pl.pallas_call(
        functools.partial(qkv_kernel, t, carry is None, last_call),
        grid_spec=pltpu.PrefetchScalarGridSpec(
            num_scalar_prefetch=1,
            grid=(NX,),
            in_specs=specs,
            out_specs=jax.tree.map(whole, out),
            scratch_shapes=[pltpu.VMEM((NX, TOK, 256), BF), pltpu.VMEM((TOK, 1536), F32)],
        ),
        out_shape=out,
        compiler_params=pltpu.CompilerParams(vmem_limit_bytes=24 * 1024 * 1024),
        cost_estimate=pl.CostEstimate(
            flops=2 * TOK * 1024 * 1536, bytes_accessed=5 << 20, transcendentals=0
        ),
    )(info, *operands)


def placed_patches(pair, unit):
    low = (unit // 2) % 4
    odd = unit % 2

    def spread(low_shift, parity):
        moves = [(s, low_shift + (s + parity) // 2) for s in range(parity, 64, 2)]
        if parity:
            moves.append((0, low_shift))
        return lambda rows: lax.ppermute(rows, SEQ, moves)

    rows = lax.switch(low * 2 + odd, [spread(i // 2, i % 2) for i in range(8)], pair)

    def moved(high):
        if high == 0:
            return lambda rows: rows
        if high % 2 == 0:
            return lambda rows: shift(rows, "z", high // 2)
        return lambda rows: lax.ppermute(rows, SEQ, [(s, (s + 4 * high) % 64) for s in range(64)])

    return lax.switch(unit // 8, [moved(i) for i in range(9)], rows)


def attend_kernel(groups, first_call, last_call, *refs):
    info = refs[0]
    z, y, c, start = info[0], info[1], info[2], info[4]
    q_ref = refs[1]
    kv_refs = refs[2 : 2 + len(groups)]
    rest = refs[2 + len(groups) :]
    count = q_ref.shape[0]
    factor = HD**-0.5 * math.log2(math.e)
    if first_call:
        top = jnp.full((1, count), -1e30, F32)
        total = jnp.zeros((1, count), F32)
        acc = jnp.zeros((HD, count), F32)
    else:
        top, total, acc = rest[0][0:1, :], rest[0][8:9, :], rest[0][16:, :]
        rest = rest[1:]
    lanes = lax.broadcasted_iota(jnp.int32, (1, TOK), 1)
    limits = []
    for j in range(NY):
        pos = z * 1024 + lax.rem(y - j + NY, NY) * 256 + c * TOK + lanes
        inside = (pos >= start) & (pos < start + IMG)
        limits.append(jnp.where(inside, start + (IMG - 1), pos))
    limit = jnp.concatenate(limits, axis=1)
    rows = lax.broadcasted_iota(jnp.int32, (TOK, count), 0)
    queries = q_ref[...]
    for kv_ref, (offset, own_core) in zip(kv_refs, groups):
        core = c if own_core else 1 - c
        for at in range(1):
            zone = lax.rem(z + offset * (1 - 2 * c) + NZ, NZ)
            block = kv_ref[at * 512 : (at + 1) * 512, :]
            scores = lax.dot_general(
                block[:, :HD], queries, (((1,), (1,)), ((), ())), preferred_element_type=F32
            )
            parts = []
            for j in range(NY):
                base = zone * 1024 + lax.rem(y - j + NY, NY) * 256 + core * TOK
                visible = rows <= limit - base
                parts.append(jnp.where(visible, scores[j * TOK : (j + 1) * TOK], -1e30))
            scores = jnp.concatenate(parts, axis=0)
            higher = jnp.maximum(top, jnp.max(scores, axis=0, keepdims=True))
            fade = jnp.exp2((top - higher) * factor)
            weights = jnp.exp2((scores - higher) * factor)
            total = total * fade + jnp.sum(weights, axis=0, keepdims=True)
            acc = acc * fade + lax.dot_general(
                block[:, HD:],
                weights.astype(BF),
                (((0,), (0,)), ((), ())),
                preferred_element_type=F32,
            )
            top = higher
    out_ref = rest[0]
    if last_call:
        out_ref[...] = (acc / total).T.astype(BF)
    else:
        out_ref[0:8, :] = jnp.broadcast_to(top, (8, count))
        out_ref[8:16, :] = jnp.broadcast_to(total, (8, count))
        out_ref[16:, :] = acc


def attend(info, queries, groups, carry, last_call):
    arrays = [array for array, _, _ in groups]
    shape = [(offset, own) for _, offset, own in groups]
    operands = [info, queries] + arrays + ([] if carry is None else [carry])
    vmem = pl.BlockSpec(memory_space=pltpu.VMEM)
    count = queries.shape[0]
    keys = sum(a.shape[0] for a in arrays)
    if last_call:
        out = jax.ShapeDtypeStruct((count, HD), BF)
    else:
        out = jax.ShapeDtypeStruct((HD + 16, count), F32)
    return pl.pallas_call(
        functools.partial(attend_kernel, shape, carry is None, last_call),
        out_shape=out,
        in_specs=[pl.BlockSpec(memory_space=pltpu.SMEM)] + [vmem] * (len(operands) - 1),
        out_specs=vmem,
        compiler_params=pltpu.CompilerParams(vmem_limit_bytes=40 * 1024 * 1024),
        cost_estimate=pl.CostEstimate(
            flops=4 * count * keys * HD,
            bytes_accessed=keys * 512,
            transcendentals=count * keys,
        ),
    )(*operands)


def shards(latents, conv_w, embed_w, text_emb, wqkv, seg_ids):
    z, y, c, x = (lax.axis_index(a) for a in ("z", "y", "c", "mp"))
    place = z * 8 + y * 2 + c
    positions = jnp.arange(seg_ids.shape[0], dtype=jnp.int32)
    start = jnp.min(jnp.where(seg_ids == 1, positions, seg_ids.shape[0])).astype(jnp.int32)

    info = jnp.stack([z, y, c, x, start]).astype(jnp.int32)

    pieces = embed_pieces(embed_w, c)

    other = swap(latents)
    chip = jnp.concatenate(
        [jnp.where(c == 0, latents, other), jnp.where(c == 0, other, latents)], axis=0
    )
    above = lax.ppermute(chip[3:], SEQ, [(i, i + 2) for i in range(62)])
    below = lax.ppermute(chip[:3], SEQ, [(i + 2, i) for i in range(62)])
    rows = jnp.where(
        c == 0,
        jnp.concatenate([above, chip, below[:1]], axis=0),
        jnp.concatenate([chip[1:], below], axis=0),
    )
    conv = lax.conv_general_dilated(
        rows[None],
        conv_w,
        (1, 1),
        ((0, 0), (1, 1)),
        dimension_numbers=("NHWC", "HWIO", "NHWC"),
        preferred_element_type=F32,
    )[0]
    own = lax.dynamic_slice_in_dim(rows[1:5], x * 64, 64, 2)
    mixed = (own.astype(F32) + jax.nn.silu(conv)).astype(BF)
    pair = mixed.reshape(2, 2, 64, 2, 64).transpose(0, 2, 1, 3, 4).reshape(TOK, 256)
    unit = start // 64
    placed = placed_patches(pair, unit)
    placed = jnp.where(2 * place - unit == -1, jnp.roll(placed, 64, axis=0), placed)
    text_emb, _ = lax.optimization_barrier((text_emb, above))
    texts = [text_emb] + [shift(text_emb, "mp", -t) for t in (1, 2, 3)]
    patches = [placed] + [shift(placed, "mp", -t) for t in (1, 2, 3)]

    own_w = call(
        block_kernel, jax.ShapeDtypeStruct((512, 128), BF), [tied(info, pair)] + pieces
    )
    own_x = swap(own_w)
    both = jnp.concatenate([own_w, own_x], axis=0)
    near_1, near_2 = along(both, 1), along(both, 2)
    held, _ = lax.optimization_barrier((near_2, patches[1]))
    far_3, far_4 = along(held, 1), along(held[:512], 2)
    operands = [info, *patches, own_w, own_x]
    for block in (near_1, near_2, far_3, far_4):
        operands += [block, swap(block)]
    columns = call(embed_kernel, jax.ShapeDtypeStruct((TOK, 1024), BF), operands, 2 * TOK * 1024 * 1024)

    weight = jnp.transpose(wqkv, (1, 0, 2))
    carry = None
    for t in (0, 1, 3, 2):
        piece = columns if t == 0 else shift(columns, "mp", -t)
        carry = qkv_part(info, t, texts, piece, weight, carry, t == 2)
    parts = [carry[0]] + [shift(carry[t], "y", t) for t in (1, 2, 3)]
    head = jnp.concatenate(parts, axis=0)
    queries, keys_values = head[:, :HD], head[:, HD:]

    first, second = keys_values, swap(keys_values)
    groups = [[(first, 0, True), (second, 0, False)]]
    for step in range(1, 5):
        first = along(first, 1)
        group = [(first, -step, True), (swap(first), step, False)]
        if step < 4:
            second = along(second, 1)
            group += [(second, -step, False), (swap(second), step, True)]
        groups.append(group)
    groups = [groups[0] + groups[1]] + groups[2:]
    carry = None
    for number, group in enumerate(groups):
        if carry is not None:
            arrays, carry = lax.optimization_barrier(([g[0] for g in group], carry))
            group = [(a, o, own) for a, (_, o, own) in zip(arrays, group)]
        carry = attend(info, queries, group, carry, number == len(groups) - 1)
    back = [carry[:TOK]]
    for t in range(1, NY):
        back.append(shift(carry[t * TOK : (t + 1) * TOK], "y", -t))
    return ordered(back, y).transpose(1, 0, 2).reshape(TOK, 4 * HD)


def solution(mesh):
    inner = Mesh(mesh.devices.reshape(NZ, NY, NC, NX), ("z", "y", "c", "mp"))
    return jax.shard_map(
        shards,
        mesh=inner,
        in_specs=(
            P(SEQ, None, None),
            P(None, None, None, "mp"),
            P(None, "mp", SEQ),
            P(SEQ, "mp"),
            P(None, None, "mp"),
            P(),
        ),
        out_specs=P(SEQ, "mp"),
        check_vma=False,
    )
```

```python
import functools
import math

import jax
import jax.numpy as jnp
from jax import lax
from jax.experimental import pallas as pl
from jax.experimental.pallas import tpu as pltpu
from jax.sharding import Mesh
from jax.sharding import PartitionSpec as P

NZ, NY, NC, NX = 8, 4, 2, 4
HD = 128
TOK = 128
IMG = 4096
SEQ = ("z", "y", "c")
SIZES = {"z": NZ, "y": NY, "c": NC, "mp": NX}
BF = jnp.bfloat16
F32 = jnp.float32


def shift(value, axis, step):
    count = SIZES[axis]
    return lax.ppermute(value, axis, [(i, (i + step) % count) for i in range(count)])


def ordered(pieces, first):
    count = len(pieces)
    twice = jnp.stack(pieces + pieces)
    return lax.dynamic_slice_in_dim(twice, (count - first) % count, count, 0)


def tied(info, other):
    return lax.optimization_barrier((info, other))[0]


def along(value, step):
    perm = []
    for z in range(NZ):
        perm.append((z * 2, (z + step) % NZ * 2))
        perm.append((z * 2 + 1, (z - step) % NZ * 2 + 1))
    return lax.ppermute(value, ("z", "c"), perm)


def swap(value):
    return shift(value, "c", 1)


def call(kernel, out_shape, operands, flops=0, limit=40):
    vmem = pl.BlockSpec(memory_space=pltpu.VMEM)
    size = sum(a.size * a.dtype.itemsize for a in operands)
    return pl.pallas_call(
        kernel,
        out_shape=out_shape,
        in_specs=[pl.BlockSpec(memory_space=pltpu.SMEM)] + [vmem] * (len(operands) - 1),
        out_specs=jax.tree.map(lambda _: vmem, out_shape),
        compiler_params=pltpu.CompilerParams(vmem_limit_bytes=limit * 1024 * 1024),
        cost_estimate=pl.CostEstimate(flops=flops, bytes_accessed=size, transcendentals=0),
    )(*operands)


def block_kernel(info, p0, p1, out):
    odd = lax.rem(info[1], 2)
    first = jnp.where(odd == 0, p0[...], p1[...])
    second = jnp.where(odd == 0, p1[...], p0[...])
    for a, value in enumerate((first, second)):
        for half in range(2):
            row = a * 256 + half * 128
            low = half * 64
            out[row : row + 128, :] = jnp.concatenate(
                [value[:, low : low + 64], value[:, 128 + low : 192 + low]], axis=1
            )


def embed_pieces(embed_w, c):
    cells = embed_w.reshape(2, 128, 64)
    packed = jnp.concatenate([cells[0], cells[1]], axis=1)
    other = swap(packed)
    both = jnp.concatenate(
        [jnp.where(c == 0, packed, other), jnp.where(c == 0, other, packed)], axis=1
    )
    pieces = []
    for k in range(2):
        perm = []
        for src_y in range(NY):
            for src_c in range(NC):
                for src_x in range(NX):
                    dst_y = (2 * src_c + k + src_x % 2) % NY
                    perm.append(
                        (src_y * 8 + src_c * 4 + src_x, dst_y * 8 + (src_x // 2) * 4 + src_y)
                    )
        pieces.append(lax.ppermute(both, ("y", "c", "mp"), perm))
    return pieces


def embed_kernel(info, p0, p1, p2, p3, own, own_x, d1, x1, d2, x2, d3, x3, d4, x4, out):
    c, x = info[2], info[3]
    pieces = [p0[...], p1[...], p2[...], p3[...]]

    def features(m):
        t = lax.rem(m - x + NX, NX)
        value = pieces[0]
        for i in range(1, NX):
            value = jnp.where(t == i, pieces[i], value)
        return value

    mine = jnp.concatenate([features(2 * c), features(2 * c + 1)], axis=1)
    other = jnp.concatenate([features(2 - 2 * c), features(3 - 2 * c)], axis=1)
    pairs = [
        (own[...], own_x[...]),
        (d1[:512, :], d1[512:, :]),
        (x1[512:, :], x1[:512, :]),
        (d2[:512, :], d2[512:, :]),
        (x2[512:, :], x2[:512, :]),
        (d3[:512, :], d3[512:, :]),
        (x3[512:, :], x3[:512, :]),
        (d4[...], x4[...]),
    ]
    for at, (first, second) in enumerate(pairs):
        part = jnp.dot(mine, first, preferred_element_type=F32)
        part = part + jnp.dot(other, second, preferred_element_type=F32)
        out[:, at * 128 : (at + 1) * 128] = part.astype(BF)


def qkv_kernel(t, first_call, last_call, info, t0, t1, t2, t3, emb, weight, *refs):
    z, y, c, x, start = info[0], info[1], info[2], info[3], info[4]
    step = pl.program_id(0)
    hidden = refs[-2]
    total = refs[-1]

    @pl.when(step == 0)
    def _():
        base = (z * 8 + y * 2 + c) * TOK
        pos = base + lax.broadcasted_iota(jnp.int32, (TOK, 128), 0)
        is_text = (pos < start) | (pos >= start + IMG)
        group = lax.rem(x + t, NX)
        for r, text in enumerate((t0, t1, t2, t3)):
            for h in range(2):
                zone = 2 * lax.rem(x + r, NX) + h
                offset = lax.rem(zone - z + NZ, NZ)
                offset = jnp.where(c == 0, offset, lax.rem(NZ - offset, NZ))
                at = jnp.where(offset < 4, 2 * offset, 15 - 2 * offset)
                part = emb[:, pl.ds(pl.multiple_of(at * 128, 128), 128)]
                word = text[:, pl.ds(pl.multiple_of((h * 4 + group) * 128, 128), 128)]
                hidden[r, :, h * 128 : (h + 1) * 128] = jnp.where(is_text, word, part)
        if first_call:
            total[...] = jnp.zeros_like(total)
        else:
            total[...] = refs[0][...]

    here = hidden[step]
    for j in range(3):
        cols = slice(j * 512, (j + 1) * 512)
        part = jnp.dot(here, weight[j, :, 0].reshape(256, 512), preferred_element_type=F32)
        total[:, cols] = total[:, cols] + part

    @pl.when(step == NX - 1)
    def _():
        if last_call:
            for k in range(NY):
                head = lax.rem(y + k, NY)
                for j in range(3):
                    value = total[:, pl.ds(pl.multiple_of(j * 512 + head * 128, 128), 128)]
                    refs[1 + k][:, j * 128 : (j + 1) * 128] = value.astype(BF)
        else:
            refs[-3][...] = total[...]


def qkv_part(info, t, texts, emb, weight, carry, last_call):
    def rows(i, info):
        return (0, lax.rem(info[3] + i, NX), lax.rem(info[3] + t, NX), 0, 0)

    def whole(array):
        return pl.BlockSpec(array.shape, lambda i, info: (0, 0))

    operands = [*texts, emb, weight] + ([] if carry is None else [carry])
    if last_call:
        out = [jax.ShapeDtypeStruct((TOK, 3 * HD), BF)] * NY
    else:
        out = jax.ShapeDtypeStruct((TOK, 1536), F32)
    specs = [whole(a) for a in (*texts, emb)]
    specs += [pl.BlockSpec((3, 2, 1, 128, 512), rows)]
    specs += [] if carry is None else [whole(carry)]
    return pl.pallas_call(
        functools.partial(qkv_kernel, t, carry is None, last_call),
        grid_spec=pltpu.PrefetchScalarGridSpec(
            num_scalar_prefetch=1,
            grid=(NX,),
            in_specs=specs,
            out_specs=jax.tree.map(whole, out),
            scratch_shapes=[pltpu.VMEM((NX, TOK, 256), BF), pltpu.VMEM((TOK, 1536), F32)],
        ),
        out_shape=out,
        compiler_params=pltpu.CompilerParams(vmem_limit_bytes=56 * 1024 * 1024),
        cost_estimate=pl.CostEstimate(
            flops=2 * TOK * 1024 * 1536, bytes_accessed=5 << 20, transcendentals=0
        ),
    )(info, *operands)


def placed_patches(pair, unit):
    low = (unit // 2) % 4
    odd = unit % 2

    def spread(low_shift, parity):
        moves = [(s, 16 + low_shift + (s + parity) // 2) for s in range(parity, 64, 2)]
        if parity:
            moves.append((0, 16 + low_shift))
        return lambda rows: lax.ppermute(rows, SEQ, moves)

    rows = lax.switch(low * 2 + odd, [spread(i // 2, i % 2) for i in range(8)], pair)

    def moved(high):
        if high == 0:
            return lambda rows: rows
        moves = [(s, s + 4 * high) for s in range(64) if 0 <= s + 4 * high < 64]
        return lambda rows: lax.ppermute(rows, SEQ, moves)

    return lax.switch(unit // 8, [moved(i - 4) for i in range(9)], rows)


def attend_kernel(groups, first_call, last_call, *refs):
    info = refs[0]
    z, y, c, start = info[0], info[1], info[2], info[4]
    q_ref = refs[1]
    kv_refs = refs[2 : 2 + len(groups)]
    rest = refs[2 + len(groups) :]
    count = q_ref.shape[0]
    factor = HD**-0.5 * math.log2(math.e)
    if first_call:
        top = jnp.full((1, count), -1e30, F32)
        total = jnp.zeros((1, count), F32)
        acc = jnp.zeros((HD, count), F32)
    else:
        top, total, acc = rest[0][0:1, :], rest[0][8:9, :], rest[0][16:, :]
        rest = rest[1:]
    lanes = lax.broadcasted_iota(jnp.int32, (1, TOK), 1)
    limits = []
    for j in range(NY):
        pos = z * 1024 + lax.rem(y - j + NY, NY) * 256 + c * TOK + lanes
        inside = (pos >= start) & (pos < start + IMG)
        limits.append(jnp.where(inside, start + (IMG - 1), pos))
    limit = jnp.concatenate(limits, axis=1)
    rows = lax.broadcasted_iota(jnp.int32, (TOK, count), 0)
    queries = q_ref[...]
    for kv_ref, (offset, own_core) in zip(kv_refs, groups):
        core = c if own_core else 1 - c
        for at in range(1):
            zone = lax.rem(z + offset * (1 - 2 * c) + NZ, NZ)
            block = kv_ref[at * 512 : (at + 1) * 512, :]
            scores = lax.dot_general(
                block[:, :HD], queries, (((1,), (1,)), ((), ())), preferred_element_type=F32
            )
            parts = []
            for j in range(NY):
                base = zone * 1024 + lax.rem(y - j + NY, NY) * 256 + core * TOK
                visible = rows <= limit - base
                parts.append(jnp.where(visible, scores[j * TOK : (j + 1) * TOK], -1e30))
            scores = jnp.concatenate(parts, axis=0)
            higher = jnp.maximum(top, jnp.max(scores, axis=0, keepdims=True))
            fade = jnp.exp2((top - higher) * factor)
            weights = jnp.exp2((scores - higher) * factor)
            total = total * fade + jnp.sum(weights, axis=0, keepdims=True)
            acc = acc * fade + lax.dot_general(
                block[:, HD:],
                weights.astype(BF),
                (((0,), (0,)), ((), ())),
                preferred_element_type=F32,
            )
            top = higher
    out_ref = rest[0]
    if last_call:
        out_ref[...] = (acc / total).T.astype(BF)
    else:
        out_ref[0:8, :] = jnp.broadcast_to(top, (8, count))
        out_ref[8:16, :] = jnp.broadcast_to(total, (8, count))
        out_ref[16:, :] = acc


def attend(info, queries, groups, carry, last_call):
    arrays = [array for array, _, _ in groups]
    shape = [(offset, own) for _, offset, own in groups]
    operands = [info, queries] + arrays + ([] if carry is None else [carry])
    vmem = pl.BlockSpec(memory_space=pltpu.VMEM)
    count = queries.shape[0]
    keys = sum(a.shape[0] for a in arrays)
    if last_call:
        out = jax.ShapeDtypeStruct((count, HD), BF)
    else:
        out = jax.ShapeDtypeStruct((HD + 16, count), F32)
    return pl.pallas_call(
        functools.partial(attend_kernel, shape, carry is None, last_call),
        out_shape=out,
        in_specs=[pl.BlockSpec(memory_space=pltpu.SMEM)] + [vmem] * (len(operands) - 1),
        out_specs=vmem,
        compiler_params=pltpu.CompilerParams(vmem_limit_bytes=40 * 1024 * 1024),
        cost_estimate=pl.CostEstimate(
            flops=4 * count * keys * HD,
            bytes_accessed=keys * 512,
            transcendentals=count * keys,
        ),
    )(*operands)


def shards(latents, conv_w, embed_w, text_emb, wqkv, seg_ids):
    z, y, c, x = (lax.axis_index(a) for a in ("z", "y", "c", "mp"))
    place = z * 8 + y * 2 + c
    positions = jnp.arange(seg_ids.shape[0], dtype=jnp.int32)
    start = jnp.min(jnp.where(seg_ids == 1, positions, seg_ids.shape[0])).astype(jnp.int32)

    info = jnp.stack([z, y, c, x, start]).astype(jnp.int32)

    pieces = embed_pieces(embed_w, c)

    other = swap(latents)
    chip = jnp.concatenate(
        [jnp.where(c == 0, latents, other), jnp.where(c == 0, other, latents)], axis=0
    )
    above = lax.ppermute(chip[3:], SEQ, [(i, i + 2) for i in range(62)])
    below = lax.ppermute(chip[:3], SEQ, [(i + 2, i) for i in range(62)])
    rows = jnp.where(
        c == 0,
        jnp.concatenate([above, chip, below[:1]], axis=0),
        jnp.concatenate([chip[1:], below], axis=0),
    )
    conv = lax.conv_general_dilated(
        rows[None],
        conv_w,
        (1, 1),
        ((0, 0), (1, 1)),
        dimension_numbers=("NHWC", "HWIO", "NHWC"),
        preferred_element_type=F32,
    )[0]
    own = lax.dynamic_slice_in_dim(rows[1:5], x * 64, 64, 2)
    mixed = (own.astype(F32) + jax.nn.silu(conv)).astype(BF)
    pair = mixed.reshape(2, 2, 64, 2, 64).transpose(0, 2, 1, 3, 4).reshape(TOK, 256)
    unit = start // 64

    text_emb, _ = lax.optimization_barrier((text_emb, other))
    texts = [text_emb] + [shift(text_emb, "mp", -t) for t in (1, 2, 3)]
    own_w = call(
        block_kernel, jax.ShapeDtypeStruct((512, 128), BF), [tied(info, pair)] + pieces
    )
    own_x = swap(own_w)
    both = jnp.concatenate([own_w, own_x], axis=0)
    near_1, near_2 = along(both, 1), along(both, 2)
    pair, texts, _ = lax.optimization_barrier((pair, texts, both))
    placed = placed_patches(pair, unit)
    placed = jnp.where(2 * place - unit == -1, jnp.roll(placed, 64, axis=0), placed)
    patches = [placed] + [shift(placed, "mp", -t) for t in (1, 2, 3)]
    held, _ = lax.optimization_barrier((near_2, placed))
    far_3, far_4 = along(held, 1), along(held[:512], 2)
    operands = [info, *patches, own_w, own_x]
    for block in (near_1, near_2, far_3, far_4):
        operands += [block, swap(block)]
    columns = call(embed_kernel, jax.ShapeDtypeStruct((TOK, 1024), BF), operands, 2 * TOK * 1024 * 1024)

    weight = jnp.transpose(wqkv, (1, 0, 2)).reshape(3, NZ, NX, 128, 512)
    carry = None
    for t in (0, 1, 3, 2):
        piece = columns if t == 0 else shift(columns, "mp", -t)
        carry = qkv_part(info, t, texts, piece, weight, carry, t == 2)
    parts = [carry[0]] + [shift(carry[t], "y", t) for t in (1, 2, 3)]
    head = jnp.concatenate(parts, axis=0)
    queries, keys_values = head[:, :HD], head[:, HD:]

    first, second = keys_values, swap(keys_values)
    groups = [[(first, 0, True), (second, 0, False)]]
    carry = None
    for step in range(1, 5):
        if step > 2:
            group = groups.pop(0)
            if step == 3:
                group = group + groups.pop(0)
            carry = attend(info, queries, group, carry, False)
            first, second, carry = lax.optimization_barrier((first, second, carry))
        first = along(first, 1)
        if step < 4:
            second = along(second, 1)
            group = [(first, -step, True), (swap(first), step, False)]
            group += [(second, -step, False), (swap(second), step, True)]
            groups.append(group)
    carry = attend(info, queries, groups.pop(0), carry, False)
    first, carry = lax.optimization_barrier((first, carry))
    carry = attend(info, queries, [(first, -4, True), (swap(first), 4, False)], carry, True)
    back = [carry[:TOK]]
    for t in range(1, NY):
        back.append(shift(carry[t * TOK : (t + 1) * TOK], "y", -t))
    return ordered(back, y).transpose(1, 0, 2).reshape(TOK, 4 * HD)


def solution(mesh):
    inner = Mesh(mesh.devices.reshape(NZ, NY, NC, NX), ("z", "y", "c", "mp"))
    return jax.shard_map(
        shards,
        mesh=inner,
        in_specs=(
            P(SEQ, None, None),
            P(None, None, None, "mp"),
            P(None, "mp", SEQ),
            P(SEQ, "mp"),
            P(None, None, "mp"),
            P(),
        ),
        out_specs=P(SEQ, "mp"),
        check_vma=False,
    )
```

```python
import functools
import math

import jax
import jax.numpy as jnp
from jax import lax
from jax.experimental import pallas as pl
from jax.experimental.pallas import tpu as pltpu
from jax.sharding import Mesh
from jax.sharding import PartitionSpec as P

NZ, NY, NC, NX = 8, 4, 2, 4
HD = 128
TOK = 128
IMG = 4096
SEQ = ("z", "y", "c")
SIZES = {"z": NZ, "y": NY, "c": NC, "mp": NX}
BF = jnp.bfloat16
F32 = jnp.float32


def shift(value, axis, step):
    count = SIZES[axis]
    return lax.ppermute(value, axis, [(i, (i + step) % count) for i in range(count)])


def ordered(pieces, first):
    count = len(pieces)
    twice = jnp.stack(pieces + pieces)
    return lax.dynamic_slice_in_dim(twice, (count - first) % count, count, 0)


def tied(info, other):
    return lax.optimization_barrier((info, other))[0]


def along(value, step):
    perm = []
    for z in range(NZ):
        perm.append((z * 2, (z + step) % NZ * 2))
        perm.append((z * 2 + 1, (z - step) % NZ * 2 + 1))
    return lax.ppermute(value, ("z", "c"), perm)


def swap(value):
    return shift(value, "c", 1)


def call(kernel, out_shape, operands, flops=0, limit=40):
    vmem = pl.BlockSpec(memory_space=pltpu.VMEM)
    size = sum(a.size * a.dtype.itemsize for a in operands)
    return pl.pallas_call(
        kernel,
        out_shape=out_shape,
        in_specs=[pl.BlockSpec(memory_space=pltpu.SMEM)] + [vmem] * (len(operands) - 1),
        out_specs=jax.tree.map(lambda _: vmem, out_shape),
        compiler_params=pltpu.CompilerParams(vmem_limit_bytes=limit * 1024 * 1024),
        cost_estimate=pl.CostEstimate(flops=flops, bytes_accessed=size, transcendentals=0),
    )(*operands)


def block_kernel(info, p0, p1, out):
    odd = lax.rem(info[1], 2)
    first = jnp.where(odd == 0, p0[...], p1[...])
    second = jnp.where(odd == 0, p1[...], p0[...])
    for a, value in enumerate((first, second)):
        for half in range(2):
            row = a * 256 + half * 128
            low = half * 64
            out[row : row + 128, :] = jnp.concatenate(
                [value[:, low : low + 64], value[:, 128 + low : 192 + low]], axis=1
            )


def embed_pieces(embed_w, c):
    cells = embed_w.reshape(2, 128, 64)
    packed = jnp.concatenate([cells[0], cells[1]], axis=1)
    other = swap(packed)
    both = jnp.concatenate(
        [jnp.where(c == 0, packed, other), jnp.where(c == 0, other, packed)], axis=1
    )
    pieces = []
    for k in range(2):
        perm = []
        for src_y in range(NY):
            for src_c in range(NC):
                for src_x in range(NX):
                    dst_y = (2 * src_c + k + src_x % 2) % NY
                    perm.append(
                        (src_y * 8 + src_c * 4 + src_x, dst_y * 8 + (src_x // 2) * 4 + src_y)
                    )
        pieces.append(lax.ppermute(both, ("y", "c", "mp"), perm))
    return pieces


def embed_kernel(info, p0, p1, p2, p3, own, own_x, d1, x1, d2, x2, d3, x3, d4, x4, out):
    c, x = info[2], info[3]
    pieces = [p0[...], p1[...], p2[...], p3[...]]

    def features(m):
        t = lax.rem(m - x + NX, NX)
        value = pieces[0]
        for i in range(1, NX):
            value = jnp.where(t == i, pieces[i], value)
        return value

    mine = jnp.concatenate([features(2 * c), features(2 * c + 1)], axis=1)
    other = jnp.concatenate([features(2 - 2 * c), features(3 - 2 * c)], axis=1)
    pairs = [
        (own[...], own_x[...]),
        (d1[:512, :], d1[512:, :]),
        (x1[512:, :], x1[:512, :]),
        (d2[:512, :], d2[512:, :]),
        (x2[512:, :], x2[:512, :]),
        (d3[:512, :], d3[512:, :]),
        (x3[512:, :], x3[:512, :]),
        (d4[...], x4[...]),
    ]
    for at, (first, second) in enumerate(pairs):
        part = jnp.dot(mine, first, preferred_element_type=F32)
        part = part + jnp.dot(other, second, preferred_element_type=F32)
        out[:, at * 128 : (at + 1) * 128] = part.astype(BF)


ARRIVALS = (0, 1, 3, 2)


def qkv_sum(t, info, texts, emb, weight, hidden):
    z, y, c, x, start = info[0], info[1], info[2], info[3], info[4]
    base = (z * 8 + y * 2 + c) * TOK
    pos = base + lax.broadcasted_iota(jnp.int32, (TOK, 128), 0)
    is_text = (pos < start) | (pos >= start + IMG)
    group = lax.rem(x + t, NX)
    for r, text in enumerate(texts):
        for h in range(2):
            zone = 2 * lax.rem(x + r, NX) + h
            offset = lax.rem(zone - z + NZ, NZ)
            offset = jnp.where(c == 0, offset, lax.rem(NZ - offset, NZ))
            at = jnp.where(offset < 4, 2 * offset, 15 - 2 * offset)
            part = emb[:, pl.ds(pl.multiple_of(at * 128, 128), 128)]
            word = text[:, pl.ds(pl.multiple_of((h * 4 + group) * 128, 128), 128)]
            col = (2 * r + h) * 128
            hidden[:, col : col + 128] = jnp.where(is_text, word, part)
    here = hidden[...]
    return [jnp.dot(here, weight[j], preferred_element_type=F32) for j in range(3)]


def qkv_first(info, t0, t1, t2, t3, emb, wqkv, total, w1, w2, w3, w0, hidden, sems):
    x = info[3]
    copies = []
    for n, t in enumerate(ARRIVALS):
        target = (w0, w1, w2, w3)[t]
        for r in range(NX):
            for h in range(2):
                row = lax.rem(x + r, NX) * 1024 + h * 512 + lax.rem(x + t, NX) * 128
                copies.append(
                    pltpu.make_async_copy(
                        wqkv.at[:, pl.ds(pl.multiple_of(row, 128), 128), :],
                        target.at[:, pl.ds((2 * r + h) * 128, 128), :],
                        sems.at[n * 8 + r * 2 + h],
                    )
                )
    for copy in copies:
        copy.start()
    for copy in copies[:8]:
        copy.wait()
    for j, part in enumerate(qkv_sum(0, info, (t0, t1, t2, t3), emb, w0, hidden)):
        total[:, j * 512 : (j + 1) * 512] = part
    for copy in copies[8:]:
        copy.wait()


def qkv_next(t, info, t0, t1, t2, t3, emb, weight, carry, out, hidden):
    for j, part in enumerate(qkv_sum(t, info, (t0, t1, t2, t3), emb, weight, hidden)):
        cols = slice(j * 512, (j + 1) * 512)
        out[:, cols] = carry[:, cols] + part


def qkv_last(t, info, t0, t1, t2, t3, emb, weight, carry, o0, o1, o2, o3, hidden, total):
    qkv_next(t, info, t0, t1, t2, t3, emb, weight, carry, total, hidden)
    for k, out in enumerate((o0, o1, o2, o3)):
        head = lax.rem(info[1] + k, NY)
        for j in range(3):
            value = total[:, pl.ds(pl.multiple_of(j * 512 + head * 128, 128), 128)]
            out[:, j * 128 : (j + 1) * 128] = value.astype(BF)


def project(info, texts, columns, wqkv):
    vmem = pl.BlockSpec(memory_space=pltpu.VMEM)
    smem = pl.BlockSpec(memory_space=pltpu.SMEM)
    weight = jax.ShapeDtypeStruct((3, 1024, 512), BF)
    total = jax.ShapeDtypeStruct((TOK, 1536), F32)
    hidden = pltpu.VMEM((TOK, 1024), BF)
    flops = 2 * TOK * 1024 * 1536
    carry, *weights = pl.pallas_call(
        qkv_first,
        out_shape=[total, weight, weight, weight],
        in_specs=[smem] + [vmem] * 5 + [pl.BlockSpec(memory_space=pl.ANY)],
        out_specs=[vmem] * 4,
        scratch_shapes=[
            pltpu.VMEM((3, 1024, 512), BF),
            hidden,
            pltpu.SemaphoreType.DMA((32,)),
        ],
        compiler_params=pltpu.CompilerParams(vmem_limit_bytes=32 * 1024 * 1024),
        cost_estimate=pl.CostEstimate(
            flops=flops, bytes_accessed=24 << 20, transcendentals=0
        ),
    )(info, *texts, columns, jnp.transpose(wqkv, (1, 0, 2)))
    for t in ARRIVALS[1:]:
        last = t == 2
        head = jax.ShapeDtypeStruct((TOK, 3 * HD), BF)
        carry = pl.pallas_call(
            functools.partial(qkv_last if last else qkv_next, t),
            out_shape=[head] * NY if last else total,
            in_specs=[smem] + [vmem] * 7,
            out_specs=[vmem] * NY if last else vmem,
            scratch_shapes=[hidden] + ([pltpu.VMEM((TOK, 1536), F32)] if last else []),
            compiler_params=pltpu.CompilerParams(vmem_limit_bytes=24 * 1024 * 1024),
            cost_estimate=pl.CostEstimate(
                flops=flops, bytes_accessed=5 << 20, transcendentals=0
            ),
        )(info, *texts, shift(columns, "mp", -t), weights[t - 1], carry)
    return carry


def placed_patches(pair, unit):
    low = (unit // 2) % 4
    odd = unit % 2

    def spread(low_shift, parity):
        moves = [(s, 16 + low_shift + (s + parity) // 2) for s in range(parity, 64, 2)]
        if parity:
            moves.append((0, 16 + low_shift))
        return lambda rows: lax.ppermute(rows, SEQ, moves)

    rows = lax.switch(low * 2 + odd, [spread(i // 2, i % 2) for i in range(8)], pair)

    def moved(high):
        if high == 0:
            return lambda rows: rows
        moves = [(s, s + 4 * high) for s in range(64) if 0 <= s + 4 * high < 64]
        return lambda rows: lax.ppermute(rows, SEQ, moves)

    return lax.switch(unit // 8, [moved(i - 4) for i in range(9)], rows)


def attend_kernel(groups, first_call, last_call, *refs):
    info = refs[0]
    z, y, c, start = info[0], info[1], info[2], info[4]
    q_ref = refs[1]
    kv_refs = refs[2 : 2 + len(groups)]
    rest = refs[2 + len(groups) :]
    count = q_ref.shape[0]
    factor = HD**-0.5 * math.log2(math.e)
    if first_call:
        top = jnp.full((1, count), -1e30, F32)
        total = jnp.zeros((1, count), F32)
        acc = jnp.zeros((HD, count), F32)
    else:
        top, total, acc = rest[0][0:1, :], rest[0][8:9, :], rest[0][16:, :]
        rest = rest[1:]
    lanes = lax.broadcasted_iota(jnp.int32, (1, TOK), 1)
    limits = []
    for j in range(NY):
        pos = z * 1024 + lax.rem(y - j + NY, NY) * 256 + c * TOK + lanes
        inside = (pos >= start) & (pos < start + IMG)
        limits.append(jnp.where(inside, start + (IMG - 1), pos))
    limit = jnp.concatenate(limits, axis=1)
    rows = lax.broadcasted_iota(jnp.int32, (TOK, count), 0)
    queries = q_ref[...]
    for kv_ref, (offset, own_core) in zip(kv_refs, groups):
        for at in range(2):
            core = c if own_core == (at == 0) else 1 - c
            zone = lax.rem(z + offset * (1 - 2 * c) + NZ, NZ)
            block = kv_ref[at * 512 : (at + 1) * 512, :]
            scores = lax.dot_general(
                block[:, :HD], queries, (((1,), (1,)), ((), ())), preferred_element_type=F32
            )
            parts = []
            for j in range(NY):
                base = zone * 1024 + lax.rem(y - j + NY, NY) * 256 + core * TOK
                visible = rows <= limit - base
                parts.append(jnp.where(visible, scores[j * TOK : (j + 1) * TOK], -1e30))
            scores = jnp.concatenate(parts, axis=0)
            higher = jnp.maximum(top, jnp.max(scores, axis=0, keepdims=True))
            fade = jnp.exp2((top - higher) * factor)
            weights = jnp.exp2((scores - higher) * factor)
            total = total * fade + jnp.sum(weights, axis=0, keepdims=True)
            acc = acc * fade + lax.dot_general(
                block[:, HD:],
                weights.astype(BF),
                (((0,), (0,)), ((), ())),
                preferred_element_type=F32,
            )
            top = higher
    out_ref = rest[0]
    if last_call:
        out_ref[...] = (acc / total).T.astype(BF)
    else:
        out_ref[0:8, :] = jnp.broadcast_to(top, (8, count))
        out_ref[8:16, :] = jnp.broadcast_to(total, (8, count))
        out_ref[16:, :] = acc


def attend(info, queries, groups, carry, last_call):
    arrays = [array for array, _, _ in groups]
    shape = [(offset, own) for _, offset, own in groups]
    operands = [info, queries] + arrays + ([] if carry is None else [carry])
    vmem = pl.BlockSpec(memory_space=pltpu.VMEM)
    count = queries.shape[0]
    keys = sum(a.shape[0] for a in arrays)
    if last_call:
        out = jax.ShapeDtypeStruct((count, HD), BF)
    else:
        out = jax.ShapeDtypeStruct((HD + 16, count), F32)
    return pl.pallas_call(
        functools.partial(attend_kernel, shape, carry is None, last_call),
        out_shape=out,
        in_specs=[pl.BlockSpec(memory_space=pltpu.SMEM)] + [vmem] * (len(operands) - 1),
        out_specs=vmem,
        compiler_params=pltpu.CompilerParams(vmem_limit_bytes=40 * 1024 * 1024),
        cost_estimate=pl.CostEstimate(
            flops=4 * count * keys * HD,
            bytes_accessed=keys * 512,
            transcendentals=count * keys,
        ),
    )(*operands)


def shards(latents, conv_w, embed_w, text_emb, wqkv, seg_ids):
    z, y, c, x = (lax.axis_index(a) for a in ("z", "y", "c", "mp"))
    place = z * 8 + y * 2 + c
    positions = jnp.arange(seg_ids.shape[0], dtype=jnp.int32)
    start = jnp.min(jnp.where(seg_ids == 1, positions, seg_ids.shape[0])).astype(jnp.int32)

    info = jnp.stack([z, y, c, x, start]).astype(jnp.int32)

    pieces = embed_pieces(embed_w, c)

    other = swap(latents)
    chip = jnp.concatenate(
        [jnp.where(c == 0, latents, other), jnp.where(c == 0, other, latents)], axis=0
    )
    moves = [(i, i - 1) for i in range(2, 64, 2)] + [(i, i + 1) for i in range(1, 62, 2)]
    beside = lax.ppermute(jnp.where(c == 0, chip[:3], chip[1:]), SEQ, moves)
    below = swap(beside[:1])
    rows = jnp.where(
        c == 0,
        jnp.concatenate([beside[2:], chip, below], axis=0),
        jnp.concatenate([chip[1:], beside], axis=0),
    )
    conv = lax.conv_general_dilated(
        rows[None],
        conv_w,
        (1, 1),
        ((0, 0), (1, 1)),
        dimension_numbers=("NHWC", "HWIO", "NHWC"),
        preferred_element_type=F32,
    )[0]
    own = lax.dynamic_slice_in_dim(rows[1:5], x * 64, 64, 2)
    mixed = (own.astype(F32) + jax.nn.silu(conv)).astype(BF)
    pair = mixed.reshape(2, 2, 64, 2, 64).transpose(0, 2, 1, 3, 4).reshape(TOK, 256)
    unit = start // 64

    text_emb, _ = lax.optimization_barrier((text_emb, other))
    texts = [text_emb] + [shift(text_emb, "mp", -t) for t in (1, 2, 3)]
    own_w = call(
        block_kernel, jax.ShapeDtypeStruct((512, 128), BF), [info] + pieces
    )
    own_x = swap(own_w)
    both = jnp.concatenate([own_w, own_x], axis=0)
    near_1, near_2 = along(both, 1), along(both, 2)
    pair, texts, _ = lax.optimization_barrier((pair, texts, both))
    placed = placed_patches(pair, unit)
    placed = jnp.where(2 * place - unit == -1, jnp.roll(placed, 64, axis=0), placed)
    patches = [placed] + [shift(placed, "mp", -t) for t in (1, 2, 3)]
    held, _ = lax.optimization_barrier((near_2, placed))
    far_3, far_4 = along(held, 1), along(held[:512], 2)
    blocks, patches = lax.optimization_barrier(((near_1, near_2, far_3, far_4), patches))
    operands = [info, *patches, own_w, own_x]
    for block in blocks:
        operands += [block, swap(block)]
    columns = call(embed_kernel, jax.ShapeDtypeStruct((TOK, 1024), BF), operands, 2 * TOK * 1024 * 1024)

    carry = project(info, texts, columns, wqkv)
    parts = [carry[0]] + [shift(carry[t], "y", t) for t in (1, 2, 3)]
    head = jnp.concatenate(parts, axis=0)
    queries, keys_values = head[:, :HD], head[:, HD:]

    block = jnp.concatenate([keys_values, swap(keys_values)], axis=0)
    groups = [[(block, 0, True)]]
    carry = None
    for step in range(1, 5):
        if step > 1:
            carry = attend(info, queries, groups.pop(0), carry, False)
            block, carry = lax.optimization_barrier((block, carry))
        if step < 4:
            block = along(block, 1)
            groups.append([(block, -step, True), (swap(block), step, False)])
    half = along(block[:512], 1)
    carry = attend(info, queries, groups.pop(0), carry, False)
    half, carry = lax.optimization_barrier((half, carry))
    last = jnp.concatenate([half, swap(half)], axis=0)
    carry = attend(info, queries, [(last, -4, True)], carry, True)
    back = [carry[:TOK]]
    for t in range(1, NY):
        back.append(shift(carry[t * TOK : (t + 1) * TOK], "y", -t))
    return ordered(back, y).transpose(1, 0, 2).reshape(TOK, 4 * HD)


def solution(mesh):
    inner = Mesh(mesh.devices.reshape(NZ, NY, NC, NX), ("z", "y", "c", "mp"))
    return jax.shard_map(
        shards,
        mesh=inner,
        in_specs=(
            P(SEQ, None, None),
            P(None, None, None, "mp"),
            P(None, "mp", SEQ),
            P(SEQ, "mp"),
            P(None, None, "mp"),
            P(),
        ),
        out_specs=P(SEQ, "mp"),
        check_vma=False,
    )
```

```python
import functools
import math

import jax
import jax.numpy as jnp
from jax import lax
from jax.experimental import pallas as pl
from jax.experimental.pallas import tpu as pltpu
from jax.sharding import Mesh
from jax.sharding import PartitionSpec as P

NZ, NY, NC, NX = 8, 4, 2, 4
HD = 128
TOK = 128
IMG = 4096
SEQ = ("z", "y", "c")
SIZES = {"z": NZ, "y": NY, "c": NC, "mp": NX}
BF = jnp.bfloat16
F32 = jnp.float32


def shift(value, axis, step):
    count = SIZES[axis]
    return lax.ppermute(value, axis, [(i, (i + step) % count) for i in range(count)])


def ordered(pieces, first):
    count = len(pieces)
    twice = jnp.stack(pieces + pieces)
    return lax.dynamic_slice_in_dim(twice, (count - first) & (count - 1), count, 0)


def tied(info, other):
    return lax.optimization_barrier((info, other))[0]


def along(value, step):
    perm = []
    for z in range(NZ):
        perm.append((z * 2, (z + step) % NZ * 2))
        perm.append((z * 2 + 1, (z - step) % NZ * 2 + 1))
    return lax.ppermute(value, ("z", "c"), perm)


def swap(value):
    return shift(value, "c", 1)


def call(kernel, out_shape, operands, flops=0, limit=40):
    vmem = pl.BlockSpec(memory_space=pltpu.VMEM)
    size = sum(a.size * a.dtype.itemsize for a in operands)
    return pl.pallas_call(
        kernel,
        out_shape=out_shape,
        in_specs=[pl.BlockSpec(memory_space=pltpu.SMEM)] + [vmem] * (len(operands) - 1),
        out_specs=jax.tree.map(lambda _: vmem, out_shape),
        compiler_params=pltpu.CompilerParams(vmem_limit_bytes=limit * 1024 * 1024),
        cost_estimate=pl.CostEstimate(flops=flops, bytes_accessed=size, transcendentals=0),
    )(*operands)


def block_kernel(info, p0, p1, out):
    odd = lax.rem(info[1], 2)
    first = jnp.where(odd == 0, p0[...], p1[...])
    second = jnp.where(odd == 0, p1[...], p0[...])
    for a, value in enumerate((first, second)):
        for half in range(2):
            row = a * 256 + half * 128
            low = half * 64
            out[row : row + 128, :] = jnp.concatenate(
                [value[:, low : low + 64], value[:, 128 + low : 192 + low]], axis=1
            )


def embed_pieces(embed_w, c):
    cells = embed_w.reshape(2, 128, 64)
    packed = jnp.concatenate([cells[0], cells[1]], axis=1)
    other = swap(packed)
    both = jnp.concatenate(
        [jnp.where(c == 0, packed, other), jnp.where(c == 0, other, packed)], axis=1
    )
    pieces = []
    for k in range(2):
        perm = []
        for src_y in range(NY):
            for src_c in range(NC):
                for src_x in range(NX):
                    dst_y = (2 * src_c + k + src_x % 2) % NY
                    perm.append(
                        (src_y * 8 + src_c * 4 + src_x, dst_y * 8 + (src_x // 2) * 4 + src_y)
                    )
        pieces.append(lax.ppermute(both, ("y", "c", "mp"), perm))
    return pieces


def embed_kernel(info, p0, p1, p2, p3, own, own_x, d1, x1, d2, x2, d3, x3, d4, x4, out):
    c, x = info[2], info[3]
    pieces = [p0[...], p1[...], p2[...], p3[...]]
    late = 2 * (info[0] * 8 + info[1] * 2 + c) * 64 - info[4] == -64

    def features(m):
        t = lax.rem(m - x + NX, NX)
        value = pieces[0]
        for i in range(1, NX):
            value = jnp.where(t == i, pieces[i], value)
        return jnp.where(late, jnp.concatenate([value[64:], value[:64]], axis=0), value)

    mine = jnp.concatenate([features(2 * c), features(2 * c + 1)], axis=1)
    other = jnp.concatenate([features(2 - 2 * c), features(3 - 2 * c)], axis=1)
    pairs = [
        (own[...], own_x[...]),
        (d1[:512, :], d1[512:, :]),
        (x1[512:, :], x1[:512, :]),
        (d2[:512, :], d2[512:, :]),
        (x2[512:, :], x2[:512, :]),
        (d3[:512, :], d3[512:, :]),
        (x3[512:, :], x3[:512, :]),
        (d4[...], x4[...]),
    ]
    for at, (first, second) in enumerate(pairs):
        part = jnp.dot(mine, first, preferred_element_type=F32)
        part = part + jnp.dot(other, second, preferred_element_type=F32)
        out[:, at * 128 : (at + 1) * 128] = part.astype(BF)


ARRIVALS = (0, 1, 3, 2)


def qkv_sum(t, info, texts, emb, weight, hidden):
    z, y, c, x, start = info[0], info[1], info[2], info[3], info[4]
    base = (z * 8 + y * 2 + c) * TOK
    pos = base + lax.broadcasted_iota(jnp.int32, (TOK, 128), 0)
    is_text = (pos < start) | (pos >= start + IMG)
    group = lax.rem(x + t, NX)
    for r, text in enumerate(texts):
        for h in range(2):
            zone = 2 * lax.rem(x + r, NX) + h
            offset = lax.rem(zone - z + NZ, NZ)
            offset = jnp.where(c == 0, offset, lax.rem(NZ - offset, NZ))
            at = jnp.where(offset < 4, 2 * offset, 15 - 2 * offset)
            part = emb[:, pl.ds(pl.multiple_of(at * 128, 128), 128)]
            word = text[:, pl.ds(pl.multiple_of((h * 4 + group) * 128, 128), 128)]
            col = (2 * r + h) * 128
            hidden[:, col : col + 128] = jnp.where(is_text, word, part)
    here = hidden[...]
    return [jnp.dot(here, weight[j], preferred_element_type=F32) for j in range(3)]


def qkv_first(info, t0, t1, t2, t3, emb, wqkv, total, w1, w2, w3, w0, hidden, sems):
    x = info[3]
    copies = []
    for n, t in enumerate(ARRIVALS):
        target = (w0, w1, w2, w3)[t]
        for r in range(NX):
            for h in range(2):
                row = lax.rem(x + r, NX) * 1024 + h * 512 + lax.rem(x + t, NX) * 128
                copies.append(
                    pltpu.make_async_copy(
                        wqkv.at[:, pl.ds(pl.multiple_of(row, 128), 128), :],
                        target.at[:, pl.ds((2 * r + h) * 128, 128), :],
                        sems.at[n * 8 + r * 2 + h],
                    )
                )
    for copy in copies:
        copy.start()
    for copy in copies[:8]:
        copy.wait()
    for j, part in enumerate(qkv_sum(0, info, (t0, t1, t2, t3), emb, w0, hidden)):
        total[:, j * 512 : (j + 1) * 512] = part
    for copy in copies[8:]:
        copy.wait()


def qkv_next(t, info, t0, t1, t2, t3, emb, weight, carry, out, hidden):
    for j, part in enumerate(qkv_sum(t, info, (t0, t1, t2, t3), emb, weight, hidden)):
        cols = slice(j * 512, (j + 1) * 512)
        out[:, cols] = carry[:, cols] + part


def qkv_last(t, info, t0, t1, t2, t3, emb, weight, carry, o0, o1, o2, o3, hidden, total):
    qkv_next(t, info, t0, t1, t2, t3, emb, weight, carry, total, hidden)
    for k, out in enumerate((o0, o1, o2, o3)):
        head = lax.rem(info[1] + k, NY)
        for j in range(3):
            value = total[:, pl.ds(pl.multiple_of(j * 512 + head * 128, 128), 128)]
            out[:, j * 128 : (j + 1) * 128] = value.astype(BF)


def project(info, texts, columns, wqkv):
    vmem = pl.BlockSpec(memory_space=pltpu.VMEM)
    smem = pl.BlockSpec(memory_space=pltpu.SMEM)
    weight = jax.ShapeDtypeStruct((3, 1024, 512), BF)
    total = jax.ShapeDtypeStruct((TOK, 1536), F32)
    hidden = pltpu.VMEM((TOK, 1024), BF)
    flops = 2 * TOK * 1024 * 1536
    carry, *weights = pl.pallas_call(
        qkv_first,
        out_shape=[total, weight, weight, weight],
        in_specs=[smem] + [vmem] * 5 + [pl.BlockSpec(memory_space=pl.ANY)],
        out_specs=[vmem] * 4,
        scratch_shapes=[
            pltpu.VMEM((3, 1024, 512), BF),
            hidden,
            pltpu.SemaphoreType.DMA((32,)),
        ],
        compiler_params=pltpu.CompilerParams(vmem_limit_bytes=32 * 1024 * 1024),
        cost_estimate=pl.CostEstimate(
            flops=flops, bytes_accessed=24 << 20, transcendentals=0
        ),
    )(info, *texts, columns, jnp.transpose(wqkv, (1, 0, 2)))
    for t in ARRIVALS[1:]:
        last = t == 2
        head = jax.ShapeDtypeStruct((TOK, 3 * HD), BF)
        carry = pl.pallas_call(
            functools.partial(qkv_last if last else qkv_next, t),
            out_shape=[head] * NY if last else total,
            in_specs=[smem] + [vmem] * 7,
            out_specs=[vmem] * NY if last else vmem,
            scratch_shapes=[hidden] + ([pltpu.VMEM((TOK, 1536), F32)] if last else []),
            compiler_params=pltpu.CompilerParams(vmem_limit_bytes=24 * 1024 * 1024),
            cost_estimate=pl.CostEstimate(
                flops=flops, bytes_accessed=5 << 20, transcendentals=0
            ),
        )(info, *texts, shift(columns, "mp", -t), weights[t - 1], carry)
    return carry


def spread_patches(pair, unit):
    def spread(low_shift, parity):
        moves = [(s, 16 + low_shift + (s + parity) // 2) for s in range(parity, 64, 2)]
        if parity:
            moves.append((0, 16 + low_shift))
        return lambda rows: lax.ppermute(rows, SEQ, moves)

    return lax.switch(unit & 7, [spread(i // 2, i % 2) for i in range(8)], pair)


def shift_patches(rows, unit):
    def moved(high):
        if high == 0:
            return lambda rows: rows
        moves = [(s, s + 4 * high) for s in range(64) if 0 <= s + 4 * high < 64]
        return lambda rows: lax.ppermute(rows, SEQ, moves)

    return lax.switch(lax.shift_right_logical(unit, 3), [moved(i - 4) for i in range(9)], rows)


def attend_kernel(groups, first_call, last_call, *refs):
    info = refs[0]
    z, y, c, start = info[0], info[1], info[2], info[4]
    q_ref = refs[1]
    kv_refs = refs[2 : 2 + len(groups)]
    rest = refs[2 + len(groups) :]
    count = q_ref.shape[0]
    factor = HD**-0.5 * math.log2(math.e)
    if first_call:
        top = jnp.full((1, count), -1e30, F32)
        total = jnp.zeros((1, count), F32)
        acc = jnp.zeros((HD, count), F32)
    else:
        top, total, acc = rest[0][0:1, :], rest[0][8:9, :], rest[0][16:, :]
        rest = rest[1:]
    lanes = lax.broadcasted_iota(jnp.int32, (1, TOK), 1)
    limits = []
    for j in range(NY):
        pos = z * 1024 + lax.rem(y - j + NY, NY) * 256 + c * TOK + lanes
        inside = (pos >= start) & (pos < start + IMG)
        limits.append(jnp.where(inside, start + (IMG - 1), pos))
    limit = jnp.concatenate(limits, axis=1)
    rows = lax.broadcasted_iota(jnp.int32, (TOK, count), 0)
    queries = q_ref[...]
    for kv_ref, (offset, own_core) in zip(kv_refs, groups):
        for at in range(2):
            core = c if own_core == (at == 0) else 1 - c
            zone = lax.rem(z + offset * (1 - 2 * c) + NZ, NZ)
            block = kv_ref[at * 512 : (at + 1) * 512, :]
            scores = lax.dot_general(
                block[:, :HD], queries, (((1,), (1,)), ((), ())), preferred_element_type=F32
            )
            parts = []
            for j in range(NY):
                base = zone * 1024 + lax.rem(y - j + NY, NY) * 256 + core * TOK
                visible = rows <= limit - base
                parts.append(jnp.where(visible, scores[j * TOK : (j + 1) * TOK], -1e30))
            scores = jnp.concatenate(parts, axis=0)
            higher = jnp.maximum(top, jnp.max(scores, axis=0, keepdims=True))
            fade = jnp.exp2((top - higher) * factor)
            weights = jnp.exp2((scores - higher) * factor)
            total = total * fade + jnp.sum(weights, axis=0, keepdims=True)
            acc = acc * fade + lax.dot_general(
                block[:, HD:],
                weights.astype(BF),
                (((0,), (0,)), ((), ())),
                preferred_element_type=F32,
            )
            top = higher
    out_ref = rest[0]
    if last_call:
        out_ref[...] = (acc / total).T.astype(BF)
    else:
        out_ref[0:8, :] = jnp.broadcast_to(top, (8, count))
        out_ref[8:16, :] = jnp.broadcast_to(total, (8, count))
        out_ref[16:, :] = acc


def attend(info, queries, groups, carry, last_call):
    arrays = [array for array, _, _ in groups]
    shape = [(offset, own) for _, offset, own in groups]
    operands = [info, queries] + arrays + ([] if carry is None else [carry])
    vmem = pl.BlockSpec(memory_space=pltpu.VMEM)
    count = queries.shape[0]
    keys = sum(a.shape[0] for a in arrays)
    if last_call:
        out = jax.ShapeDtypeStruct((count, HD), BF)
    else:
        out = jax.ShapeDtypeStruct((HD + 16, count), F32)
    return pl.pallas_call(
        functools.partial(attend_kernel, shape, carry is None, last_call),
        out_shape=out,
        in_specs=[pl.BlockSpec(memory_space=pltpu.SMEM)] + [vmem] * (len(operands) - 1),
        out_specs=vmem,
        compiler_params=pltpu.CompilerParams(vmem_limit_bytes=40 * 1024 * 1024),
        cost_estimate=pl.CostEstimate(
            flops=4 * count * keys * HD,
            bytes_accessed=keys * 512,
            transcendentals=count * keys,
        ),
    )(*operands)


def shards(latents, conv_w, embed_w, text_emb, wqkv, seg_ids):
    z, y, c, x = (lax.axis_index(a) for a in ("z", "y", "c", "mp"))
    place = z * 8 + y * 2 + c
    positions = jnp.arange(seg_ids.shape[0], dtype=jnp.int32)
    start = jnp.min(jnp.where(seg_ids == 1, positions, seg_ids.shape[0])).astype(jnp.int32)

    info = jnp.stack([z, y, c, x, start]).astype(jnp.int32)

    pieces = embed_pieces(embed_w, c)

    other = swap(latents)
    chip = jnp.concatenate(
        [jnp.where(c == 0, latents, other), jnp.where(c == 0, other, latents)], axis=0
    )
    moves = [(i, i - 1) for i in range(2, 64, 2)] + [(i, i + 1) for i in range(1, 62, 2)]
    beside = lax.ppermute(jnp.where(c == 0, chip[:3], chip[1:]), SEQ, moves)
    below = swap(beside[:1])
    rows = jnp.where(
        c == 0,
        jnp.concatenate([beside[2:], chip, below], axis=0),
        jnp.concatenate([chip[1:], beside], axis=0),
    )
    conv = lax.conv_general_dilated(
        rows[None],
        conv_w,
        (1, 1),
        ((0, 0), (1, 1)),
        dimension_numbers=("NHWC", "HWIO", "NHWC"),
        preferred_element_type=F32,
    )[0]
    own = lax.dynamic_slice_in_dim(rows[1:5], x * 64, 64, 2)
    mixed = (own.astype(F32) + jax.nn.silu(conv)).astype(BF)
    pair = mixed.reshape(2, 2, 64, 2, 64).transpose(0, 2, 1, 3, 4).reshape(TOK, 256)
    unit = lax.shift_right_logical(start, 6)

    text_emb, _ = lax.optimization_barrier((text_emb, pair))
    texts = [text_emb] + [shift(text_emb, "mp", -t) for t in (1, 2, 3)]
    own_w = call(
        block_kernel, jax.ShapeDtypeStruct((512, 128), BF), [tied(info, beside)] + pieces
    )
    own_x = swap(own_w)
    both = jnp.concatenate([own_w, own_x], axis=0)
    near_1, near_2 = along(both, 1), along(both, 2)
    rows = spread_patches(pair, unit)
    rows, texts, near_2 = lax.optimization_barrier((rows, texts, near_2))
    placed = shift_patches(rows, unit)
    patches = [placed] + [shift(placed, "mp", -t) for t in (1, 2, 3)]
    far_3, far_4 = along(near_2, 1), along(near_2[:512], 2)
    blocks, patches = lax.optimization_barrier(((near_1, near_2, far_3, far_4), patches))
    operands = [info, *patches, own_w, own_x]
    for block in blocks:
        operands += [block, swap(block)]
    columns = call(embed_kernel, jax.ShapeDtypeStruct((TOK, 1024), BF), operands, 2 * TOK * 1024 * 1024)

    carry = project(info, texts, columns, wqkv)
    parts = [carry[0]] + [shift(carry[t], "y", t) for t in (1, 2, 3)]
    head = jnp.concatenate(parts, axis=0)
    queries, keys_values = head[:, :HD], head[:, HD:]

    block = jnp.concatenate([keys_values, swap(keys_values)], axis=0)
    group = [(block, 0, True)]
    block = along(block, 1)
    carry = None
    for step in range(1, 4):
        carry = attend(info, queries, group, carry, False)
        block, carry = lax.optimization_barrier((block, carry))
        group = [(block, -step, True), (swap(block), step, False)]
        block = along(block if step < 3 else block[:512], 1)
    carry = attend(info, queries, group, carry, False)
    block, carry = lax.optimization_barrier((block, carry))
    last = jnp.concatenate([block, swap(block)], axis=0)
    carry = attend(info, queries, [(last, -4, True)], carry, True)
    back = [carry[:TOK]]
    for t in range(1, NY):
        back.append(shift(carry[t * TOK : (t + 1) * TOK], "y", -t))
    return ordered(back, y).transpose(1, 0, 2).reshape(TOK, 4 * HD)


def solution(mesh):
    inner = Mesh(mesh.devices.reshape(NZ, NY, NC, NX), ("z", "y", "c", "mp"))
    return jax.shard_map(
        shards,
        mesh=inner,
        in_specs=(
            P(SEQ, None, None),
            P(None, None, None, "mp"),
            P(None, "mp", SEQ),
            P(SEQ, "mp"),
            P(None, None, "mp"),
            P(),
        ),
        out_specs=P(SEQ, "mp"),
        check_vma=False,
    )
```

```python
import functools
import math

import jax
import jax.numpy as jnp
from jax import lax
from jax.experimental import pallas as pl
from jax.experimental.pallas import tpu as pltpu
from jax.sharding import Mesh
from jax.sharding import PartitionSpec as P

NZ, NY, NC, NX = 8, 4, 2, 4
HD = 128
TOK = 128
IMG = 4096
SEQ = ("z", "y", "c")
SIZES = {"z": NZ, "y": NY, "c": NC, "mp": NX}
BF = jnp.bfloat16
F32 = jnp.float32


def shift(value, axis, step):
    count = SIZES[axis]
    return lax.ppermute(value, axis, [(i, (i + step) % count) for i in range(count)])


def ordered(pieces, first):
    count = len(pieces)
    twice = jnp.stack(pieces + pieces)
    return lax.dynamic_slice_in_dim(twice, (count - first) & (count - 1), count, 0)


def tied(info, other):
    return lax.optimization_barrier((info, other))[0]


def along(value, step):
    perm = []
    for z in range(NZ):
        perm.append((z * 2, (z + step) % NZ * 2))
        perm.append((z * 2 + 1, (z - step) % NZ * 2 + 1))
    return lax.ppermute(value, ("z", "c"), perm)


def swap(value):
    return shift(value, "c", 1)


def call(kernel, out_shape, operands, flops=0, limit=40):
    vmem = pl.BlockSpec(memory_space=pltpu.VMEM)
    size = sum(a.size * a.dtype.itemsize for a in operands)
    return pl.pallas_call(
        kernel,
        out_shape=out_shape,
        in_specs=[pl.BlockSpec(memory_space=pltpu.SMEM)] + [vmem] * (len(operands) - 1),
        out_specs=jax.tree.map(lambda _: vmem, out_shape),
        compiler_params=pltpu.CompilerParams(vmem_limit_bytes=limit * 1024 * 1024),
        cost_estimate=pl.CostEstimate(flops=flops, bytes_accessed=size, transcendentals=0),
    )(*operands)


def block_kernel(info, p0, p1, out):
    odd = lax.rem(info[1], 2)
    first = jnp.where(odd == 0, p0[...], p1[...])
    second = jnp.where(odd == 0, p1[...], p0[...])
    for a, value in enumerate((first, second)):
        for half in range(2):
            row = a * 256 + half * 128
            low = half * 64
            out[row : row + 128, :] = jnp.concatenate(
                [value[:, low : low + 64], value[:, 128 + low : 192 + low]], axis=1
            )


def embed_pieces(embed_w, c):
    cells = embed_w.reshape(2, 128, 64)
    packed = jnp.concatenate([cells[0], cells[1]], axis=1)
    other = swap(packed)
    both = jnp.concatenate(
        [jnp.where(c == 0, packed, other), jnp.where(c == 0, other, packed)], axis=1
    )
    pieces = []
    for k in range(2):
        perm = []
        for src_y in range(NY):
            for src_c in range(NC):
                for src_x in range(NX):
                    dst_y = (2 * src_c + k + src_x % 2) % NY
                    perm.append(
                        (src_y * 8 + src_c * 4 + src_x, dst_y * 8 + (src_x // 2) * 4 + src_y)
                    )
        pieces.append(lax.ppermute(both, ("y", "c", "mp"), perm))
    return pieces


def embed_kernel(info, p0, p1, p2, p3, own, own_x, d1, x1, d2, x2, d3, x3, d4, x4, out):
    c, x = info[2], info[3]
    pieces = [p0[...], p1[...], p2[...], p3[...]]
    late = 2 * (info[0] * 8 + info[1] * 2 + c) * 64 - info[4] == -64

    def features(m):
        t = lax.rem(m - x + NX, NX)
        value = pieces[0]
        for i in range(1, NX):
            value = jnp.where(t == i, pieces[i], value)
        return jnp.where(late, jnp.concatenate([value[64:], value[:64]], axis=0), value)

    mine = jnp.concatenate([features(2 * c), features(2 * c + 1)], axis=1)
    other = jnp.concatenate([features(2 - 2 * c), features(3 - 2 * c)], axis=1)
    pairs = [
        (own[...], own_x[...]),
        (d1[:512, :], d1[512:, :]),
        (x1[512:, :], x1[:512, :]),
        (d2[:512, :], d2[512:, :]),
        (x2[512:, :], x2[:512, :]),
        (d3[:512, :], d3[512:, :]),
        (x3[512:, :], x3[:512, :]),
        (d4[...], x4[...]),
    ]
    for at, (first, second) in enumerate(pairs):
        part = jnp.dot(mine, first, preferred_element_type=F32)
        part = part + jnp.dot(other, second, preferred_element_type=F32)
        out[:, at * 128 : (at + 1) * 128] = part.astype(BF)


ARRIVALS = (0, 1, 3, 2)


def qkv_sum(t, info, texts, emb, weight, hidden):
    z, y, c, x, start = info[0], info[1], info[2], info[3], info[4]
    base = (z * 8 + y * 2 + c) * TOK
    pos = base + lax.broadcasted_iota(jnp.int32, (TOK, 128), 0)
    is_text = (pos < start) | (pos >= start + IMG)
    group = lax.rem(x + t, NX)
    for r, text in enumerate(texts):
        for h in range(2):
            zone = 2 * lax.rem(x + r, NX) + h
            offset = lax.rem(zone - z + NZ, NZ)
            offset = jnp.where(c == 0, offset, lax.rem(NZ - offset, NZ))
            at = jnp.where(offset < 4, 2 * offset, 15 - 2 * offset)
            part = emb[:, pl.ds(pl.multiple_of(at * 128, 128), 128)]
            word = text[:, pl.ds(pl.multiple_of((h * 4 + group) * 128, 128), 128)]
            col = (2 * r + h) * 128
            hidden[:, col : col + 128] = jnp.where(is_text, word, part)
    here = hidden[...]
    return [jnp.dot(here, weight[j], preferred_element_type=F32) for j in range(3)]


def qkv_first(info, t0, t1, t2, t3, emb, wqkv, total, w1, w2, w3, w0, hidden, sems):
    x = info[3]
    copies = []
    for n, t in enumerate(ARRIVALS):
        target = (w0, w1, w2, w3)[t]
        for r in range(NX):
            for h in range(2):
                row = lax.rem(x + r, NX) * 1024 + h * 512 + lax.rem(x + t, NX) * 128
                copies.append(
                    pltpu.make_async_copy(
                        wqkv.at[:, pl.ds(pl.multiple_of(row, 128), 128), :],
                        target.at[:, pl.ds((2 * r + h) * 128, 128), :],
                        sems.at[n * 8 + r * 2 + h],
                    )
                )
    for copy in copies:
        copy.start()
    for copy in copies[:8]:
        copy.wait()
    for j, part in enumerate(qkv_sum(0, info, (t0, t1, t2, t3), emb, w0, hidden)):
        total[:, j * 512 : (j + 1) * 512] = part
    for copy in copies[8:]:
        copy.wait()


def qkv_next(t, info, t0, t1, t2, t3, emb, weight, carry, out, hidden):
    for j, part in enumerate(qkv_sum(t, info, (t0, t1, t2, t3), emb, weight, hidden)):
        cols = slice(j * 512, (j + 1) * 512)
        out[:, cols] = carry[:, cols] + part


def qkv_last(t, info, t0, t1, t2, t3, emb, weight, carry, o0, o1, o2, o3, hidden, total):
    qkv_next(t, info, t0, t1, t2, t3, emb, weight, carry, total, hidden)
    for k, out in enumerate((o0, o1, o2, o3)):
        head = lax.rem(info[1] + k, NY)
        for j in range(3):
            value = total[:, pl.ds(pl.multiple_of(j * 512 + head * 128, 128), 128)]
            out[:, j * 128 : (j + 1) * 128] = value.astype(BF)


def project(info, texts, columns, wqkv):
    vmem = pl.BlockSpec(memory_space=pltpu.VMEM)
    smem = pl.BlockSpec(memory_space=pltpu.SMEM)
    weight = jax.ShapeDtypeStruct((3, 1024, 512), BF)
    total = jax.ShapeDtypeStruct((TOK, 1536), F32)
    hidden = pltpu.VMEM((TOK, 1024), BF)
    flops = 2 * TOK * 1024 * 1536
    carry, *weights = pl.pallas_call(
        qkv_first,
        out_shape=[total, weight, weight, weight],
        in_specs=[smem] + [vmem] * 5 + [pl.BlockSpec(memory_space=pl.ANY)],
        out_specs=[vmem] * 4,
        scratch_shapes=[
            pltpu.VMEM((3, 1024, 512), BF),
            hidden,
            pltpu.SemaphoreType.DMA((32,)),
        ],
        compiler_params=pltpu.CompilerParams(vmem_limit_bytes=32 * 1024 * 1024),
        cost_estimate=pl.CostEstimate(
            flops=flops, bytes_accessed=24 << 20, transcendentals=0
        ),
    )(info, *texts, columns, jnp.transpose(wqkv, (1, 0, 2)))
    for t in ARRIVALS[1:]:
        last = t == 2
        head = jax.ShapeDtypeStruct((TOK, 3 * HD), BF)
        carry = pl.pallas_call(
            functools.partial(qkv_last if last else qkv_next, t),
            out_shape=[head] * NY if last else total,
            in_specs=[smem] + [vmem] * 7,
            out_specs=[vmem] * NY if last else vmem,
            scratch_shapes=[hidden] + ([pltpu.VMEM((TOK, 1536), F32)] if last else []),
            compiler_params=pltpu.CompilerParams(vmem_limit_bytes=24 * 1024 * 1024),
            cost_estimate=pl.CostEstimate(
                flops=flops, bytes_accessed=5 << 20, transcendentals=0
            ),
        )(info, *texts, shift(columns, "mp", -t), weights[t - 1], carry)
    return carry


def spread_patches(pair, unit):
    def spread(low_shift, parity):
        moves = [(s, 16 + low_shift + (s + parity) // 2) for s in range(parity, 64, 2)]
        if parity:
            moves.append((0, 16 + low_shift))
        return lambda rows: lax.ppermute(rows, SEQ, moves)

    return lax.switch(unit & 7, [spread(i // 2, i % 2) for i in range(8)], pair)


def shift_patches(rows, unit):
    def moved(high):
        if high == 0:
            return lambda rows: rows
        moves = [(s, s + 4 * high) for s in range(64) if 0 <= s + 4 * high < 64]
        return lambda rows: lax.ppermute(rows, SEQ, moves)

    return lax.switch(lax.shift_right_logical(unit, 3), [moved(i - 4) for i in range(9)], rows)


def attend_kernel(groups, first_call, last_call, *refs):
    info = refs[0]
    z, y, c, start = info[0], info[1], info[2], info[4]
    q_ref = refs[1]
    kv_refs = refs[2 : 2 + len(groups)]
    rest = refs[2 + len(groups) :]
    count = q_ref.shape[0]
    factor = HD**-0.5 * math.log2(math.e)
    if first_call:
        top = jnp.full((1, count), -1e30, F32)
        total = jnp.zeros((1, count), F32)
        acc = jnp.zeros((HD, count), F32)
    else:
        top, total, acc = rest[0][0:1, :], rest[0][8:9, :], rest[0][16:, :]
        rest = rest[1:]
    lanes = lax.broadcasted_iota(jnp.int32, (1, TOK), 1)
    limits = []
    for j in range(NY):
        pos = z * 1024 + lax.rem(y - j + NY, NY) * 256 + c * TOK + lanes
        inside = (pos >= start) & (pos < start + IMG)
        limits.append(jnp.where(inside, start + (IMG - 1), pos))
    limit = jnp.concatenate(limits, axis=1)
    rows = lax.broadcasted_iota(jnp.int32, (TOK, count), 0)
    queries = q_ref[...]
    for kv_ref, (offset, own_core) in zip(kv_refs, groups):
        for at in range(1):
            core = c if own_core else 1 - c
            zone = lax.rem(z + offset * (1 - 2 * c) + NZ, NZ)
            block = kv_ref[at * 512 : (at + 1) * 512, :]
            scores = lax.dot_general(
                block[:, :HD], queries, (((1,), (1,)), ((), ())), preferred_element_type=F32
            )
            parts = []
            for j in range(NY):
                base = zone * 1024 + lax.rem(y - j + NY, NY) * 256 + core * TOK
                visible = rows <= limit - base
                parts.append(jnp.where(visible, scores[j * TOK : (j + 1) * TOK], -1e30))
            scores = jnp.concatenate(parts, axis=0)
            higher = jnp.maximum(top, jnp.max(scores, axis=0, keepdims=True))
            fade = jnp.exp2((top - higher) * factor)
            weights = jnp.exp2((scores - higher) * factor)
            total = total * fade + jnp.sum(weights, axis=0, keepdims=True)
            acc = acc * fade + lax.dot_general(
                block[:, HD:],
                weights.astype(BF),
                (((0,), (0,)), ((), ())),
                preferred_element_type=F32,
            )
            top = higher
    out_ref = rest[0]
    if last_call:
        out_ref[...] = (acc / total).T.astype(BF)
    else:
        out_ref[0:8, :] = jnp.broadcast_to(top, (8, count))
        out_ref[8:16, :] = jnp.broadcast_to(total, (8, count))
        out_ref[16:, :] = acc


def attend(info, queries, groups, carry, last_call):
    arrays = [array for array, _, _ in groups]
    shape = [(offset, own) for _, offset, own in groups]
    operands = [info, queries] + arrays + ([] if carry is None else [carry])
    vmem = pl.BlockSpec(memory_space=pltpu.VMEM)
    count = queries.shape[0]
    keys = sum(a.shape[0] for a in arrays)
    if last_call:
        out = jax.ShapeDtypeStruct((count, HD), BF)
    else:
        out = jax.ShapeDtypeStruct((HD + 16, count), F32)
    return pl.pallas_call(
        functools.partial(attend_kernel, shape, carry is None, last_call),
        out_shape=out,
        in_specs=[pl.BlockSpec(memory_space=pltpu.SMEM)] + [vmem] * (len(operands) - 1),
        out_specs=vmem,
        compiler_params=pltpu.CompilerParams(vmem_limit_bytes=40 * 1024 * 1024),
        cost_estimate=pl.CostEstimate(
            flops=4 * count * keys * HD,
            bytes_accessed=keys * 512,
            transcendentals=count * keys,
        ),
    )(*operands)


def shards(latents, conv_w, embed_w, text_emb, wqkv, seg_ids):
    z, y, c, x = (lax.axis_index(a) for a in ("z", "y", "c", "mp"))
    place = z * 8 + y * 2 + c
    positions = jnp.arange(seg_ids.shape[0], dtype=jnp.int32)
    start = jnp.min(jnp.where(seg_ids == 1, positions, seg_ids.shape[0])).astype(jnp.int32)

    info = jnp.stack([z, y, c, x, start]).astype(jnp.int32)

    pieces = embed_pieces(embed_w, c)

    other = swap(latents)
    chip = jnp.concatenate(
        [jnp.where(c == 0, latents, other), jnp.where(c == 0, other, latents)], axis=0
    )
    moves = [(i, i - 1) for i in range(2, 64, 2)] + [(i, i + 1) for i in range(1, 62, 2)]
    beside = lax.ppermute(jnp.where(c == 0, chip[:3], chip[1:]), SEQ, moves)
    below = swap(beside[:1])
    rows = jnp.where(
        c == 0,
        jnp.concatenate([beside[2:], chip, below], axis=0),
        jnp.concatenate([chip[1:], beside], axis=0),
    )
    conv = lax.conv_general_dilated(
        rows[None],
        conv_w,
        (1, 1),
        ((0, 0), (1, 1)),
        dimension_numbers=("NHWC", "HWIO", "NHWC"),
        preferred_element_type=F32,
    )[0]
    own = lax.dynamic_slice_in_dim(rows[1:5], x * 64, 64, 2)
    mixed = (own.astype(F32) + jax.nn.silu(conv)).astype(BF)
    pair = mixed.reshape(2, 2, 64, 2, 64).transpose(0, 2, 1, 3, 4).reshape(TOK, 256)
    unit = lax.shift_right_logical(start, 6)

    text_emb, _ = lax.optimization_barrier((text_emb, pair))
    texts = [text_emb] + [shift(text_emb, "mp", -t) for t in (1, 2, 3)]
    own_w = call(
        block_kernel, jax.ShapeDtypeStruct((512, 128), BF), [tied(info, pair)] + pieces
    )
    own_x = swap(own_w)
    both = jnp.concatenate([own_w, own_x], axis=0)
    near_1, near_2 = along(both, 1), along(both, 2)
    rows = spread_patches(pair, unit)
    rows, texts, near_2 = lax.optimization_barrier((rows, texts, near_2))
    placed = shift_patches(rows, unit)
    patches = [placed] + [shift(placed, "mp", -t) for t in (1, 2, 3)]
    far_3, far_4 = along(near_2, 1), along(near_2[:512], 2)
    near, _ = lax.optimization_barrier(((near_1, near_2), placed))
    far, patches = lax.optimization_barrier(((far_3, far_4), patches))
    operands = [info, *patches, own_w, own_x]
    for block in near + far:
        operands += [block, swap(block)]
    columns = call(embed_kernel, jax.ShapeDtypeStruct((TOK, 1024), BF), operands, 2 * TOK * 1024 * 1024)

    carry = project(info, texts, columns, wqkv)
    parts = [carry[0]] + [shift(carry[t], "y", t) for t in (1, 2, 3)]
    head = jnp.concatenate(parts, axis=0)
    queries, keys_values = head[:, :HD], head[:, HD:]

    pair = (keys_values, swap(keys_values))
    group = [(pair[0], 0, True), (pair[1], 0, False)]
    pair = tuple(along(block, 1) for block in pair)
    carry = None
    for step in range(1, 4):
        carry = attend(info, queries, group, carry, False)
        group, sent = [], []
        for block, own in zip(pair, (True, False)):
            block, carry = lax.optimization_barrier((block, carry))
            if own or step < 3:
                sent.append(along(block, 1))
            group += [(block, -step, own), (swap(block), step, not own)]
        pair = sent
    carry = attend(info, queries, group, carry, False)
    pair, carry = lax.optimization_barrier((pair, carry))
    group = [(pair[0], -4, True), (swap(pair[0]), 4, False)]
    carry = attend(info, queries, group, carry, True)
    back = [carry[:TOK]]
    for t in range(1, NY):
        back.append(shift(carry[t * TOK : (t + 1) * TOK], "y", -t))
    return ordered(back, y).transpose(1, 0, 2).reshape(TOK, 4 * HD)


def solution(mesh):
    inner = Mesh(mesh.devices.reshape(NZ, NY, NC, NX), ("z", "y", "c", "mp"))
    return jax.shard_map(
        shards,
        mesh=inner,
        in_specs=(
            P(SEQ, None, None),
            P(None, None, None, "mp"),
            P(None, "mp", SEQ),
            P(SEQ, "mp"),
            P(None, None, "mp"),
            P(),
        ),
        out_specs=P(SEQ, "mp"),
        check_vma=False,
    )
```

```python
import functools
import itertools
import math

import jax
import jax.numpy as jnp
from jax import lax
from jax.experimental import pallas as pl
from jax.experimental.pallas import tpu as pltpu
from jax.sharding import Mesh
from jax.sharding import PartitionSpec as P

NZ, NY, NC, NX = 8, 4, 2, 4
HD = 128
TOK = 128
IMG = 4096
SEQ = ("z", "y", "c")
SIZES = {"z": NZ, "y": NY, "c": NC, "mp": NX}
BF = jnp.bfloat16
F32 = jnp.float32


def shift(value, axis, step):
    count = SIZES[axis]
    return lax.ppermute(value, axis, [(i, (i + step) % count) for i in range(count)])


def ordered(pieces, first):
    count = len(pieces)
    twice = jnp.stack(pieces + pieces)
    return lax.dynamic_slice_in_dim(twice, (count - first) & (count - 1), count, 0)


def tied(info, other):
    return lax.optimization_barrier((info, other))[0]


def along(value, step):
    perm = []
    for z in range(NZ):
        perm.append((z * 2, (z + step) % NZ * 2))
        perm.append((z * 2 + 1, (z - step) % NZ * 2 + 1))
    return lax.ppermute(value, ("z", "c"), perm)


def swap(value):
    return shift(value, "c", 1)


def call(kernel, out_shape, operands, flops=0, limit=40):
    vmem = pl.BlockSpec(memory_space=pltpu.VMEM)
    size = sum(a.size * a.dtype.itemsize for a in operands)
    return pl.pallas_call(
        kernel,
        out_shape=out_shape,
        in_specs=[pl.BlockSpec(memory_space=pltpu.SMEM)] + [vmem] * (len(operands) - 1),
        out_specs=jax.tree.map(lambda _: vmem, out_shape),
        compiler_params=pltpu.CompilerParams(vmem_limit_bytes=limit * 1024 * 1024),
        cost_estimate=pl.CostEstimate(flops=flops, bytes_accessed=size, transcendentals=0),
    )(*operands)


def block_kernel(info, p0, p1, out):
    odd = lax.rem(info[1], 2)
    first = jnp.where(odd == 0, p0[...], p1[...])
    second = jnp.where(odd == 0, p1[...], p0[...])
    for a, value in enumerate((first, second)):
        for half in range(2):
            row = a * 256 + half * 128
            low = half * 64
            out[row : row + 128, :] = jnp.concatenate(
                [value[:, low : low + 64], value[:, 128 + low : 192 + low]], axis=1
            )


def flat(z, y, c, x):
    return ((z * NY + y) * NC + c) * NX + x


def embed_pieces(embed_w, c):
    cells = embed_w.reshape(2, 128, 64)
    packed = jnp.concatenate([cells[0], cells[1]], axis=1)
    other = swap(packed)
    both = jnp.concatenate(
        [jnp.where(c == 0, packed, other), jnp.where(c == 0, other, packed)], axis=1
    )
    pieces = []
    for k in range(2):
        perm = []
        for z, y, c, x in itertools.product(range(NZ), range(NY), range(NC), range(NX)):
            to = ((z + 2 * y) % NZ, (2 * c + k + x % 2) % NY, x // 2, z // 2)
            perm.append((flat(z, y, c, x), flat(*to)))
        pieces.append(lax.ppermute(both, ("z", "y", "c", "mp"), perm))
    return pieces


OFFSETS = (0, -1, 1, -2, 2, -3, 3, 4)


def hidden_kernel(info, text, p0, p1, p2, p3, own, own_x, d1, x1, d2, x2, d3, x3, d4, x4, out):
    z, y, c, x, start = info[0], info[1], info[2], info[3], info[4]
    pieces = [p0[...], p1[...], p2[...], p3[...]]
    base = (z * 8 + y * 2 + c) * TOK
    late = base - start == -64
    pos = base + lax.broadcasted_iota(jnp.int32, (TOK, 128), 0)
    is_text = (pos < start) | (pos >= start + IMG)

    def features(m):
        t = lax.rem(m - x + NX, NX)
        value = pieces[0]
        for i in range(1, NX):
            value = jnp.where(t == i, pieces[i], value)
        return jnp.where(late, jnp.concatenate([value[64:], value[:64]], axis=0), value)

    mine = jnp.concatenate([features(2 * c), features(2 * c + 1)], axis=1)
    other = jnp.concatenate([features(2 - 2 * c), features(3 - 2 * c)], axis=1)
    pairs = [
        (own[...], own_x[...]),
        (d1[:512, :], d1[512:, :]),
        (x1[512:, :], x1[:512, :]),
        (d2[:512, :], d2[512:, :]),
        (x2[512:, :], x2[:512, :]),
        (d3[:512, :], d3[512:, :]),
        (x3[512:, :], x3[:512, :]),
        (d4[...], x4[...]),
    ]
    for at, (first, second) in enumerate(pairs):
        part = jnp.dot(mine, first, preferred_element_type=F32)
        part = part + jnp.dot(other, second, preferred_element_type=F32)
        zone = z + OFFSETS[at] * (1 - 2 * c) + NZ
        place = lax.rem(zone - 2 * x + NZ, NZ)
        place = 4 * (place & 1) + lax.shift_right_logical(place, 1)
        cols = pl.ds(pl.multiple_of(place * 128, 128), 128)
        out[:, cols] = jnp.where(is_text, text[:, cols], part.astype(BF))


ARRIVALS = (0, 1, 3, 2)


def qkv_first(info, hidden, wqkv, total, w1, w2, w3, w0, sems):
    x = info[3]
    copies = []
    for n, t in enumerate(ARRIVALS):
        target = (w0, w1, w2, w3)[t]
        for j in range(3):
            for h in range(4):
                row = lax.rem(x + t, NX) * 1024 + h * 256
                copies.append(
                    pltpu.make_async_copy(
                        wqkv.at[j, pl.ds(pl.multiple_of(row, 256), 256), :],
                        target.at[j, pl.ds(h * 256, 256), :],
                        sems.at[n * 12 + j * 4 + h],
                    )
                )
    for copy in copies:
        copy.start()
    for copy in copies[:12]:
        copy.wait()
    for j in range(3):
        cols = slice(j * 512, (j + 1) * 512)
        total[:, cols] = jnp.dot(hidden[...], w0[j], preferred_element_type=F32)
    for copy in copies[12:]:
        copy.wait()


def qkv_next(info, hidden, weight, carry, out):
    for j in range(3):
        cols = slice(j * 512, (j + 1) * 512)
        out[:, cols] = carry[:, cols] + jnp.dot(
            hidden[...], weight[j], preferred_element_type=F32
        )


def qkv_last(info, hidden, weight, carry, o0, o1, o2, o3, total):
    qkv_next(info, hidden, weight, carry, total)
    for k, out in enumerate((o0, o1, o2, o3)):
        head = lax.rem(info[1] + k, NY)
        for j in range(3):
            value = total[:, pl.ds(pl.multiple_of(j * 512 + head * 128, 128), 128)]
            out[:, j * 128 : (j + 1) * 128] = value.astype(BF)


def project(info, hidden, wqkv):
    vmem = pl.BlockSpec(memory_space=pltpu.VMEM)
    smem = pl.BlockSpec(memory_space=pltpu.SMEM)
    weight = jax.ShapeDtypeStruct((3, 1024, 512), BF)
    total = jax.ShapeDtypeStruct((TOK, 1536), F32)
    flops = 2 * TOK * 1024 * 1536
    carry, *weights = pl.pallas_call(
        qkv_first,
        out_shape=[total, weight, weight, weight],
        in_specs=[smem, vmem, pl.BlockSpec(memory_space=pl.ANY)],
        out_specs=[vmem] * 4,
        scratch_shapes=[pltpu.VMEM((3, 1024, 512), BF), pltpu.SemaphoreType.DMA((48,))],
        compiler_params=pltpu.CompilerParams(vmem_limit_bytes=32 * 1024 * 1024),
        cost_estimate=pl.CostEstimate(
            flops=flops, bytes_accessed=24 << 20, transcendentals=0
        ),
    )(info, hidden, jnp.transpose(wqkv, (1, 0, 2)))
    for t in ARRIVALS[1:]:
        last = t == 2
        head = jax.ShapeDtypeStruct((TOK, 3 * HD), BF)
        carry = pl.pallas_call(
            qkv_last if last else qkv_next,
            out_shape=[head] * NY if last else total,
            in_specs=[smem] + [vmem] * 3,
            out_specs=[vmem] * NY if last else vmem,
            scratch_shapes=[pltpu.VMEM((TOK, 1536), F32)] if last else [],
            compiler_params=pltpu.CompilerParams(vmem_limit_bytes=24 * 1024 * 1024),
            cost_estimate=pl.CostEstimate(
                flops=flops, bytes_accessed=5 << 20, transcendentals=0
            ),
        )(info, shift(hidden, "mp", -t), weights[t - 1], carry)
    return carry


def spread_patches(pair, unit):
    def spread(low_shift, parity):
        moves = [(s, 16 + low_shift + (s + parity) // 2) for s in range(parity, 64, 2)]
        if parity:
            moves.append((0, 16 + low_shift))
        return lambda rows: lax.ppermute(rows, SEQ, moves)

    return lax.switch(unit & 7, [spread(i // 2, i % 2) for i in range(8)], pair)


def shift_patches(rows, unit):
    def moved(high):
        if high == 0:
            return lambda rows: rows
        moves = [(s, s + 4 * high) for s in range(64) if 0 <= s + 4 * high < 64]
        return lambda rows: lax.ppermute(rows, SEQ, moves)

    return lax.switch(lax.shift_right_logical(unit, 3), [moved(i - 4) for i in range(9)], rows)


def attend_kernel(groups, first_call, last_call, *refs):
    info = refs[0]
    z, y, c, start = info[0], info[1], info[2], info[4]
    q_ref = refs[1]
    kv_refs = refs[2 : 2 + len(groups)]
    rest = refs[2 + len(groups) :]
    count = q_ref.shape[0]
    factor = HD**-0.5 * math.log2(math.e)
    if first_call:
        top = jnp.full((1, count), -1e30, F32)
        total = jnp.zeros((1, count), F32)
        acc = jnp.zeros((HD, count), F32)
    else:
        top, total, acc = rest[0][0:1, :], rest[0][8:9, :], rest[0][16:, :]
        rest = rest[1:]
    lanes = lax.broadcasted_iota(jnp.int32, (1, TOK), 1)
    limits = []
    for j in range(NY):
        pos = z * 1024 + lax.rem(y - j + NY, NY) * 256 + c * TOK + lanes
        inside = (pos >= start) & (pos < start + IMG)
        limits.append(jnp.where(inside, start + (IMG - 1), pos))
    limit = jnp.concatenate(limits, axis=1)
    rows = lax.broadcasted_iota(jnp.int32, (TOK, count), 0)
    queries = q_ref[...]
    for kv_ref, (offset, own_core) in zip(kv_refs, groups):
        for at in range(2):
            core = c if own_core == (at == 0) else 1 - c
            zone = lax.rem(z + offset * (1 - 2 * c) + NZ, NZ)
            block = kv_ref[at * 512 : (at + 1) * 512, :]
            scores = lax.dot_general(
                block[:, :HD], queries, (((1,), (1,)), ((), ())), preferred_element_type=F32
            )
            parts = []
            for j in range(NY):
                base = zone * 1024 + lax.rem(y - j + NY, NY) * 256 + core * TOK
                visible = rows <= limit - base
                parts.append(jnp.where(visible, scores[j * TOK : (j + 1) * TOK], -1e30))
            scores = jnp.concatenate(parts, axis=0)
            higher = jnp.maximum(top, jnp.max(scores, axis=0, keepdims=True))
            fade = jnp.exp2((top - higher) * factor)
            weights = jnp.exp2((scores - higher) * factor)
            total = total * fade + jnp.sum(weights, axis=0, keepdims=True)
            acc = acc * fade + lax.dot_general(
                block[:, HD:],
                weights.astype(BF),
                (((0,), (0,)), ((), ())),
                preferred_element_type=F32,
            )
            top = higher
    out_ref = rest[0]
    if last_call:
        out_ref[...] = (acc / total).T.astype(BF)
    else:
        out_ref[0:8, :] = jnp.broadcast_to(top, (8, count))
        out_ref[8:16, :] = jnp.broadcast_to(total, (8, count))
        out_ref[16:, :] = acc


def attend(info, queries, groups, carry, last_call):
    arrays = [array for array, _, _ in groups]
    shape = [(offset, own) for _, offset, own in groups]
    operands = [info, queries] + arrays + ([] if carry is None else [carry])
    vmem = pl.BlockSpec(memory_space=pltpu.VMEM)
    count = queries.shape[0]
    keys = sum(a.shape[0] for a in arrays)
    if last_call:
        out = jax.ShapeDtypeStruct((count, HD), BF)
    else:
        out = jax.ShapeDtypeStruct((HD + 16, count), F32)
    return pl.pallas_call(
        functools.partial(attend_kernel, shape, carry is None, last_call),
        out_shape=out,
        in_specs=[pl.BlockSpec(memory_space=pltpu.SMEM)] + [vmem] * (len(operands) - 1),
        out_specs=vmem,
        compiler_params=pltpu.CompilerParams(vmem_limit_bytes=40 * 1024 * 1024),
        cost_estimate=pl.CostEstimate(
            flops=4 * count * keys * HD,
            bytes_accessed=keys * 512,
            transcendentals=count * keys,
        ),
    )(*operands)


def shards(latents, conv_w, embed_w, text_emb, wqkv, seg_ids):
    z, y, c, x = (lax.axis_index(a) for a in ("z", "y", "c", "mp"))
    place = z * 8 + y * 2 + c
    pieces = embed_pieces(embed_w, c)

    other = swap(latents)
    chip = jnp.concatenate(
        [jnp.where(c == 0, latents, other), jnp.where(c == 0, other, latents)], axis=0
    )
    moves = [(i, i - 1) for i in range(2, 64, 2)] + [(i, i + 1) for i in range(1, 62, 2)]
    beside = lax.ppermute(jnp.where(c == 0, chip[:3], chip[1:]), SEQ, moves)
    below = swap(beside[:1])

    seg_ids, _ = lax.optimization_barrier((seg_ids, beside))
    positions = jnp.arange(seg_ids.shape[0], dtype=jnp.int32)
    start = jnp.min(jnp.where(seg_ids == 1, positions, seg_ids.shape[0])).astype(jnp.int32)
    info = jnp.stack([z, y, c, x, start]).astype(jnp.int32)

    rows = jnp.where(
        c == 0,
        jnp.concatenate([beside[2:], chip, below], axis=0),
        jnp.concatenate([chip[1:], beside], axis=0),
    )
    conv = lax.conv_general_dilated(
        rows[None],
        conv_w,
        (1, 1),
        ((0, 0), (1, 1)),
        dimension_numbers=("NHWC", "HWIO", "NHWC"),
        preferred_element_type=F32,
    )[0]
    own = lax.dynamic_slice_in_dim(rows[1:5], x * 64, 64, 2)
    mixed = (own.astype(F32) + jax.nn.silu(conv)).astype(BF)
    pair = mixed.reshape(2, 2, 64, 2, 64).transpose(0, 2, 1, 3, 4).reshape(TOK, 256)
    unit = lax.shift_right_logical(start, 6)

    rows = spread_patches(pair, unit)
    own_w = call(
        block_kernel, jax.ShapeDtypeStruct((512, 128), BF), [tied(info, rows)] + pieces
    )
    own_x = swap(own_w)
    both = jnp.concatenate([own_w, own_x], axis=0)
    near_1, near_2 = along(both, 1), along(both, 2)
    rows, _ = lax.optimization_barrier((rows, both))
    placed = shift_patches(rows, unit)
    near_2, placed = lax.optimization_barrier((near_2, placed))
    patches = [placed] + [shift(placed, "mp", -t) for t in (1, 2, 3)]
    far_3, far_4 = along(near_2, 1), along(near_2[:512], 2)
    blocks, patches = lax.optimization_barrier(((near_1, near_2, far_3, far_4), patches))
    operands = [info, text_emb, *patches, own_w, own_x]
    for block in blocks:
        operands += [block, swap(block)]
    hidden = call(
        hidden_kernel, jax.ShapeDtypeStruct((TOK, 1024), BF), operands, 2 * TOK * 1024 * 1024
    )

    carry = project(info, hidden, wqkv)
    parts = [carry[0]] + [shift(carry[t], "y", t) for t in (1, 2, 3)]
    head = jnp.concatenate(parts, axis=0)
    queries, keys_values = head[:, :HD], head[:, HD:]

    block = jnp.concatenate([keys_values, swap(keys_values)], axis=0)
    group = [(block, 0, True)]
    block = along(block, 1)
    carry = None
    for step in range(1, 4):
        carry = attend(info, queries, group, carry, False)
        block, carry = lax.optimization_barrier((block, carry))
        group = [(block, -step, True), (swap(block), step, False)]
        block = along(block if step < 3 else block[:512], 1)
    carry = attend(info, queries, group, carry, False)
    block, carry = lax.optimization_barrier((block, carry))
    last = jnp.concatenate([block, swap(block)], axis=0)
    carry = attend(info, queries, [(last, -4, True)], carry, True)
    back = [carry[:TOK]]
    for t in range(1, NY):
        back.append(shift(carry[t * TOK : (t + 1) * TOK], "y", -t))
    return ordered(back, y).transpose(1, 0, 2).reshape(TOK, 4 * HD)


def solution(mesh):
    inner = Mesh(mesh.devices.reshape(NZ, NY, NC, NX), ("z", "y", "c", "mp"))
    return jax.shard_map(
        shards,
        mesh=inner,
        in_specs=(
            P(SEQ, None, None),
            P(None, None, None, "mp"),
            P(None, "mp", SEQ),
            P(SEQ, "mp"),
            P(None, None, "mp"),
            P(),
        ),
        out_specs=P(SEQ, "mp"),
        check_vma=False,
    )
```

```python
import functools
import itertools
import math

import jax
import jax.numpy as jnp
from jax import lax
from jax.experimental import pallas as pl
from jax.experimental.pallas import tpu as pltpu
from jax.sharding import Mesh
from jax.sharding import PartitionSpec as P

NZ, NY, NC, NX = 8, 4, 2, 4
HD = 128
TOK = 128
IMG = 4096
SEQ = ("z", "y", "c")
SIZES = {"z": NZ, "y": NY, "c": NC, "mp": NX}
BF = jnp.bfloat16
F32 = jnp.float32


def shift(value, axis, step):
    count = SIZES[axis]
    return lax.ppermute(value, axis, [(i, (i + step) % count) for i in range(count)])


def ordered(pieces, first):
    count = len(pieces)
    twice = jnp.stack(pieces + pieces)
    return lax.dynamic_slice_in_dim(twice, (count - first) & (count - 1), count, 0)


def tied(info, other):
    return lax.optimization_barrier((info, other))[0]


def along(value, step):
    perm = []
    for z in range(NZ):
        perm.append((z * 2, (z + step) % NZ * 2))
        perm.append((z * 2 + 1, (z - step) % NZ * 2 + 1))
    return lax.ppermute(value, ("z", "c"), perm)


def swap(value):
    return shift(value, "c", 1)


def call(kernel, out_shape, operands, flops=0, limit=40):
    vmem = pl.BlockSpec(memory_space=pltpu.VMEM)
    size = sum(a.size * a.dtype.itemsize for a in operands)
    return pl.pallas_call(
        kernel,
        out_shape=out_shape,
        in_specs=[pl.BlockSpec(memory_space=pltpu.SMEM)] + [vmem] * (len(operands) - 1),
        out_specs=jax.tree.map(lambda _: vmem, out_shape),
        compiler_params=pltpu.CompilerParams(vmem_limit_bytes=limit * 1024 * 1024),
        cost_estimate=pl.CostEstimate(flops=flops, bytes_accessed=size, transcendentals=0),
    )(*operands)


def block_kernel(info, p0, p1, out):
    odd = lax.rem(info[1], 2)
    first = jnp.where(odd == 0, p0[...], p1[...])
    second = jnp.where(odd == 0, p1[...], p0[...])
    for a, value in enumerate((first, second)):
        for half in range(2):
            row = a * 256 + half * 128
            low = half * 64
            out[row : row + 128, :] = jnp.concatenate(
                [value[:, low : low + 64], value[:, 128 + low : 192 + low]], axis=1
            )


def flat(z, y, c, x):
    return ((z * NY + y) * NC + c) * NX + x


def embed_pieces(embed_w, c):
    cells = embed_w.reshape(2, 128, 64)
    packed = jnp.concatenate([cells[0], cells[1]], axis=1)
    other = swap(packed)
    both = jnp.concatenate(
        [jnp.where(c == 0, packed, other), jnp.where(c == 0, other, packed)], axis=1
    )
    pieces = []
    for k in range(2):
        perm = []
        for z, y, c, x in itertools.product(range(NZ), range(NY), range(NC), range(NX)):
            to = ((z + 2 * y) % NZ, (2 * c + k + x % 2) % NY, x // 2, z // 2)
            perm.append((flat(z, y, c, x), flat(*to)))
        pieces.append(lax.ppermute(both, ("z", "y", "c", "mp"), perm))
    return pieces


OFFSETS = (0, -1, 1, -2, 2, -3, 3, 4)


def hidden_kernel(info, text, p0, p1, p2, p3, own, own_x, d1, x1, d2, x2, d3, x3, d4, x4, out):
    z, y, c, x, start = info[0], info[1], info[2], info[3], info[4]
    pieces = [p0[...], p1[...], p2[...], p3[...]]
    base = (z * 8 + y * 2 + c) * TOK
    late = base - start == -64
    pos = base + lax.broadcasted_iota(jnp.int32, (TOK, 128), 0)
    is_text = (pos < start) | (pos >= start + IMG)

    def features(m):
        t = lax.rem(m - x + NX, NX)
        value = pieces[0]
        for i in range(1, NX):
            value = jnp.where(t == i, pieces[i], value)
        return jnp.where(late, jnp.concatenate([value[64:], value[:64]], axis=0), value)

    mine = jnp.concatenate([features(2 * c), features(2 * c + 1)], axis=1)
    other = jnp.concatenate([features(2 - 2 * c), features(3 - 2 * c)], axis=1)
    pairs = [
        (own[...], own_x[...]),
        (d1[:512, :], d1[512:, :]),
        (x1[512:, :], x1[:512, :]),
        (d2[:512, :], d2[512:, :]),
        (x2[512:, :], x2[:512, :]),
        (d3[:512, :], d3[512:, :]),
        (x3[512:, :], x3[:512, :]),
        (d4[...], x4[...]),
    ]
    for at, (first, second) in enumerate(pairs):
        part = jnp.dot(mine, first, preferred_element_type=F32)
        part = part + jnp.dot(other, second, preferred_element_type=F32)
        zone = z + OFFSETS[at] * (1 - 2 * c) + NZ
        place = lax.rem(zone - 2 * x + NZ, NZ)
        place = 4 * (place & 1) + lax.shift_right_logical(place, 1)
        cols = pl.ds(pl.multiple_of(place * 128, 128), 128)
        out[:, cols] = jnp.where(is_text, text[:, cols], part.astype(BF))


ARRIVALS = (0, 1, 3, 2)


def qkv_first(info, hidden, wqkv, total, w1, w2, w3, w0, sems):
    x = info[3]
    copies = []
    for n, t in enumerate(ARRIVALS):
        target = (w0, w1, w2, w3)[t]
        for j in range(3):
            for h in range(4):
                row = lax.rem(x + t, NX) * 1024 + h * 256
                copies.append(
                    pltpu.make_async_copy(
                        wqkv.at[j, pl.ds(pl.multiple_of(row, 256), 256), :],
                        target.at[j, pl.ds(h * 256, 256), :],
                        sems.at[n * 12 + j * 4 + h],
                    )
                )
    for copy in copies:
        copy.start()
    for copy in copies[:12]:
        copy.wait()
    for j in range(3):
        cols = slice(j * 512, (j + 1) * 512)
        total[:, cols] = jnp.dot(hidden[...], w0[j], preferred_element_type=F32)
    for copy in copies[12:]:
        copy.wait()


def qkv_next(info, hidden, weight, carry, out):
    for j in range(3):
        cols = slice(j * 512, (j + 1) * 512)
        out[:, cols] = carry[:, cols] + jnp.dot(
            hidden[...], weight[j], preferred_element_type=F32
        )


def qkv_last(info, hidden, weight, carry, o0, o1, o2, o3, total):
    qkv_next(info, hidden, weight, carry, total)
    for k, out in enumerate((o0, o1, o2, o3)):
        head = lax.rem(info[1] + k, NY)
        for j in range(3):
            value = total[:, pl.ds(pl.multiple_of(j * 512 + head * 128, 128), 128)]
            out[:, j * 128 : (j + 1) * 128] = value.astype(BF)


def project(info, hidden, wqkv):
    vmem = pl.BlockSpec(memory_space=pltpu.VMEM)
    smem = pl.BlockSpec(memory_space=pltpu.SMEM)
    weight = jax.ShapeDtypeStruct((3, 1024, 512), BF)
    total = jax.ShapeDtypeStruct((TOK, 1536), F32)
    flops = 2 * TOK * 1024 * 1536
    carry, *weights = pl.pallas_call(
        qkv_first,
        out_shape=[total, weight, weight, weight],
        in_specs=[smem, vmem, pl.BlockSpec(memory_space=pl.ANY)],
        out_specs=[vmem] * 4,
        scratch_shapes=[pltpu.VMEM((3, 1024, 512), BF), pltpu.SemaphoreType.DMA((48,))],
        compiler_params=pltpu.CompilerParams(vmem_limit_bytes=32 * 1024 * 1024),
        cost_estimate=pl.CostEstimate(
            flops=flops, bytes_accessed=24 << 20, transcendentals=0
        ),
    )(info, hidden, jnp.transpose(wqkv, (1, 0, 2)))
    for t in ARRIVALS[1:]:
        last = t == 2
        head = jax.ShapeDtypeStruct((TOK, 3 * HD), BF)
        carry = pl.pallas_call(
            qkv_last if last else qkv_next,
            out_shape=[head] * NY if last else total,
            in_specs=[smem] + [vmem] * 3,
            out_specs=[vmem] * NY if last else vmem,
            scratch_shapes=[pltpu.VMEM((TOK, 1536), F32)] if last else [],
            compiler_params=pltpu.CompilerParams(vmem_limit_bytes=24 * 1024 * 1024),
            cost_estimate=pl.CostEstimate(
                flops=flops, bytes_accessed=5 << 20, transcendentals=0
            ),
        )(info, shift(hidden, "mp", -t), weights[t - 1], carry)
    return carry


def spread_patches(pair, unit):
    def spread(low_shift, parity):
        moves = [(s, 16 + low_shift + (s + parity) // 2) for s in range(parity, 64, 2)]
        if parity:
            moves.append((0, 16 + low_shift))
        return lambda rows: lax.ppermute(rows, SEQ, moves)

    return lax.switch(unit & 7, [spread(i // 2, i % 2) for i in range(8)], pair)


def shift_patches(rows, unit):
    def moved(high):
        if high == 0:
            return lambda rows: rows
        moves = [(s, s + 4 * high) for s in range(64) if 0 <= s + 4 * high < 64]
        return lambda rows: lax.ppermute(rows, SEQ, moves)

    return lax.switch(lax.shift_right_logical(unit, 3), [moved(i - 4) for i in range(9)], rows)


FACTOR = HD**-0.5 * math.log2(math.e)


def attend_kernel(groups, first_call, last_call, info, q0, q1, *refs):
    z, y, c, start = info[0], info[1], info[2], info[4]
    kv_refs = refs[: len(groups)]
    rest = refs[len(groups) :]
    queries = jnp.concatenate([q0[...], q1[...]], axis=0)
    count = queries.shape[0]
    if first_call:
        top = jnp.full((1, count), -1e30, F32)
        total = jnp.zeros((1, count), F32)
        acc = jnp.zeros((HD, count), F32)
    else:
        top, total, acc = rest[0][0:1, :], rest[0][8:9, :], rest[0][16:, :]
        rest = rest[1:]
    lanes = lax.broadcasted_iota(jnp.int32, (1, TOK), 1)
    limits = []
    for core in (c, 1 - c):
        for j in range(NY):
            pos = z * 1024 + lax.rem(y - j + NY, NY) * 256 + core * TOK + lanes
            inside = (pos >= start) & (pos < start + IMG)
            limits.append(jnp.where(inside, start + (IMG - 1), pos))
    limit = jnp.concatenate(limits, axis=1)
    rows = lax.broadcasted_iota(jnp.int32, (TOK, count), 0)
    for kv_ref, (offset, own_core) in zip(kv_refs, groups):
        core = c if own_core else 1 - c
        zone = lax.rem(z + offset * (1 - 2 * c) + NZ, NZ)
        block = kv_ref[...]
        scores = lax.dot_general(
            block[:, :HD], queries, (((1,), (1,)), ((), ())), preferred_element_type=F32
        )
        parts = []
        for j in range(NY):
            base = zone * 1024 + lax.rem(y - j + NY, NY) * 256 + core * TOK
            visible = rows <= limit - base
            parts.append(jnp.where(visible, scores[j * TOK : (j + 1) * TOK], -1e30))
        scores = jnp.concatenate(parts, axis=0)
        higher = jnp.maximum(top, jnp.max(scores, axis=0, keepdims=True))
        fade = jnp.exp2((top - higher) * FACTOR)
        weights = jnp.exp2((scores - higher) * FACTOR)
        total = total * fade + jnp.sum(weights, axis=0, keepdims=True)
        acc = acc * fade + lax.dot_general(
            block[:, HD:],
            weights.astype(BF),
            (((0,), (0,)), ((), ())),
            preferred_element_type=F32,
        )
        top = higher
    if last_call:
        spans = ((rest[0], slice(0, count // 2)), (rest[1], slice(count // 2, count)))
    else:
        spans = ((rest[0], slice(0, count)),)
    for out_ref, span in spans:
        width = out_ref.shape[1]
        out_ref[0:8, :] = jnp.broadcast_to(top[:, span], (8, width))
        out_ref[8:16, :] = jnp.broadcast_to(total[:, span], (8, width))
        out_ref[16:, :] = acc[:, span]


def merge_kernel(info, mine, other, out):
    higher = jnp.maximum(mine[0:1, :], other[0:1, :])
    fade = jnp.exp2((mine[0:1, :] - higher) * FACTOR)
    fade_x = jnp.exp2((other[0:1, :] - higher) * FACTOR)
    total = mine[8:9, :] * fade + other[8:9, :] * fade_x
    acc = mine[16:, :] * fade + other[16:, :] * fade_x
    out[...] = (acc / total).T.astype(BF)


def attend(info, queries, group, carry, last_call):
    arrays = [array for array, _, _ in group]
    shape = [(offset, own) for _, offset, own in group]
    operands = [info, *queries] + arrays + ([] if carry is None else [carry])
    vmem = pl.BlockSpec(memory_space=pltpu.VMEM)
    count = 2 * queries[0].shape[0]
    keys = sum(a.shape[0] for a in arrays)
    if last_call:
        out = [jax.ShapeDtypeStruct((HD + 16, count // 2), F32)] * 2
    else:
        out = jax.ShapeDtypeStruct((HD + 16, count), F32)
    return pl.pallas_call(
        functools.partial(attend_kernel, shape, carry is None, last_call),
        out_shape=out,
        in_specs=[pl.BlockSpec(memory_space=pltpu.SMEM)] + [vmem] * (len(operands) - 1),
        out_specs=[vmem] * 2 if last_call else vmem,
        compiler_params=pltpu.CompilerParams(vmem_limit_bytes=40 * 1024 * 1024),
        cost_estimate=pl.CostEstimate(
            flops=4 * count * keys * HD,
            bytes_accessed=keys * 512,
            transcendentals=count * keys,
        ),
    )(*operands)


def shards(latents, conv_w, embed_w, text_emb, wqkv, seg_ids):
    z, y, c, x = (lax.axis_index(a) for a in ("z", "y", "c", "mp"))
    place = z * 8 + y * 2 + c
    pieces = embed_pieces(embed_w, c)

    other = swap(latents)
    chip = jnp.concatenate(
        [jnp.where(c == 0, latents, other), jnp.where(c == 0, other, latents)], axis=0
    )
    moves = [(i, i - 1) for i in range(2, 64, 2)] + [(i, i + 1) for i in range(1, 62, 2)]
    beside = lax.ppermute(jnp.where(c == 0, chip[:3], chip[1:]), SEQ, moves)
    below = swap(beside[:1])

    seg_ids, _ = lax.optimization_barrier((seg_ids, beside))
    positions = jnp.arange(seg_ids.shape[0], dtype=jnp.int32)
    start = jnp.min(jnp.where(seg_ids == 1, positions, seg_ids.shape[0])).astype(jnp.int32)
    info = jnp.stack([z, y, c, x, start]).astype(jnp.int32)

    rows = jnp.where(
        c == 0,
        jnp.concatenate([beside[2:], chip, below], axis=0),
        jnp.concatenate([chip[1:], beside], axis=0),
    )
    conv = lax.conv_general_dilated(
        rows[None],
        conv_w,
        (1, 1),
        ((0, 0), (1, 1)),
        dimension_numbers=("NHWC", "HWIO", "NHWC"),
        preferred_element_type=F32,
    )[0]
    own = lax.dynamic_slice_in_dim(rows[1:5], x * 64, 64, 2)
    mixed = (own.astype(F32) + jax.nn.silu(conv)).astype(BF)
    pair = mixed.reshape(2, 2, 64, 2, 64).transpose(0, 2, 1, 3, 4).reshape(TOK, 256)
    unit = lax.shift_right_logical(start, 6)

    rows = spread_patches(pair, unit)
    own_w = call(
        block_kernel, jax.ShapeDtypeStruct((512, 128), BF), [tied(info, rows)] + pieces
    )
    own_x = swap(own_w)
    both = jnp.concatenate([own_w, own_x], axis=0)
    near_1, near_2 = along(both, 1), along(both, 2)
    rows, _ = lax.optimization_barrier((rows, both))
    placed = shift_patches(rows, unit)
    near_2, placed = lax.optimization_barrier((near_2, placed))
    patches = [placed] + [shift(placed, "mp", -t) for t in (1, 2, 3)]
    far_3, far_4 = along(near_2, 1), along(near_2[:512], 2)
    blocks, patches = lax.optimization_barrier(((near_1, near_2, far_3, far_4), patches))
    operands = [info, text_emb, *patches, own_w, own_x]
    for block in blocks:
        operands += [block, swap(block)]
    hidden = call(
        hidden_kernel, jax.ShapeDtypeStruct((TOK, 1024), BF), operands, 2 * TOK * 1024 * 1024
    )

    carry = project(info, hidden, wqkv)
    parts = [carry[0]] + [shift(carry[t], "y", t) for t in (1, 2, 3)]
    head = jnp.concatenate(parts, axis=0)
    other = swap(head)

    queries = (head[:, :HD], other[:, :HD])
    group = [(head[:, HD:], 0, True)]
    pair = (along(head[:, HD:], 1), along(other[:, HD:], 1))
    carry = None
    for step in range(1, 4):
        carry = attend(info, queries, group, carry, False)
        group, sent = [], []
        for block, own in zip(pair, (True, False)):
            block, carry = lax.optimization_barrier((block, carry))
            if own or step < 3:
                sent.append(along(block, 1))
            group.append((block, -step, own))
        pair = sent
    carry = attend(info, queries, group, carry, False)
    last, carry = lax.optimization_barrier((pair[0], carry))
    mine, other = attend(info, queries, [(last, -4, True)], carry, True)
    carry = call(
        merge_kernel, jax.ShapeDtypeStruct((NY * TOK, HD), BF), [info, mine, swap(other)]
    )
    back = [carry[:TOK]]
    for t in range(1, NY):
        back.append(shift(carry[t * TOK : (t + 1) * TOK], "y", -t))
    return ordered(back, y).transpose(1, 0, 2).reshape(TOK, 4 * HD)


def solution(mesh):
    inner = Mesh(mesh.devices.reshape(NZ, NY, NC, NX), ("z", "y", "c", "mp"))
    return jax.shard_map(
        shards,
        mesh=inner,
        in_specs=(
            P(SEQ, None, None),
            P(None, None, None, "mp"),
            P(None, "mp", SEQ),
            P(SEQ, "mp"),
            P(None, None, "mp"),
            P(),
        ),
        out_specs=P(SEQ, "mp"),
        check_vma=False,
    )
```

```python
import functools
import itertools
import math

import jax
import jax.numpy as jnp
from jax import lax
from jax.experimental import pallas as pl
from jax.experimental.pallas import tpu as pltpu
from jax.sharding import Mesh
from jax.sharding import PartitionSpec as P

NZ, NY, NC, NX = 8, 4, 2, 4
HD = 128
TOK = 128
IMG = 4096
SEQ = ("z", "y", "c")
SIZES = {"z": NZ, "y": NY, "c": NC, "mp": NX}
BF = jnp.bfloat16
F32 = jnp.float32


def shift(value, axis, step):
    count = SIZES[axis]
    return lax.ppermute(value, axis, [(i, (i + step) % count) for i in range(count)])


def ordered(pieces, first):
    count = len(pieces)
    twice = jnp.stack(pieces + pieces)
    return lax.dynamic_slice_in_dim(twice, (count - first) & (count - 1), count, 0)


def tied(info, other):
    return lax.optimization_barrier((info, other))[0]


def along(value, step):
    perm = []
    for z in range(NZ):
        perm.append((z * 2, (z + step) % NZ * 2))
        perm.append((z * 2 + 1, (z - step) % NZ * 2 + 1))
    return lax.ppermute(value, ("z", "c"), perm)


def swap(value):
    return shift(value, "c", 1)


def call(kernel, out_shape, operands, flops=0, limit=40):
    vmem = pl.BlockSpec(memory_space=pltpu.VMEM)
    size = sum(a.size * a.dtype.itemsize for a in operands)
    return pl.pallas_call(
        kernel,
        out_shape=out_shape,
        in_specs=[pl.BlockSpec(memory_space=pltpu.SMEM)] + [vmem] * (len(operands) - 1),
        out_specs=jax.tree.map(lambda _: vmem, out_shape),
        compiler_params=pltpu.CompilerParams(vmem_limit_bytes=limit * 1024 * 1024),
        cost_estimate=pl.CostEstimate(flops=flops, bytes_accessed=size, transcendentals=0),
    )(*operands)


def block_kernel(info, p0, p1, out):
    odd = lax.rem(info[1], 2)
    first = jnp.where(odd == 0, p0[...], p1[...])
    second = jnp.where(odd == 0, p1[...], p0[...])
    for a, value in enumerate((first, second)):
        for half in range(2):
            row = a * 256 + half * 128
            low = half * 64
            out[row : row + 128, :] = jnp.concatenate(
                [value[:, low : low + 64], value[:, 128 + low : 192 + low]], axis=1
            )


def flat(z, y, c, x):
    return ((z * NY + y) * NC + c) * NX + x


def embed_pieces(embed_w, c, first):
    cells = embed_w.reshape(2, 128, 64)
    packed = jnp.concatenate([cells[0], cells[1]], axis=1)
    other = swap(packed)
    both = jnp.concatenate(
        [jnp.where(c == 0, packed, other), jnp.where(c == 0, other, packed)], axis=1
    )
    both, _ = lax.optimization_barrier((both, first))
    pieces = []
    for k in range(2):
        perm = []
        for z, y, c, x in itertools.product(range(NZ), range(NY), range(NC), range(NX)):
            to = ((z + 2 * y) % NZ, (2 * c + k + x % 2) % NY, x // 2, z // 2)
            perm.append((flat(z, y, c, x), flat(*to)))
        pieces.append(lax.ppermute(both, ("z", "y", "c", "mp"), perm))
    return pieces


OFFSETS = (0, -1, 1, -2, 2, -3, 3, 4)


def hidden_kernel(info, text, p0, p1, p2, p3, own, own_x, d1, x1, d2, x2, d3, x3, d4, x4, out):
    z, y, c, x, start = info[0], info[1], info[2], info[3], info[4]
    pieces = [p0[...], p1[...], p2[...], p3[...]]
    base = (z * 8 + y * 2 + c) * TOK
    late = base - start == -64
    pos = base + lax.broadcasted_iota(jnp.int32, (TOK, 128), 0)
    is_text = (pos < start) | (pos >= start + IMG)

    def features(m):
        t = lax.rem(m - x + NX, NX)
        value = pieces[0]
        for i in range(1, NX):
            value = jnp.where(t == i, pieces[i], value)
        return jnp.where(late, jnp.concatenate([value[64:], value[:64]], axis=0), value)

    mine = jnp.concatenate([features(2 * c), features(2 * c + 1)], axis=1)
    other = jnp.concatenate([features(2 - 2 * c), features(3 - 2 * c)], axis=1)
    pairs = [
        (own[...], own_x[...]),
        (d1[:512, :], d1[512:, :]),
        (x1[512:, :], x1[:512, :]),
        (d2[:512, :], d2[512:, :]),
        (x2[512:, :], x2[:512, :]),
        (d3[:512, :], d3[512:, :]),
        (x3[512:, :], x3[:512, :]),
        (d4[...], x4[...]),
    ]
    for at, (first, second) in enumerate(pairs):
        part = jnp.dot(mine, first, preferred_element_type=F32)
        part = part + jnp.dot(other, second, preferred_element_type=F32)
        zone = z + OFFSETS[at] * (1 - 2 * c) + NZ
        place = lax.rem(zone - 2 * x + NZ, NZ)
        place = 4 * (place & 1) + lax.shift_right_logical(place, 1)
        cols = pl.ds(pl.multiple_of(place * 128, 128), 128)
        out[:, cols] = jnp.where(is_text, text[:, cols], part.astype(BF))


ARRIVALS = (0, 1, 3, 2)


def qkv_first(info, hidden, wqkv, total, w1, w2, w3, w0, sems):
    x = info[3]
    copies = []
    for n, t in enumerate(ARRIVALS):
        target = (w0, w1, w2, w3)[t]
        for j in range(3):
            for h in range(4):
                row = lax.rem(x + t, NX) * 1024 + h * 256
                copies.append(
                    pltpu.make_async_copy(
                        wqkv.at[j, pl.ds(pl.multiple_of(row, 256), 256), :],
                        target.at[j, pl.ds(h * 256, 256), :],
                        sems.at[n * 12 + j * 4 + h],
                    )
                )
    for copy in copies:
        copy.start()
    for copy in copies[:12]:
        copy.wait()
    for j in range(3):
        cols = slice(j * 512, (j + 1) * 512)
        total[:, cols] = jnp.dot(hidden[...], w0[j], preferred_element_type=F32)
    for copy in copies[12:]:
        copy.wait()


def qkv_next(info, hidden, weight, carry, out):
    for j in range(3):
        cols = slice(j * 512, (j + 1) * 512)
        out[:, cols] = carry[:, cols] + jnp.dot(
            hidden[...], weight[j], preferred_element_type=F32
        )


def qkv_last(info, hidden, weight, carry, o0, o1, o2, o3, total):
    qkv_next(info, hidden, weight, carry, total)
    for k, out in enumerate((o0, o1, o2, o3)):
        head = lax.rem(info[1] + k, NY)
        for j in range(3):
            value = total[:, pl.ds(pl.multiple_of(j * 512 + head * 128, 128), 128)]
            out[:, j * 128 : (j + 1) * 128] = value.astype(BF)


def project(info, hidden, wqkv):
    vmem = pl.BlockSpec(memory_space=pltpu.VMEM)
    smem = pl.BlockSpec(memory_space=pltpu.SMEM)
    weight = jax.ShapeDtypeStruct((3, 1024, 512), BF)
    total = jax.ShapeDtypeStruct((TOK, 1536), F32)
    flops = 2 * TOK * 1024 * 1536
    carry, *weights = pl.pallas_call(
        qkv_first,
        out_shape=[total, weight, weight, weight],
        in_specs=[smem, vmem, pl.BlockSpec(memory_space=pl.ANY)],
        out_specs=[vmem] * 4,
        scratch_shapes=[pltpu.VMEM((3, 1024, 512), BF), pltpu.SemaphoreType.DMA((48,))],
        compiler_params=pltpu.CompilerParams(vmem_limit_bytes=32 * 1024 * 1024),
        cost_estimate=pl.CostEstimate(
            flops=flops, bytes_accessed=24 << 20, transcendentals=0
        ),
    )(info, hidden, jnp.transpose(wqkv, (1, 0, 2)))
    after, before = shift(hidden, "mp", -1), shift(hidden, "mp", 1)
    after, before, carry = lax.optimization_barrier((after, before, carry))
    moves = []
    for x in range(NX):
        moves.append((x, (x - 1) % NX))
        moves.append((NX + x, NX + (x + 1) % NX))
    relayed = lax.ppermute(jnp.where(lax.axis_index("c") == 0, after, before), ("c", "mp"), moves)
    arrived = {1: after, 3: before, 2: relayed}
    for t in ARRIVALS[1:]:
        last = t == 2
        head = jax.ShapeDtypeStruct((TOK, 3 * HD), BF)
        carry = pl.pallas_call(
            qkv_last if last else qkv_next,
            out_shape=[head] * NY if last else total,
            in_specs=[smem] + [vmem] * 3,
            out_specs=[vmem] * NY if last else vmem,
            scratch_shapes=[pltpu.VMEM((TOK, 1536), F32)] if last else [],
            compiler_params=pltpu.CompilerParams(vmem_limit_bytes=24 * 1024 * 1024),
            cost_estimate=pl.CostEstimate(
                flops=flops, bytes_accessed=5 << 20, transcendentals=0
            ),
        )(info, arrived[t], weights[t - 1], carry)
    return carry


def spread_patches(pair, unit):
    def spread(low_shift, parity):
        moves = [(s, 16 + low_shift + (s + parity) // 2) for s in range(parity, 64, 2)]
        if parity:
            moves.append((0, 16 + low_shift))
        return lambda rows: lax.ppermute(rows, SEQ, moves)

    return lax.switch(unit & 7, [spread(i // 2, i % 2) for i in range(8)], pair)


def shift_patches(rows, unit):
    def moved(high):
        if high == 0:
            return lambda rows: rows
        moves = [(s, s + 4 * high) for s in range(64) if 0 <= s + 4 * high < 64]
        return lambda rows: lax.ppermute(rows, SEQ, moves)

    return lax.switch(lax.shift_right_logical(unit, 3), [moved(i - 4) for i in range(9)], rows)


FACTOR = HD**-0.5 * math.log2(math.e)


def attend_kernel(groups, first_call, last_call, info, q0, q1, *refs):
    z, y, c, start = info[0], info[1], info[2], info[4]
    kv_refs = refs[: len(groups)]
    rest = refs[len(groups) :]
    queries = jnp.concatenate([q0[...], q1[...]], axis=0)
    count = queries.shape[0]
    state = rest[-1]
    if first_call:
        state[0:8, :] = jnp.full((8, count), -1e30, F32)
        state[8:, :] = jnp.zeros((HD + 8, count), F32)
    else:
        state[...] = rest[0][...]
        rest = rest[1:]
    lanes = lax.broadcasted_iota(jnp.int32, (1, TOK), 1)
    limits = []
    for core in (c, 1 - c):
        for j in range(NY):
            pos = z * 1024 + lax.rem(y - j + NY, NY) * 256 + core * TOK + lanes
            inside = (pos >= start) & (pos < start + IMG)
            limits.append(jnp.where(inside, start + (IMG - 1), pos))
    limit = jnp.concatenate(limits, axis=1)
    rows = lax.broadcasted_iota(jnp.int32, (TOK, count), 0)
    no_image = (z * 1024 + 1024 <= start) | (z * 1024 >= start + IMG)
    all_image = (z * 1024 >= start) & (z * 1024 + 1024 <= start + IMG)

    def add(kv_ref, zone, core, masked):
        scores = lax.dot_general(
            kv_ref[:, :HD], queries, (((1,), (1,)), ((), ())), preferred_element_type=F32
        )
        if masked:
            parts = []
            for j in range(NY):
                base = zone * 1024 + lax.rem(y - j + NY, NY) * 256 + core * TOK
                visible = rows <= limit - base
                parts.append(jnp.where(visible, scores[j * TOK : (j + 1) * TOK], -1e30))
            scores = jnp.concatenate(parts, axis=0)
        top = state[0:1, :]
        higher = jnp.maximum(top, jnp.max(scores, axis=0, keepdims=True))
        fade = jnp.exp2((top - higher) * FACTOR)
        weights = jnp.exp2((scores - higher) * FACTOR)
        total = state[8:9, :] * fade + jnp.sum(weights, axis=0, keepdims=True)
        state[16:, :] = state[16:, :] * fade + lax.dot_general(
            kv_ref[:, HD:],
            weights.astype(BF),
            (((0,), (0,)), ((), ())),
            preferred_element_type=F32,
        )
        state[0:8, :] = jnp.broadcast_to(higher, (8, count))
        state[8:16, :] = jnp.broadcast_to(total, (8, count))

    for kv_ref, (offset, own_core) in zip(kv_refs, groups):
        core = c if own_core else 1 - c
        zone = lax.rem(z + offset * (1 - 2 * c) + NZ, NZ)
        full = (zone < z) | (all_image & (zone * 1024 + 1024 <= start + IMG))
        empty = (zone > z) & (no_image | (zone * 1024 >= start + IMG))
        pl.when(full)(functools.partial(add, kv_ref, zone, core, False))
        pl.when(jnp.logical_not(full | empty))(functools.partial(add, kv_ref, zone, core, True))
    if last_call:
        rest[0][...] = state[:, : count // 2]
        rest[1][...] = state[:, count // 2 :]


def merge_kernel(info, mine, other, out):
    higher = jnp.maximum(mine[0:1, :], other[0:1, :])
    fade = jnp.exp2((mine[0:1, :] - higher) * FACTOR)
    fade_x = jnp.exp2((other[0:1, :] - higher) * FACTOR)
    total = mine[8:9, :] * fade + other[8:9, :] * fade_x
    acc = mine[16:, :] * fade + other[16:, :] * fade_x
    out[...] = (acc / total).T.astype(BF)


def attend(info, queries, group, carry, last_call):
    arrays = [array for array, _, _ in group]
    shape = [(offset, own) for _, offset, own in group]
    operands = [info, *queries] + arrays + ([] if carry is None else [carry])
    vmem = pl.BlockSpec(memory_space=pltpu.VMEM)
    count = 2 * queries[0].shape[0]
    keys = sum(a.shape[0] for a in arrays)
    if last_call:
        out = [jax.ShapeDtypeStruct((HD + 16, count // 2), F32)] * 2
    else:
        out = jax.ShapeDtypeStruct((HD + 16, count), F32)
    return pl.pallas_call(
        functools.partial(attend_kernel, shape, carry is None, last_call),
        out_shape=out,
        in_specs=[pl.BlockSpec(memory_space=pltpu.SMEM)] + [vmem] * (len(operands) - 1),
        out_specs=[vmem] * 2 if last_call else vmem,
        scratch_shapes=[pltpu.VMEM((HD + 16, count), F32)] if last_call else [],
        compiler_params=pltpu.CompilerParams(vmem_limit_bytes=40 * 1024 * 1024),
        cost_estimate=pl.CostEstimate(
            flops=4 * count * keys * HD,
            bytes_accessed=keys * 512,
            transcendentals=count * keys,
        ),
    )(*operands)


def shards(latents, conv_w, embed_w, text_emb, wqkv, seg_ids):
    z, y, c, x = (lax.axis_index(a) for a in ("z", "y", "c", "mp"))
    place = z * 8 + y * 2 + c
    other = swap(latents)
    chip = jnp.concatenate(
        [jnp.where(c == 0, latents, other), jnp.where(c == 0, other, latents)], axis=0
    )
    moves = [(i, i - 1) for i in range(2, 64, 2)] + [(i, i + 1) for i in range(1, 62, 2)]
    payload = jnp.where(c == 0, chip[:3], chip[1:])
    beside = lax.ppermute(payload, SEQ, moves)
    seg_ids, _ = lax.optimization_barrier((seg_ids, payload))
    positions = jnp.arange(seg_ids.shape[0], dtype=jnp.int32)
    start = jnp.min(jnp.where(seg_ids == 1, positions, seg_ids.shape[0])).astype(jnp.int32)
    info = jnp.stack([z, y, c, x, start]).astype(jnp.int32)
    beside, info = lax.optimization_barrier((beside, info))
    below = swap(beside[:1])

    pieces = embed_pieces(embed_w, c, beside)

    rows = jnp.where(
        c == 0,
        jnp.concatenate([beside[2:], chip, below], axis=0),
        jnp.concatenate([chip[1:], beside], axis=0),
    )
    conv = lax.conv_general_dilated(
        rows[None],
        conv_w,
        (1, 1),
        ((0, 0), (1, 1)),
        dimension_numbers=("NHWC", "HWIO", "NHWC"),
        preferred_element_type=F32,
    )[0]
    own = lax.dynamic_slice_in_dim(rows[1:5], x * 64, 64, 2)
    mixed = (own.astype(F32) + jax.nn.silu(conv)).astype(BF)
    pair = mixed.reshape(2, 2, 64, 2, 64).transpose(0, 2, 1, 3, 4).reshape(TOK, 256)
    unit = lax.shift_right_logical(start, 6)

    rows = spread_patches(pair, unit)
    own_w = call(
        block_kernel, jax.ShapeDtypeStruct((512, 128), BF), [tied(info, rows)] + pieces
    )
    own_x = swap(own_w)
    both = jnp.concatenate([own_w, own_x], axis=0)
    near_1, near_2 = along(both, 1), along(both, 2)
    rows, _ = lax.optimization_barrier((rows, both))
    placed = shift_patches(rows, unit)
    near_2, placed = lax.optimization_barrier((near_2, placed))
    patches = [placed] + [shift(placed, "mp", -t) for t in (1, 2, 3)]
    far_3, far_4 = along(near_2, 1), along(near_2[:512], 2)
    blocks, patches = lax.optimization_barrier(((near_1, near_2, far_3, far_4), patches))
    operands = [info, text_emb, *patches, own_w, own_x]
    for block in blocks:
        operands += [block, swap(block)]
    hidden = call(
        hidden_kernel, jax.ShapeDtypeStruct((TOK, 1024), BF), operands, 2 * TOK * 1024 * 1024
    )

    carry = project(info, hidden, wqkv)
    parts = [carry[0]] + [shift(carry[t], "y", t) for t in (1, 2, 3)]
    head = jnp.concatenate(parts, axis=0)
    other = swap(head)

    queries = (head[:, :HD], other[:, :HD])
    group = [(head[:, HD:], 0, True)]
    pair = (along(head[:, HD:], 1), along(other[:, HD:], 1))
    carry = None
    for step in range(1, 4):
        carry = attend(info, queries, group, carry, False)
        group, sent = [], []
        for block, own in zip(pair, (True, False)):
            block, carry = lax.optimization_barrier((block, carry))
            if own or step < 3:
                sent.append(along(block, 1))
            group.append((block, -step, own))
        pair = sent
    carry = attend(info, queries, group, carry, False)
    last, carry = lax.optimization_barrier((pair[0], carry))
    mine, other = attend(info, queries, [(last, -4, True)], carry, True)
    carry = call(
        merge_kernel, jax.ShapeDtypeStruct((NY * TOK, HD), BF), [info, mine, swap(other)]
    )
    back = [carry[:TOK]]
    for t in range(1, NY):
        back.append(shift(carry[t * TOK : (t + 1) * TOK], "y", -t))
    return ordered(back, y).transpose(1, 0, 2).reshape(TOK, 4 * HD)


def solution(mesh):
    inner = Mesh(mesh.devices.reshape(NZ, NY, NC, NX), ("z", "y", "c", "mp"))
    return jax.shard_map(
        shards,
        mesh=inner,
        in_specs=(
            P(SEQ, None, None),
            P(None, None, None, "mp"),
            P(None, "mp", SEQ),
            P(SEQ, "mp"),
            P(None, None, "mp"),
            P(),
        ),
        out_specs=P(SEQ, "mp"),
        check_vma=False,
    )
```

```python
import functools
import itertools
import math

import jax
import jax.numpy as jnp
from jax import lax
from jax.experimental import pallas as pl
from jax.experimental.pallas import tpu as pltpu
from jax.sharding import Mesh
from jax.sharding import PartitionSpec as P

NZ, NY, NC, NX = 8, 4, 2, 4
HD = 128
TOK = 128
IMG = 4096
SEQ = ("z", "y", "c")
SIZES = {"z": NZ, "y": NY, "c": NC, "mp": NX}
BF = jnp.bfloat16
F32 = jnp.float32


def shift(value, axis, step):
    count = SIZES[axis]
    return lax.ppermute(value, axis, [(i, (i + step) % count) for i in range(count)])


def ordered(pieces, first):
    count = len(pieces)
    twice = jnp.stack(pieces + pieces)
    return lax.dynamic_slice_in_dim(twice, (count - first) & (count - 1), count, 0)


def tied(info, other):
    return lax.optimization_barrier((info, other))[0]


def along(value, step):
    perm = []
    for z in range(NZ):
        perm.append((z * 2, (z + step) % NZ * 2))
        perm.append((z * 2 + 1, (z - step) % NZ * 2 + 1))
    return lax.ppermute(value, ("z", "c"), perm)


def swap(value):
    return shift(value, "c", 1)


def call(kernel, out_shape, operands, flops=0, limit=40):
    vmem = pl.BlockSpec(memory_space=pltpu.VMEM)
    size = sum(a.size * a.dtype.itemsize for a in operands)
    return pl.pallas_call(
        kernel,
        out_shape=out_shape,
        in_specs=[pl.BlockSpec(memory_space=pltpu.SMEM)] + [vmem] * (len(operands) - 1),
        out_specs=jax.tree.map(lambda _: vmem, out_shape),
        compiler_params=pltpu.CompilerParams(vmem_limit_bytes=limit * 1024 * 1024),
        cost_estimate=pl.CostEstimate(flops=flops, bytes_accessed=size, transcendentals=0),
    )(*operands)


def block_kernel(info, p0, p1, out):
    odd = lax.rem(info[1], 2)
    first = jnp.where(odd == 0, p0[...], p1[...])
    second = jnp.where(odd == 0, p1[...], p0[...])
    for a, value in enumerate((first, second)):
        for half in range(2):
            row = a * 256 + half * 128
            low = half * 64
            out[row : row + 128, :] = jnp.concatenate(
                [value[:, low : low + 64], value[:, 128 + low : 192 + low]], axis=1
            )


def flat(z, y, c, x):
    return ((z * NY + y) * NC + c) * NX + x


def embed_pieces(embed_w, c):
    cells = embed_w.reshape(2, 128, 64)
    packed = jnp.concatenate([cells[0], cells[1]], axis=1)
    other = swap(packed)
    both = jnp.concatenate(
        [jnp.where(c == 0, packed, other), jnp.where(c == 0, other, packed)], axis=1
    )
    pieces = []
    for k in range(2):
        perm = []
        for z, y, c, x in itertools.product(range(NZ), range(NY), range(NC), range(NX)):
            to = ((z + 2 * y) % NZ, (2 * c + k + x % 2) % NY, x // 2, z // 2)
            perm.append((flat(z, y, c, x), flat(*to)))
        pieces.append(lax.ppermute(both, ("z", "y", "c", "mp"), perm))
    return pieces


OFFSETS = (0, -1, 1, -2, 2, -3, 3, 4)


def hidden_kernel(info, text, p0, p1, p2, p3, own, own_x, d1, x1, d2, x2, d3, x3, d4, x4, out):
    z, y, c, x, start = info[0], info[1], info[2], info[3], info[4]
    pieces = [p0[...], p1[...], p2[...], p3[...]]
    base = (z * 8 + y * 2 + c) * TOK
    late = base - start == -64
    pos = base + lax.broadcasted_iota(jnp.int32, (TOK, 128), 0)
    is_text = (pos < start) | (pos >= start + IMG)

    def features(m):
        t = lax.rem(m - x + NX, NX)
        value = pieces[0]
        for i in range(1, NX):
            value = jnp.where(t == i, pieces[i], value)
        return jnp.where(late, jnp.concatenate([value[64:], value[:64]], axis=0), value)

    mine = jnp.concatenate([features(2 * c), features(2 * c + 1)], axis=1)
    other = jnp.concatenate([features(2 - 2 * c), features(3 - 2 * c)], axis=1)
    pairs = [
        (own[...], own_x[...]),
        (d1[:512, :], d1[512:, :]),
        (x1[512:, :], x1[:512, :]),
        (d2[:512, :], d2[512:, :]),
        (x2[512:, :], x2[:512, :]),
        (d3[:512, :], d3[512:, :]),
        (x3[512:, :], x3[:512, :]),
        (d4[...], x4[...]),
    ]
    for at, (first, second) in enumerate(pairs):
        part = jnp.dot(mine, first, preferred_element_type=F32)
        part = part + jnp.dot(other, second, preferred_element_type=F32)
        zone = z + OFFSETS[at] * (1 - 2 * c) + NZ
        place = lax.rem(zone - 2 * x + NZ, NZ)
        place = 4 * (place & 1) + lax.shift_right_logical(place, 1)
        cols = pl.ds(pl.multiple_of(place * 128, 128), 128)
        out[:, cols] = jnp.where(is_text, text[:, cols], part.astype(BF))


ARRIVALS = (0, 1, 3, 2)


def qkv_first(info, hidden, wqkv, total, w1, w2, w3, w0, sems):
    x = info[3]
    copies = []
    for n, t in enumerate(ARRIVALS):
        target = (w0, w1, w2, w3)[t]
        for j in range(3):
            for h in range(4):
                row = lax.rem(x + t, NX) * 1024 + h * 256
                copies.append(
                    pltpu.make_async_copy(
                        wqkv.at[j, pl.ds(pl.multiple_of(row, 256), 256), :],
                        target.at[j, pl.ds(h * 256, 256), :],
                        sems.at[n * 12 + j * 4 + h],
                    )
                )
    for copy in copies:
        copy.start()
    for copy in copies[:12]:
        copy.wait()
    for j in range(3):
        cols = slice(j * 512, (j + 1) * 512)
        total[:, cols] = jnp.dot(hidden[...], w0[j], preferred_element_type=F32)
    for copy in copies[12:]:
        copy.wait()


def qkv_next(info, hidden, weight, carry, out):
    for j in range(3):
        cols = slice(j * 512, (j + 1) * 512)
        out[:, cols] = carry[:, cols] + jnp.dot(
            hidden[...], weight[j], preferred_element_type=F32
        )


def qkv_last(info, hidden, weight, carry, o0, o1, o2, o3, total):
    qkv_next(info, hidden, weight, carry, total)
    for k, out in enumerate((o0, o1, o2, o3)):
        head = lax.rem(info[1] + k, NY)
        for j in range(3):
            value = total[:, pl.ds(pl.multiple_of(j * 512 + head * 128, 128), 128)]
            out[:, j * 128 : (j + 1) * 128] = value.astype(BF)


def project(info, hidden, wqkv):
    vmem = pl.BlockSpec(memory_space=pltpu.VMEM)
    smem = pl.BlockSpec(memory_space=pltpu.SMEM)
    weight = jax.ShapeDtypeStruct((3, 1024, 512), BF)
    total = jax.ShapeDtypeStruct((TOK, 1536), F32)
    flops = 2 * TOK * 1024 * 1536
    carry, *weights = pl.pallas_call(
        qkv_first,
        out_shape=[total, weight, weight, weight],
        in_specs=[smem, vmem, pl.BlockSpec(memory_space=pl.ANY)],
        out_specs=[vmem] * 4,
        scratch_shapes=[pltpu.VMEM((3, 1024, 512), BF), pltpu.SemaphoreType.DMA((48,))],
        compiler_params=pltpu.CompilerParams(vmem_limit_bytes=32 * 1024 * 1024),
        cost_estimate=pl.CostEstimate(
            flops=flops, bytes_accessed=24 << 20, transcendentals=0
        ),
    )(info, hidden, jnp.transpose(wqkv, (1, 0, 2)))
    after, before = shift(hidden, "mp", -1), shift(hidden, "mp", 1)
    after, before, carry = lax.optimization_barrier((after, before, carry))
    moves = []
    for x in range(NX):
        moves.append((x, (x - 1) % NX))
        moves.append((NX + x, NX + (x + 1) % NX))
    relayed = lax.ppermute(jnp.where(lax.axis_index("c") == 0, after, before), ("c", "mp"), moves)
    arrived = {1: after, 3: before, 2: relayed}
    for t in ARRIVALS[1:]:
        last = t == 2
        head = jax.ShapeDtypeStruct((TOK, 3 * HD), BF)
        carry = pl.pallas_call(
            qkv_last if last else qkv_next,
            out_shape=[head] * NY if last else total,
            in_specs=[smem] + [vmem] * 3,
            out_specs=[vmem] * NY if last else vmem,
            scratch_shapes=[pltpu.VMEM((TOK, 1536), F32)] if last else [],
            compiler_params=pltpu.CompilerParams(vmem_limit_bytes=24 * 1024 * 1024),
            cost_estimate=pl.CostEstimate(
                flops=flops, bytes_accessed=5 << 20, transcendentals=0
            ),
        )(info, arrived[t], weights[t - 1], carry)
    return carry


def spread_patches(pair, unit):
    def spread(low_shift, parity):
        moves = [(s, 16 + low_shift + (s + parity) // 2) for s in range(parity, 64, 2)]
        if parity:
            moves.append((0, 16 + low_shift))
        return lambda rows: lax.ppermute(rows, SEQ, moves)

    return lax.switch(unit & 7, [spread(i // 2, i % 2) for i in range(8)], pair)


def shift_patches(rows, unit):
    def moved(high):
        if high == 0:
            return lambda rows: rows
        moves = [(s, s + 4 * high) for s in range(64) if 0 <= s + 4 * high < 64]
        return lambda rows: lax.ppermute(rows, SEQ, moves)

    return lax.switch(lax.shift_right_logical(unit, 3), [moved(i - 4) for i in range(9)], rows)


FACTOR = HD**-0.5 * math.log2(math.e)


def attend_kernel(cores, offset, first_call, last_call, info, queries, *refs):
    z, y, c, start = info[0], info[1], info[2], info[4]
    kv_refs = refs[: len(cores)]
    rest = refs[len(cores) :]
    count = queries.shape[0]
    state = rest[-1]
    if first_call:
        before = None
    else:
        before, rest = rest[0], rest[1:]
    zone = lax.rem(z + offset * (1 - 2 * c) + NZ, NZ)
    no_image = (z * 1024 + 1024 <= start) | (z * 1024 >= start + IMG)
    all_image = (z * 1024 >= start) & (z * 1024 + 1024 <= start + IMG)
    full = (zone < z) | (all_image & (zone * 1024 + 1024 <= start + IMG))
    empty = (zone > z) & (no_image | (zone * 1024 >= start + IMG))

    def limits():
        lanes = lax.broadcasted_iota(jnp.int32, (1, TOK), 1)
        found = []
        for core in (c, 1 - c):
            for j in range(NY):
                pos = z * 1024 + lax.rem(y - j + NY, NY) * 256 + core * TOK + lanes
                inside = (pos >= start) & (pos < start + IMG)
                found.append(jnp.where(inside, start + (IMG - 1), pos))
        return jnp.concatenate(found, axis=1)

    def add(masked):
        if masked:
            limit = limits()
            rows = lax.broadcasted_iota(jnp.int32, (TOK, count), 0)
        found = []
        for kv_ref, own_core in zip(kv_refs, cores):
            scores = lax.dot_general(
                kv_ref[:, :HD],
                queries[...],
                (((1,), (1,)), ((), ())),
                preferred_element_type=F32,
            )
            if masked:
                core = c if own_core else 1 - c
                parts = []
                for j in range(NY):
                    base = zone * 1024 + lax.rem(y - j + NY, NY) * 256 + core * TOK
                    visible = rows <= limit - base
                    parts.append(jnp.where(visible, scores[j * TOK : (j + 1) * TOK], -1e30))
                scores = jnp.concatenate(parts, axis=0)
            found.append(scores)
        if before is None:
            top = jnp.full((1, count), -1e30, F32)
        else:
            top = before[0:1, :]
        higher = top
        for scores in found:
            higher = jnp.maximum(higher, jnp.max(scores, axis=0, keepdims=True))
        total, acc = 0.0, 0.0
        if before is not None:
            fade = jnp.exp2((top - higher) * FACTOR)
            total, acc = before[8:9, :] * fade, before[16:, :] * fade
        for kv_ref, scores in zip(kv_refs, found):
            weights = jnp.exp2((scores - higher) * FACTOR)
            total = total + jnp.sum(weights, axis=0, keepdims=True)
            acc = acc + lax.dot_general(
                kv_ref[:, HD:],
                weights.astype(BF),
                (((0,), (0,)), ((), ())),
                preferred_element_type=F32,
            )
        state[0:8, :] = jnp.broadcast_to(higher, (8, count))
        state[8:16, :] = jnp.broadcast_to(total, (8, count))
        state[16:, :] = acc

    pl.when(full)(functools.partial(add, False))
    pl.when(jnp.logical_not(full | empty))(functools.partial(add, True))
    if before is not None:

        @pl.when(empty)
        def _():
            state[...] = before[...]

    if last_call:
        rest[0][...] = state[:, : count // 2]
        rest[1][...] = state[:, count // 2 :]


def merge_kernel(info, mine, other, out):
    higher = jnp.maximum(mine[0:1, :], other[0:1, :])
    fade = jnp.exp2((mine[0:1, :] - higher) * FACTOR)
    fade_x = jnp.exp2((other[0:1, :] - higher) * FACTOR)
    total = mine[8:9, :] * fade + other[8:9, :] * fade_x
    acc = mine[16:, :] * fade + other[16:, :] * fade_x
    out[...] = (acc / total).T.astype(BF)


def attend(info, queries, group, carry, last_call):
    arrays = [array for array, _, _ in group]
    cores = [own for _, _, own in group]
    operands = [info, queries] + arrays + ([] if carry is None else [carry])
    vmem = pl.BlockSpec(memory_space=pltpu.VMEM)
    count = queries.shape[0]
    keys = sum(a.shape[0] for a in arrays)
    if last_call:
        out = [jax.ShapeDtypeStruct((HD + 16, count // 2), F32)] * 2
    else:
        out = jax.ShapeDtypeStruct((HD + 16, count), F32)
    return pl.pallas_call(
        functools.partial(attend_kernel, cores, group[0][1], carry is None, last_call),
        out_shape=out,
        in_specs=[pl.BlockSpec(memory_space=pltpu.SMEM)] + [vmem] * (len(operands) - 1),
        out_specs=[vmem] * 2 if last_call else vmem,
        scratch_shapes=[pltpu.VMEM((HD + 16, count), F32)] if last_call else [],
        compiler_params=pltpu.CompilerParams(vmem_limit_bytes=40 * 1024 * 1024),
        cost_estimate=pl.CostEstimate(
            flops=4 * count * keys * HD,
            bytes_accessed=keys * 512,
            transcendentals=count * keys,
        ),
    )(*operands)


def shards(latents, conv_w, embed_w, text_emb, wqkv, seg_ids):
    z, y, c, x = (lax.axis_index(a) for a in ("z", "y", "c", "mp"))
    place = z * 8 + y * 2 + c
    other = swap(latents)
    chip = jnp.concatenate(
        [jnp.where(c == 0, latents, other), jnp.where(c == 0, other, latents)], axis=0
    )
    moves = [(i, i - 1) for i in range(2, 64, 2)] + [(i, i + 1) for i in range(1, 62, 2)]
    payload = jnp.where(c == 0, chip[:3], chip[1:])
    beside = lax.ppermute(payload, SEQ, moves)
    seg_ids, _ = lax.optimization_barrier((seg_ids, beside))
    positions = jnp.arange(seg_ids.shape[0], dtype=jnp.int32)
    start = jnp.min(jnp.where(seg_ids == 1, positions, seg_ids.shape[0])).astype(jnp.int32)
    info = jnp.stack([z, y, c, x, start]).astype(jnp.int32)
    below = swap(beside[:1])

    pieces = embed_pieces(embed_w, c)

    rows = jnp.where(
        c == 0,
        jnp.concatenate([beside[2:], chip, below], axis=0),
        jnp.concatenate([chip[1:], beside], axis=0),
    )
    conv = lax.conv_general_dilated(
        rows[None],
        conv_w,
        (1, 1),
        ((0, 0), (1, 1)),
        dimension_numbers=("NHWC", "HWIO", "NHWC"),
        preferred_element_type=F32,
    )[0]
    own = lax.dynamic_slice_in_dim(rows[1:5], x * 64, 64, 2)
    mixed = (own.astype(F32) + jax.nn.silu(conv)).astype(BF)
    pair = mixed.reshape(2, 2, 64, 2, 64).transpose(0, 2, 1, 3, 4).reshape(TOK, 256)
    unit = lax.shift_right_logical(start, 6)

    rows = spread_patches(pair, unit)
    own_w = call(
        block_kernel, jax.ShapeDtypeStruct((512, 128), BF), [tied(info, rows)] + pieces
    )
    own_x = swap(own_w)
    both = jnp.concatenate([own_w, own_x], axis=0)
    near_1, near_2 = along(both, 1), along(both, 2)
    rows, _ = lax.optimization_barrier((rows, both))
    placed = shift_patches(rows, unit)
    near_2, placed = lax.optimization_barrier((near_2, placed))
    patches = [placed] + [shift(placed, "mp", -t) for t in (1, 2, 3)]
    far_3, far_4 = along(near_2, 1), along(near_2[:512], 2)
    blocks, patches = lax.optimization_barrier(((near_1, near_2, far_3, far_4), patches))
    operands = [info, text_emb, *patches, own_w, own_x]
    for block in blocks:
        operands += [block, swap(block)]
    hidden = call(
        hidden_kernel, jax.ShapeDtypeStruct((TOK, 1024), BF), operands, 2 * TOK * 1024 * 1024
    )

    carry = project(info, hidden, wqkv)
    parts = [carry[0]] + [shift(carry[t], "y", t) for t in (1, 2, 3)]
    head = jnp.concatenate(parts, axis=0)
    other = swap(head)

    queries = jnp.concatenate([head[:, :HD], other[:, :HD]], axis=0)
    group = [(head[:, HD:], 0, True)]
    pair = (along(head[:, HD:], 1), along(other[:, HD:], 1))
    carry = None
    for step in range(1, 4):
        carry = attend(info, queries, group, carry, False)
        group, sent = [], []
        for block, own in zip(pair, (True, False)):
            block, carry = lax.optimization_barrier((block, carry))
            if own or step < 3:
                sent.append(along(block, 1))
            group.append((block, -step, own))
        pair = sent
    carry = attend(info, queries, group, carry, False)
    last, carry = lax.optimization_barrier((pair[0], carry))
    mine, other = attend(info, queries, [(last, -4, True)], carry, True)
    carry = call(
        merge_kernel, jax.ShapeDtypeStruct((NY * TOK, HD), BF), [info, mine, swap(other)]
    )
    back = [carry[:TOK]]
    for t in range(1, NY):
        back.append(shift(carry[t * TOK : (t + 1) * TOK], "y", -t))
    return ordered(back, y).transpose(1, 0, 2).reshape(TOK, 4 * HD)


def solution(mesh):
    inner = Mesh(mesh.devices.reshape(NZ, NY, NC, NX), ("z", "y", "c", "mp"))
    return jax.shard_map(
        shards,
        mesh=inner,
        in_specs=(
            P(SEQ, None, None),
            P(None, None, None, "mp"),
            P(None, "mp", SEQ),
            P(SEQ, "mp"),
            P(None, None, "mp"),
            P(),
        ),
        out_specs=P(SEQ, "mp"),
        check_vma=False,
    )
```

```python
import functools
import itertools
import math

import jax
import jax.numpy as jnp
from jax import lax
from jax.experimental import pallas as pl
from jax.experimental.pallas import tpu as pltpu
from jax.sharding import Mesh
from jax.sharding import PartitionSpec as P

NZ, NY, NC, NX = 8, 4, 2, 4
HD = 128
TOK = 128
IMG = 4096
SEQ = ("z", "y", "c")
SIZES = {"z": NZ, "y": NY, "c": NC, "mp": NX}
BF = jnp.bfloat16
F32 = jnp.float32


def shift(value, axis, step):
    count = SIZES[axis]
    return lax.ppermute(value, axis, [(i, (i + step) % count) for i in range(count)])


def ordered(pieces, first):
    count = len(pieces)
    twice = jnp.stack(pieces + pieces)
    return lax.dynamic_slice_in_dim(twice, (count - first) & (count - 1), count, 0)


def tied(info, other):
    return lax.optimization_barrier((info, other))[0]


def along(value, step):
    perm = []
    for z in range(NZ):
        perm.append((z * 2, (z + step) % NZ * 2))
        perm.append((z * 2 + 1, (z - step) % NZ * 2 + 1))
    return lax.ppermute(value, ("z", "c"), perm)


def swap(value):
    return shift(value, "c", 1)


def call(kernel, out_shape, operands, flops=0, limit=40):
    vmem = pl.BlockSpec(memory_space=pltpu.VMEM)
    size = sum(a.size * a.dtype.itemsize for a in operands)
    return pl.pallas_call(
        kernel,
        out_shape=out_shape,
        in_specs=[pl.BlockSpec(memory_space=pltpu.SMEM)] + [vmem] * (len(operands) - 1),
        out_specs=jax.tree.map(lambda _: vmem, out_shape),
        compiler_params=pltpu.CompilerParams(vmem_limit_bytes=limit * 1024 * 1024),
        cost_estimate=pl.CostEstimate(flops=flops, bytes_accessed=size, transcendentals=0),
    )(*operands)


def block_kernel(info, p0, p1, out):
    odd = lax.rem(info[1], 2)
    first = jnp.where(odd == 0, p0[...], p1[...])
    second = jnp.where(odd == 0, p1[...], p0[...])
    for a, value in enumerate((first, second)):
        for half in range(2):
            row = a * 256 + half * 128
            low = half * 64
            out[row : row + 128, :] = jnp.concatenate(
                [value[:, low : low + 64], value[:, 128 + low : 192 + low]], axis=1
            )


def flat(y, c, x):
    return (y * NC + c) * NX + x


def embed_pieces(embed_w, c):
    cells = embed_w.reshape(2, 128, 64)
    packed = jnp.concatenate([cells[0], cells[1]], axis=1)
    other = swap(packed)
    both = jnp.concatenate(
        [jnp.where(c == 0, packed, other), jnp.where(c == 0, other, packed)], axis=1
    )
    pieces = []
    for k in range(2):
        perm = []
        for y, c, x in itertools.product(range(NY), range(NC), range(NX)):
            to = ((2 * c + k + x % 2) % NY, x // 2, y)
            perm.append((flat(y, c, x), flat(*to)))
        pieces.append(lax.ppermute(both, ("y", "c", "mp"), perm))
    return pieces


OFFSETS = (0, -1, 1, -2, 2, -3, 3, 4)


def hidden_kernel(info, text, p0, p1, p2, p3, own, own_x, d1, x1, d2, x2, d3, x3, d4, x4, out):
    z, y, c, x, start = info[0], info[1], info[2], info[3], info[4]
    pieces = [p0[...], p1[...], p2[...], p3[...]]
    base = (z * 8 + y * 2 + c) * TOK
    late = base - start == -64
    pos = base + lax.broadcasted_iota(jnp.int32, (TOK, 128), 0)
    is_text = (pos < start) | (pos >= start + IMG)

    def features(m):
        t = lax.rem(m - x + NX, NX)
        value = pieces[0]
        for i in range(1, NX):
            value = jnp.where(t == i, pieces[i], value)
        return jnp.where(late, jnp.concatenate([value[64:], value[:64]], axis=0), value)

    mine = jnp.concatenate([features(2 * c), features(2 * c + 1)], axis=1)
    other = jnp.concatenate([features(2 - 2 * c), features(3 - 2 * c)], axis=1)
    pairs = [
        (own[...], own_x[...]),
        (d1[:512, :], d1[512:, :]),
        (x1[512:, :], x1[:512, :]),
        (d2[:512, :], d2[512:, :]),
        (x2[512:, :], x2[:512, :]),
        (d3[:512, :], d3[512:, :]),
        (x3[512:, :], x3[:512, :]),
        (d4[...], x4[...]),
    ]
    for at, (first, second) in enumerate(pairs):
        part = jnp.dot(mine, first, preferred_element_type=F32)
        part = part + jnp.dot(other, second, preferred_element_type=F32)
        place = lax.rem(z + OFFSETS[at] * (1 - 2 * c) + NZ, NZ)
        cols = pl.ds(pl.multiple_of(place * 128, 128), 128)
        out[:, cols] = jnp.where(is_text, text[:, cols], part.astype(BF))


ARRIVALS = (0, 1, 3, 2)


def qkv_add(t, info, hidden, weights, before, out):
    z, y, c, x, start = info[0], info[1], info[2], info[3], info[4]
    base = (z * 8 + y * 2 + c) * TOK
    text_0 = (base < start) | (base >= start + IMG)
    text_1 = (base + 64 < start) | (base + 64 >= start + IMG)
    group = lax.rem(x + t, NX)

    def text(j):
        return jnp.dot(hidden[...], weights[t][j], preferred_element_type=F32)

    def image(j):
        total = 0.0
        for r, weight in enumerate(weights):
            quarter = lax.rem(x + r, NX)
            for h in range(2):
                col = pl.multiple_of((2 * quarter + h) * 128, 128)
                row = pl.multiple_of(h * 512 + group * 128, 128)
                total = total + jnp.dot(
                    hidden[:, pl.ds(col, 128)],
                    weight[j, pl.ds(row, 128), :],
                    preferred_element_type=F32,
                )
        return total

    def both(j):
        first = lax.broadcasted_iota(jnp.int32, (TOK, 512), 0) < 64
        return jnp.where(first == text_0, text(j), image(j))

    def add(product):
        for j in range(3):
            cols = slice(j * 512, (j + 1) * 512)
            value = product(j)
            out[:, cols] = value if before is None else before[:, cols] + value

    pl.when(text_0 & text_1)(lambda: add(text))
    pl.when(jnp.logical_not(text_0 | text_1))(lambda: add(image))
    pl.when(text_0 != text_1)(lambda: add(both))


def qkv_first(info, hidden, wqkv, total, w0, w1, w2, w3, sems):
    x = info[3]
    weights = (w0, w1, w2, w3)
    copies = []
    for t in range(NX):
        for j in range(3):
            for h in range(4):
                row = lax.rem(x + t, NX) * 1024 + h * 256
                copies.append(
                    pltpu.make_async_copy(
                        wqkv.at[j, pl.ds(pl.multiple_of(row, 256), 256), :],
                        weights[t].at[j, pl.ds(h * 256, 256), :],
                        sems.at[t * 12 + j * 4 + h],
                    )
                )
    for copy in copies:
        copy.start()
    for copy in copies:
        copy.wait()
    qkv_add(0, info, hidden, weights, None, total)


def qkv_next(t, info, hidden, w0, w1, w2, w3, carry, out):
    qkv_add(t, info, hidden, (w0, w1, w2, w3), carry, out)


def qkv_last(t, info, hidden, w0, w1, w2, w3, carry, o0, o1, o2, o3, total):
    qkv_add(t, info, hidden, (w0, w1, w2, w3), carry, total)
    for k, out in enumerate((o0, o1, o2, o3)):
        head = lax.rem(info[1] + k, NY)
        for j in range(3):
            value = total[:, pl.ds(pl.multiple_of(j * 512 + head * 128, 128), 128)]
            out[:, j * 128 : (j + 1) * 128] = value.astype(BF)


def project(info, hidden, wqkv):
    vmem = pl.BlockSpec(memory_space=pltpu.VMEM)
    smem = pl.BlockSpec(memory_space=pltpu.SMEM)
    weight = jax.ShapeDtypeStruct((3, 1024, 512), BF)
    total = jax.ShapeDtypeStruct((TOK, 1536), F32)
    flops = 2 * TOK * 1024 * 1536
    carry, *weights = pl.pallas_call(
        qkv_first,
        out_shape=[total] + [weight] * NX,
        in_specs=[smem, vmem, pl.BlockSpec(memory_space=pl.ANY)],
        out_specs=[vmem] * (1 + NX),
        scratch_shapes=[pltpu.SemaphoreType.DMA((48,))],
        compiler_params=pltpu.CompilerParams(vmem_limit_bytes=32 * 1024 * 1024),
        cost_estimate=pl.CostEstimate(
            flops=flops, bytes_accessed=24 << 20, transcendentals=0
        ),
    )(info, hidden, jnp.transpose(wqkv, (1, 0, 2)))
    after, before = shift(hidden, "mp", -1), shift(hidden, "mp", 1)
    after, before, carry = lax.optimization_barrier((after, before, carry))
    moves = []
    for x in range(NX):
        moves.append((x, (x - 1) % NX))
        moves.append((NX + x, NX + (x + 1) % NX))
    relayed = lax.ppermute(jnp.where(lax.axis_index("c") == 0, after, before), ("c", "mp"), moves)
    arrived = {1: after, 3: before, 2: relayed}
    for t in ARRIVALS[1:]:
        last = t == 2
        head = jax.ShapeDtypeStruct((TOK, 3 * HD), BF)
        carry = pl.pallas_call(
            functools.partial(qkv_last if last else qkv_next, t),
            out_shape=[head] * NY if last else total,
            in_specs=[smem] + [vmem] * (2 + NX),
            out_specs=[vmem] * NY if last else vmem,
            scratch_shapes=[pltpu.VMEM((TOK, 1536), F32)] if last else [],
            compiler_params=pltpu.CompilerParams(vmem_limit_bytes=24 * 1024 * 1024),
            cost_estimate=pl.CostEstimate(
                flops=flops, bytes_accessed=5 << 20, transcendentals=0
            ),
        )(info, arrived[t], *weights, carry)
    return carry


def spread_patches(pair, unit):
    def spread(low_shift, parity):
        moves = [(s, 16 + low_shift + (s + parity) // 2) for s in range(parity, 64, 2)]
        if parity:
            moves.append((0, 16 + low_shift))
        return lambda rows: lax.ppermute(rows, SEQ, moves)

    return lax.switch(unit & 7, [spread(i // 2, i % 2) for i in range(8)], pair)


def shift_patches(rows, unit):
    def moved(high):
        if high == 0:
            return lambda rows: rows
        moves = [(s, s + 4 * high) for s in range(64) if 0 <= s + 4 * high < 64]
        return lambda rows: lax.ppermute(rows, SEQ, moves)

    return lax.switch(lax.shift_right_logical(unit, 3), [moved(i - 4) for i in range(9)], rows)


FACTOR = HD**-0.5 * math.log2(math.e)


def attend_kernel(cores, offset, first_call, last_call, info, queries, *refs):
    z, y, c, start = info[0], info[1], info[2], info[4]
    kv_refs = refs[: len(cores)]
    rest = refs[len(cores) :]
    count = queries.shape[0]
    state = rest[-1]
    if first_call:
        before = None
    else:
        before, rest = rest[0], rest[1:]
    zone = lax.rem(z + offset * (1 - 2 * c) + NZ, NZ)
    no_image = (z * 1024 + 1024 <= start) | (z * 1024 >= start + IMG)
    all_image = (z * 1024 >= start) & (z * 1024 + 1024 <= start + IMG)
    full = (zone < z) | (all_image & (zone * 1024 + 1024 <= start + IMG))
    empty = (zone > z) & (no_image | (zone * 1024 >= start + IMG))

    def limits():
        lanes = lax.broadcasted_iota(jnp.int32, (1, TOK), 1)
        found = []
        for core in (c, 1 - c):
            for j in range(NY):
                pos = z * 1024 + lax.rem(y - j + NY, NY) * 256 + core * TOK + lanes
                inside = (pos >= start) & (pos < start + IMG)
                found.append(jnp.where(inside, start + (IMG - 1), pos))
        return jnp.concatenate(found, axis=1)

    def add(masked):
        if masked:
            limit = limits()
            rows = lax.broadcasted_iota(jnp.int32, (TOK, count), 0)
        found = []
        for kv_ref, own_core in zip(kv_refs, cores):
            scores = lax.dot_general(
                kv_ref[:, :HD],
                queries[...],
                (((1,), (1,)), ((), ())),
                preferred_element_type=F32,
            )
            if masked:
                core = c if own_core else 1 - c
                parts = []
                for j in range(NY):
                    base = zone * 1024 + lax.rem(y - j + NY, NY) * 256 + core * TOK
                    visible = rows <= limit - base
                    parts.append(jnp.where(visible, scores[j * TOK : (j + 1) * TOK], -1e30))
                scores = jnp.concatenate(parts, axis=0)
            found.append(scores)
        if before is None:
            top = jnp.full((1, count), -1e30, F32)
        else:
            top = before[0:1, :]
        higher = top
        for scores in found:
            higher = jnp.maximum(higher, jnp.max(scores, axis=0, keepdims=True))
        total, acc = 0.0, 0.0
        if before is not None:
            fade = jnp.exp2((top - higher) * FACTOR)
            total, acc = before[8:9, :] * fade, before[16:, :] * fade
        for kv_ref, scores in zip(kv_refs, found):
            weights = jnp.exp2((scores - higher) * FACTOR)
            total = total + jnp.sum(weights, axis=0, keepdims=True)
            acc = acc + lax.dot_general(
                kv_ref[:, HD:],
                weights.astype(BF),
                (((0,), (0,)), ((), ())),
                preferred_element_type=F32,
            )
        state[0:8, :] = jnp.broadcast_to(higher, (8, count))
        state[8:16, :] = jnp.broadcast_to(total, (8, count))
        state[16:, :] = acc

    pl.when(full)(functools.partial(add, False))
    pl.when(jnp.logical_not(full | empty))(functools.partial(add, True))
    if before is not None:

        @pl.when(empty)
        def _():
            state[...] = before[...]

    if last_call:
        rest[0][...] = state[:, : count // 2]
        rest[1][...] = state[:, count // 2 :]


def merge_kernel(info, mine, other, out):
    higher = jnp.maximum(mine[0:1, :], other[0:1, :])
    fade = jnp.exp2((mine[0:1, :] - higher) * FACTOR)
    fade_x = jnp.exp2((other[0:1, :] - higher) * FACTOR)
    total = mine[8:9, :] * fade + other[8:9, :] * fade_x
    acc = mine[16:, :] * fade + other[16:, :] * fade_x
    out[...] = (acc / total).T.astype(BF)


def attend(info, queries, group, carry, last_call):
    arrays = [array for array, _, _ in group]
    cores = [own for _, _, own in group]
    operands = [info, queries] + arrays + ([] if carry is None else [carry])
    vmem = pl.BlockSpec(memory_space=pltpu.VMEM)
    count = queries.shape[0]
    keys = sum(a.shape[0] for a in arrays)
    if last_call:
        out = [jax.ShapeDtypeStruct((HD + 16, count // 2), F32)] * 2
    else:
        out = jax.ShapeDtypeStruct((HD + 16, count), F32)
    return pl.pallas_call(
        functools.partial(attend_kernel, cores, group[0][1], carry is None, last_call),
        out_shape=out,
        in_specs=[pl.BlockSpec(memory_space=pltpu.SMEM)] + [vmem] * (len(operands) - 1),
        out_specs=[vmem] * 2 if last_call else vmem,
        scratch_shapes=[pltpu.VMEM((HD + 16, count), F32)] if last_call else [],
        compiler_params=pltpu.CompilerParams(vmem_limit_bytes=40 * 1024 * 1024),
        cost_estimate=pl.CostEstimate(
            flops=4 * count * keys * HD,
            bytes_accessed=keys * 512,
            transcendentals=count * keys,
        ),
    )(*operands)


def shards(latents, conv_w, embed_w, text_emb, wqkv, seg_ids):
    z, y, c, x = (lax.axis_index(a) for a in ("z", "y", "c", "mp"))
    place = z * 8 + y * 2 + c
    other = swap(latents)
    chip = jnp.concatenate(
        [jnp.where(c == 0, latents, other), jnp.where(c == 0, other, latents)], axis=0
    )
    moves = [(i, i - 1) for i in range(2, 64, 2)] + [(i, i + 1) for i in range(1, 62, 2)]
    payload = jnp.where(c == 0, chip[:3], chip[1:])
    beside = lax.ppermute(payload, SEQ, moves)
    seg_ids, _ = lax.optimization_barrier((seg_ids, beside))
    positions = jnp.arange(seg_ids.shape[0], dtype=jnp.int32)
    start = jnp.min(jnp.where(seg_ids == 1, positions, seg_ids.shape[0])).astype(jnp.int32)
    info = jnp.stack([z, y, c, x, start]).astype(jnp.int32)
    below = swap(beside[:1])

    pieces = embed_pieces(embed_w, c)

    rows = jnp.where(
        c == 0,
        jnp.concatenate([beside[2:], chip, below], axis=0),
        jnp.concatenate([chip[1:], beside], axis=0),
    )
    conv = lax.conv_general_dilated(
        rows[None],
        conv_w,
        (1, 1),
        ((0, 0), (1, 1)),
        dimension_numbers=("NHWC", "HWIO", "NHWC"),
        preferred_element_type=F32,
    )[0]
    own = lax.dynamic_slice_in_dim(rows[1:5], x * 64, 64, 2)
    mixed = (own.astype(F32) + jax.nn.silu(conv)).astype(BF)
    pair = mixed.reshape(2, 2, 64, 2, 64).transpose(0, 2, 1, 3, 4).reshape(TOK, 256)
    unit = lax.shift_right_logical(start, 6)

    rows = spread_patches(pair, unit)
    own_w = call(
        block_kernel, jax.ShapeDtypeStruct((512, 128), BF), [tied(info, rows)] + pieces
    )
    own_x = swap(own_w)
    both = jnp.concatenate([own_w, own_x], axis=0)
    near_1, near_2 = along(both, 1), along(both, 2)
    rows, _ = lax.optimization_barrier((rows, both))
    placed = shift_patches(rows, unit)
    near_2, placed = lax.optimization_barrier((near_2, placed))
    patches = [placed] + [shift(placed, "mp", -t) for t in (1, 2, 3)]
    far_3, far_4 = along(near_2, 1), along(near_2[:512], 2)
    blocks, patches = lax.optimization_barrier(((near_1, near_2, far_3, far_4), patches))
    operands = [info, text_emb, *patches, own_w, own_x]
    for block in blocks:
        operands += [block, swap(block)]
    hidden = call(
        hidden_kernel, jax.ShapeDtypeStruct((TOK, 1024), BF), operands, 2 * TOK * 1024 * 1024
    )

    carry = project(info, hidden, wqkv)
    parts = [carry[0]] + [shift(carry[t], "y", t) for t in (1, 2, 3)]
    head = jnp.concatenate(parts, axis=0)
    other = swap(head)

    queries = jnp.concatenate([head[:, :HD], other[:, :HD]], axis=0)
    group = [(head[:, HD:], 0, True)]
    pair = (along(head[:, HD:], 1), along(other[:, HD:], 1))
    carry = None
    for step in range(1, 4):
        carry = attend(info, queries, group, carry, False)
        group, sent = [], []
        for block, own in zip(pair, (True, False)):
            block, carry = lax.optimization_barrier((block, carry))
            if own or step < 3:
                sent.append(along(block, 1))
            group.append((block, -step, own))
        pair = sent
    carry = attend(info, queries, group, carry, False)
    last, carry = lax.optimization_barrier((pair[0], carry))
    mine, other = attend(info, queries, [(last, -4, True)], carry, True)
    carry = call(
        merge_kernel, jax.ShapeDtypeStruct((NY * TOK, HD), BF), [info, mine, swap(other)]
    )
    back = [carry[:TOK]]
    for t in range(1, NY):
        back.append(shift(carry[t * TOK : (t + 1) * TOK], "y", -t))
    return ordered(back, y).transpose(1, 0, 2).reshape(TOK, 4 * HD)


def solution(mesh):
    inner = Mesh(mesh.devices.reshape(NZ, NY, NC, NX), ("z", "y", "c", "mp"))
    return jax.shard_map(
        shards,
        mesh=inner,
        in_specs=(
            P(SEQ, None, None),
            P(None, None, None, "mp"),
            P(None, "mp", SEQ),
            P(SEQ, "mp"),
            P(None, None, "mp"),
            P(),
        ),
        out_specs=P(SEQ, "mp"),
        check_vma=False,
    )
```

```python
import functools
import itertools
import math

import jax
import jax.numpy as jnp
from jax import lax
from jax.experimental import pallas as pl
from jax.experimental.pallas import tpu as pltpu
from jax.sharding import Mesh
from jax.sharding import PartitionSpec as P

NZ, NY, NC, NX = 8, 4, 2, 4
HD = 128
TOK = 128
IMG = 4096
SEQ = ("z", "y", "c")
SIZES = {"z": NZ, "y": NY, "c": NC, "mp": NX}
BF = jnp.bfloat16
F32 = jnp.float32


def shift(value, axis, step):
    count = SIZES[axis]
    return lax.ppermute(value, axis, [(i, (i + step) % count) for i in range(count)])


def ordered(pieces, first):
    count = len(pieces)
    twice = jnp.stack(pieces + pieces)
    return lax.dynamic_slice_in_dim(twice, (count - first) & (count - 1), count, 0)


def tied(info, other):
    return lax.optimization_barrier((info, other))[0]


def along(value, step):
    perm = []
    for z in range(NZ):
        perm.append((z * 2, (z + step) % NZ * 2))
        perm.append((z * 2 + 1, (z - step) % NZ * 2 + 1))
    return lax.ppermute(value, ("z", "c"), perm)


def swap(value):
    return shift(value, "c", 1)


def call(kernel, out_shape, operands, flops=0, limit=40):
    vmem = pl.BlockSpec(memory_space=pltpu.VMEM)
    size = sum(a.size * a.dtype.itemsize for a in operands)
    return pl.pallas_call(
        kernel,
        out_shape=out_shape,
        in_specs=[pl.BlockSpec(memory_space=pltpu.SMEM)] + [vmem] * (len(operands) - 1),
        out_specs=jax.tree.map(lambda _: vmem, out_shape),
        compiler_params=pltpu.CompilerParams(vmem_limit_bytes=limit * 1024 * 1024),
        cost_estimate=pl.CostEstimate(flops=flops, bytes_accessed=size, transcendentals=0),
    )(*operands)


def locate_kernel(segments, out):
    shape = segments.shape
    pos = lax.broadcasted_iota(jnp.int32, shape, 0) * 128 + lax.broadcasted_iota(jnp.int32, shape, 1)
    first = jnp.where(segments[...] == 1, pos, 64 * 128).astype(F32)
    start = jnp.min(first).astype(jnp.int32)
    for i, axis in enumerate(("z", "y", "c", "mp")):
        out[i] = lax.axis_index(axis)
    out[4] = start
    out[5] = lax.shift_right_logical(start, 6)
    out[6] = 0
    out[7] = 0


def block_kernel(info, p0, p1, out):
    odd = lax.rem(info[1], 2)
    first = jnp.where(odd == 0, p0[...], p1[...])
    second = jnp.where(odd == 0, p1[...], p0[...])
    for a, value in enumerate((first, second)):
        for half in range(2):
            row = a * 256 + half * 128
            low = half * 64
            out[row : row + 128, :] = jnp.concatenate(
                [value[:, low : low + 64], value[:, 128 + low : 192 + low]], axis=1
            )


def flat(y, c, x):
    return (y * NC + c) * NX + x


def embed_pieces(embed_w, c):
    cells = embed_w.reshape(2, 128, 64)
    packed = jnp.concatenate([cells[0], cells[1]], axis=1)
    other = swap(packed)
    both = jnp.concatenate(
        [jnp.where(c == 0, packed, other), jnp.where(c == 0, other, packed)], axis=1
    )
    pieces = []
    for k in range(2):
        perm = []
        for y, c, x in itertools.product(range(NY), range(NC), range(NX)):
            to = ((2 * c + k + x % 2) % NY, x // 2, y)
            perm.append((flat(y, c, x), flat(*to)))
        pieces.append(lax.ppermute(both, ("y", "c", "mp"), perm))
    return pieces


OFFSETS = (0, -1, 1, -2, 2, -3, 3, 4)


def hidden_kernel(info, text, p0, p1, p2, p3, own, own_x, d1, x1, d2, x2, d3, x3, d4, x4, out):
    z, y, c, x, start = info[0], info[1], info[2], info[3], info[4]
    pieces = [p0[...], p1[...], p2[...], p3[...]]
    base = (z * 8 + y * 2 + c) * TOK
    late = base - start == -64
    pos = base + lax.broadcasted_iota(jnp.int32, (TOK, 128), 0)
    is_text = (pos < start) | (pos >= start + IMG)

    def features(m):
        t = lax.rem(m - x + NX, NX)
        value = pieces[0]
        for i in range(1, NX):
            value = jnp.where(t == i, pieces[i], value)
        return jnp.where(late, jnp.concatenate([value[64:], value[:64]], axis=0), value)

    mine = jnp.concatenate([features(2 * c), features(2 * c + 1)], axis=1)
    other = jnp.concatenate([features(2 - 2 * c), features(3 - 2 * c)], axis=1)
    pairs = [
        (own[...], own_x[...]),
        (d1[:512, :], d1[512:, :]),
        (x1[512:, :], x1[:512, :]),
        (d2[:512, :], d2[512:, :]),
        (x2[512:, :], x2[:512, :]),
        (d3[:512, :], d3[512:, :]),
        (x3[512:, :], x3[:512, :]),
        (d4[...], x4[...]),
    ]
    for at, (first, second) in enumerate(pairs):
        part = jnp.dot(mine, first, preferred_element_type=F32)
        part = part + jnp.dot(other, second, preferred_element_type=F32)
        place = lax.rem(z + OFFSETS[at] * (1 - 2 * c) + NZ, NZ)
        cols = pl.ds(pl.multiple_of(place * 128, 128), 128)
        out[:, cols] = jnp.where(is_text, text[:, cols], part.astype(BF))


ARRIVALS = (0, 1, 3, 2)


def qkv_add(t, info, hidden, weights, before, out):
    z, y, c, x, start = info[0], info[1], info[2], info[3], info[4]
    base = (z * 8 + y * 2 + c) * TOK
    text_0 = (base < start) | (base >= start + IMG)
    text_1 = (base + 64 < start) | (base + 64 >= start + IMG)
    group = lax.rem(x + t, NX)

    def text(j):
        return jnp.dot(hidden[...], weights[t][j], preferred_element_type=F32)

    def image(j):
        total = 0.0
        for r, weight in enumerate(weights):
            quarter = lax.rem(x + r, NX)
            for h in range(2):
                col = pl.multiple_of((2 * quarter + h) * 128, 128)
                row = pl.multiple_of(h * 512 + group * 128, 128)
                total = total + jnp.dot(
                    hidden[:, pl.ds(col, 128)],
                    weight[j, pl.ds(row, 128), :],
                    preferred_element_type=F32,
                )
        return total

    def both(j):
        first = lax.broadcasted_iota(jnp.int32, (TOK, 512), 0) < 64
        return jnp.where(first == text_0, text(j), image(j))

    def add(product):
        for j in range(3):
            cols = slice(j * 512, (j + 1) * 512)
            value = product(j)
            out[:, cols] = value if before is None else before[:, cols] + value

    pl.when(text_0 & text_1)(lambda: add(text))
    pl.when(jnp.logical_not(text_0 | text_1))(lambda: add(image))
    pl.when(text_0 != text_1)(lambda: add(both))


def qkv_first(info, hidden, wqkv, total, w0, w1, w2, w3, sems):
    x = info[3]
    weights = (w0, w1, w2, w3)
    copies = []
    for t in range(NX):
        for j in range(3):
            for h in range(4):
                row = lax.rem(x + t, NX) * 1024 + h * 256
                copies.append(
                    pltpu.make_async_copy(
                        wqkv.at[j, pl.ds(pl.multiple_of(row, 256), 256), :],
                        weights[t].at[j, pl.ds(h * 256, 256), :],
                        sems.at[t * 12 + j * 4 + h],
                    )
                )
    for copy in copies:
        copy.start()
    for copy in copies:
        copy.wait()
    qkv_add(0, info, hidden, weights, None, total)


def qkv_next(t, info, hidden, w0, w1, w2, w3, carry, out):
    qkv_add(t, info, hidden, (w0, w1, w2, w3), carry, out)


def qkv_last(t, info, hidden, w0, w1, w2, w3, carry, o0, o1, o2, o3, total):
    qkv_add(t, info, hidden, (w0, w1, w2, w3), carry, total)
    for k, out in enumerate((o0, o1, o2, o3)):
        head = lax.rem(info[1] + k, NY)
        for j in range(3):
            value = total[:, pl.ds(pl.multiple_of(j * 512 + head * 128, 128), 128)]
            out[:, j * 128 : (j + 1) * 128] = value.astype(BF)


def project(info, hidden, wqkv):
    vmem = pl.BlockSpec(memory_space=pltpu.VMEM)
    smem = pl.BlockSpec(memory_space=pltpu.SMEM)
    weight = jax.ShapeDtypeStruct((3, 1024, 512), BF)
    total = jax.ShapeDtypeStruct((TOK, 1536), F32)
    flops = 2 * TOK * 1024 * 1536
    carry, *weights = pl.pallas_call(
        qkv_first,
        out_shape=[total] + [weight] * NX,
        in_specs=[smem, vmem, pl.BlockSpec(memory_space=pl.ANY)],
        out_specs=[vmem] * (1 + NX),
        scratch_shapes=[pltpu.SemaphoreType.DMA((48,))],
        compiler_params=pltpu.CompilerParams(vmem_limit_bytes=32 * 1024 * 1024),
        cost_estimate=pl.CostEstimate(
            flops=flops, bytes_accessed=24 << 20, transcendentals=0
        ),
    )(info, hidden, jnp.transpose(wqkv, (1, 0, 2)))
    after, before = shift(hidden, "mp", -1), shift(hidden, "mp", 1)
    after, before, carry = lax.optimization_barrier((after, before, carry))
    moves = []
    for x in range(NX):
        moves.append((x, (x - 1) % NX))
        moves.append((NX + x, NX + (x + 1) % NX))
    relayed = lax.ppermute(jnp.where(lax.axis_index("c") == 0, after, before), ("c", "mp"), moves)
    arrived = {1: after, 3: before, 2: relayed}
    for t in ARRIVALS[1:]:
        last = t == 2
        head = jax.ShapeDtypeStruct((TOK, 3 * HD), BF)
        carry = pl.pallas_call(
            functools.partial(qkv_last if last else qkv_next, t),
            out_shape=[head] * NY if last else total,
            in_specs=[smem] + [vmem] * (2 + NX),
            out_specs=[vmem] * NY if last else vmem,
            scratch_shapes=[pltpu.VMEM((TOK, 1536), F32)] if last else [],
            compiler_params=pltpu.CompilerParams(vmem_limit_bytes=24 * 1024 * 1024),
            cost_estimate=pl.CostEstimate(
                flops=flops, bytes_accessed=5 << 20, transcendentals=0
            ),
        )(info, arrived[t], *weights, carry)
    return carry


def spread_patches(pair, unit):
    def spread(low_shift, parity):
        moves = [(s, 16 + low_shift + (s + parity) // 2) for s in range(parity, 64, 2)]
        if parity:
            moves.append((0, 16 + low_shift))
        return lambda rows: lax.ppermute(rows, SEQ, moves)

    return lax.switch(unit & 7, [spread(i // 2, i % 2) for i in range(8)], pair)


def shift_patches(rows, unit):
    def moved(high):
        if high == 0:
            return lambda rows: rows
        moves = [(s, s + 4 * high) for s in range(64) if 0 <= s + 4 * high < 64]
        return lambda rows: lax.ppermute(rows, SEQ, moves)

    return lax.switch(lax.shift_right_logical(unit, 3), [moved(i - 4) for i in range(9)], rows)


FACTOR = HD**-0.5 * math.log2(math.e)


def attend_kernel(cores, offset, first_call, last_call, info, queries, *refs):
    z, y, c, start = info[0], info[1], info[2], info[4]
    kv_refs = refs[: len(cores)]
    rest = refs[len(cores) :]
    count = queries.shape[0]
    state = rest[-1]
    if first_call:
        before = None
    else:
        before, rest = rest[0], rest[1:]
    zone = lax.rem(z + offset * (1 - 2 * c) + NZ, NZ)
    no_image = (z * 1024 + 1024 <= start) | (z * 1024 >= start + IMG)
    all_image = (z * 1024 >= start) & (z * 1024 + 1024 <= start + IMG)
    full = (zone < z) | (all_image & (zone * 1024 + 1024 <= start + IMG))
    empty = (zone > z) & (no_image | (zone * 1024 >= start + IMG))

    def limits():
        lanes = lax.broadcasted_iota(jnp.int32, (1, TOK), 1)
        found = []
        for core in (c, 1 - c):
            for j in range(NY):
                pos = z * 1024 + lax.rem(y - j + NY, NY) * 256 + core * TOK + lanes
                inside = (pos >= start) & (pos < start + IMG)
                found.append(jnp.where(inside, start + (IMG - 1), pos))
        return jnp.concatenate(found, axis=1)

    def add(masked):
        if masked:
            limit = limits()
            rows = lax.broadcasted_iota(jnp.int32, (TOK, count), 0)
        found = []
        for kv_ref, own_core in zip(kv_refs, cores):
            scores = lax.dot_general(
                kv_ref[:, :HD],
                queries[...],
                (((1,), (1,)), ((), ())),
                preferred_element_type=F32,
            )
            if masked:
                core = c if own_core else 1 - c
                parts = []
                for j in range(NY):
                    base = zone * 1024 + lax.rem(y - j + NY, NY) * 256 + core * TOK
                    visible = rows <= limit - base
                    parts.append(jnp.where(visible, scores[j * TOK : (j + 1) * TOK], -1e30))
                scores = jnp.concatenate(parts, axis=0)
            found.append(scores)
        if before is None:
            top = jnp.full((1, count), -1e30, F32)
        else:
            top = before[0:1, :]
        higher = top
        for scores in found:
            higher = jnp.maximum(higher, jnp.max(scores, axis=0, keepdims=True))
        total, acc = 0.0, 0.0
        if before is not None:
            fade = jnp.exp2((top - higher) * FACTOR)
            total, acc = before[8:9, :] * fade, before[16:, :] * fade
        for kv_ref, scores in zip(kv_refs, found):
            weights = jnp.exp2((scores - higher) * FACTOR)
            total = total + jnp.sum(weights, axis=0, keepdims=True)
            acc = acc + lax.dot_general(
                kv_ref[:, HD:],
                weights.astype(BF),
                (((0,), (0,)), ((), ())),
                preferred_element_type=F32,
            )
        state[0:8, :] = jnp.broadcast_to(higher, (8, count))
        state[8:16, :] = jnp.broadcast_to(total, (8, count))
        state[16:, :] = acc

    pl.when(full)(functools.partial(add, False))
    pl.when(jnp.logical_not(full | empty))(functools.partial(add, True))
    if before is not None:

        @pl.when(empty)
        def _():
            state[...] = before[...]

    if last_call:
        rest[0][...] = state[:, : count // 2]
        rest[1][...] = state[:, count // 2 :]


def merge_kernel(info, mine, other, out):
    higher = jnp.maximum(mine[0:1, :], other[0:1, :])
    fade = jnp.exp2((mine[0:1, :] - higher) * FACTOR)
    fade_x = jnp.exp2((other[0:1, :] - higher) * FACTOR)
    total = mine[8:9, :] * fade + other[8:9, :] * fade_x
    acc = mine[16:, :] * fade + other[16:, :] * fade_x
    out[...] = (acc / total).T.astype(BF)


def attend(info, queries, group, carry, last_call):
    arrays = [array for array, _, _ in group]
    cores = [own for _, _, own in group]
    operands = [info, queries] + arrays + ([] if carry is None else [carry])
    vmem = pl.BlockSpec(memory_space=pltpu.VMEM)
    count = queries.shape[0]
    keys = sum(a.shape[0] for a in arrays)
    if last_call:
        out = [jax.ShapeDtypeStruct((HD + 16, count // 2), F32)] * 2
    else:
        out = jax.ShapeDtypeStruct((HD + 16, count), F32)
    return pl.pallas_call(
        functools.partial(attend_kernel, cores, group[0][1], carry is None, last_call),
        out_shape=out,
        in_specs=[pl.BlockSpec(memory_space=pltpu.SMEM)] + [vmem] * (len(operands) - 1),
        out_specs=[vmem] * 2 if last_call else vmem,
        scratch_shapes=[pltpu.VMEM((HD + 16, count), F32)] if last_call else [],
        compiler_params=pltpu.CompilerParams(vmem_limit_bytes=40 * 1024 * 1024),
        cost_estimate=pl.CostEstimate(
            flops=4 * count * keys * HD,
            bytes_accessed=keys * 512,
            transcendentals=count * keys,
        ),
    )(*operands)


def shards(latents, conv_w, embed_w, text_emb, wqkv, seg_ids):
    z, y, c, x = (lax.axis_index(a) for a in ("z", "y", "c", "mp"))
    place = z * 8 + y * 2 + c
    other = swap(latents)
    chip = jnp.concatenate(
        [jnp.where(c == 0, latents, other), jnp.where(c == 0, other, latents)], axis=0
    )
    moves = [(i, i - 1) for i in range(2, 64, 2)] + [(i, i + 1) for i in range(1, 62, 2)]
    payload = jnp.where(c == 0, chip[:3], chip[1:])
    beside = lax.ppermute(payload, SEQ, moves)
    seg_ids, _ = lax.optimization_barrier((seg_ids, payload))
    info = pl.pallas_call(
        locate_kernel,
        out_shape=jax.ShapeDtypeStruct((8,), jnp.int32),
        in_specs=[pl.BlockSpec(memory_space=pltpu.VMEM)],
        out_specs=pl.BlockSpec(memory_space=pltpu.SMEM),
        cost_estimate=pl.CostEstimate(flops=0, bytes_accessed=8 << 20, transcendentals=0),
    )(seg_ids.reshape(64, 128))
    beside, info = lax.optimization_barrier((beside, info))
    below = swap(beside[:1])

    pieces = embed_pieces(embed_w, c)

    rows = jnp.where(
        c == 0,
        jnp.concatenate([beside[2:], chip, below], axis=0),
        jnp.concatenate([chip[1:], beside], axis=0),
    )
    conv = lax.conv_general_dilated(
        rows[None],
        conv_w,
        (1, 1),
        ((0, 0), (1, 1)),
        dimension_numbers=("NHWC", "HWIO", "NHWC"),
        preferred_element_type=F32,
    )[0]
    own = lax.dynamic_slice_in_dim(rows[1:5], x * 64, 64, 2)
    mixed = (own.astype(F32) + jax.nn.silu(conv)).astype(BF)
    pair = mixed.reshape(2, 2, 64, 2, 64).transpose(0, 2, 1, 3, 4).reshape(TOK, 256)
    unit = info[5]

    rows = spread_patches(pair, unit)
    own_w = call(
        block_kernel, jax.ShapeDtypeStruct((512, 128), BF), [tied(info, rows)] + pieces
    )
    own_x = swap(own_w)
    both = jnp.concatenate([own_w, own_x], axis=0)
    near_1, near_2 = along(both, 1), along(both, 2)
    rows, _ = lax.optimization_barrier((rows, both))
    placed = shift_patches(rows, unit)
    near_2, placed = lax.optimization_barrier((near_2, placed))
    patches = [placed] + [shift(placed, "mp", -t) for t in (1, 2, 3)]
    far_3, far_4 = along(near_2, 1), along(near_2[:512], 2)
    blocks, patches = lax.optimization_barrier(((near_1, near_2, far_3, far_4), patches))
    operands = [info, text_emb, *patches, own_w, own_x]
    for block in blocks:
        operands += [block, swap(block)]
    hidden = call(
        hidden_kernel, jax.ShapeDtypeStruct((TOK, 1024), BF), operands, 2 * TOK * 1024 * 1024
    )

    carry = project(info, hidden, wqkv)
    parts = [carry[0]] + [shift(carry[t], "y", t) for t in (1, 2, 3)]
    head = jnp.concatenate(parts, axis=0)
    other = swap(head)

    queries = jnp.concatenate([head[:, :HD], other[:, :HD]], axis=0)
    group = [(head[:, HD:], 0, True)]
    pair = (along(head[:, HD:], 1), along(other[:, HD:], 1))
    carry = None
    for step in range(1, 4):
        carry = attend(info, queries, group, carry, False)
        group, sent = [], []
        for block, own in zip(pair, (True, False)):
            block, carry = lax.optimization_barrier((block, carry))
            if own or step < 3:
                sent.append(along(block, 1))
            group.append((block, -step, own))
        pair = sent
    carry = attend(info, queries, group, carry, False)
    last, carry = lax.optimization_barrier((pair[0], carry))
    mine, other = attend(info, queries, [(last, -4, True)], carry, True)
    carry = call(
        merge_kernel, jax.ShapeDtypeStruct((NY * TOK, HD), BF), [info, mine, swap(other)]
    )
    back = [carry[:TOK]]
    for t in range(1, NY):
        back.append(shift(carry[t * TOK : (t + 1) * TOK], "y", -t))
    return ordered(back, y).transpose(1, 0, 2).reshape(TOK, 4 * HD)


def solution(mesh):
    inner = Mesh(mesh.devices.reshape(NZ, NY, NC, NX), ("z", "y", "c", "mp"))
    return jax.shard_map(
        shards,
        mesh=inner,
        in_specs=(
            P(SEQ, None, None),
            P(None, None, None, "mp"),
            P(None, "mp", SEQ),
            P(SEQ, "mp"),
            P(None, None, "mp"),
            P(),
        ),
        out_specs=P(SEQ, "mp"),
        check_vma=False,
    )
```

```python
import functools
import itertools
import math

import jax
import jax.numpy as jnp
from jax import lax
from jax.experimental import pallas as pl
from jax.experimental.pallas import tpu as pltpu
from jax.sharding import Mesh
from jax.sharding import PartitionSpec as P

NZ, NY, NC, NX = 8, 4, 2, 4
HD = 128
TOK = 128
IMG = 4096
SEQ = ("z", "y", "c")
SIZES = {"z": NZ, "y": NY, "c": NC, "mp": NX}
BF = jnp.bfloat16
F32 = jnp.float32


def shift(value, axis, step):
    count = SIZES[axis]
    return lax.ppermute(value, axis, [(i, (i + step) % count) for i in range(count)])


def ordered(pieces, first):
    count = len(pieces)
    twice = jnp.stack(pieces + pieces)
    return lax.dynamic_slice_in_dim(twice, (count - first) & (count - 1), count, 0)


def tied(info, other):
    return lax.optimization_barrier((info, other))[0]


def along(value, step):
    perm = []
    for z in range(NZ):
        perm.append((z * 2, (z + step) % NZ * 2))
        perm.append((z * 2 + 1, (z - step) % NZ * 2 + 1))
    return lax.ppermute(value, ("z", "c"), perm)


def swap(value):
    return shift(value, "c", 1)


def call(kernel, out_shape, operands, flops=0, limit=40):
    vmem = pl.BlockSpec(memory_space=pltpu.VMEM)
    size = sum(a.size * a.dtype.itemsize for a in operands)
    return pl.pallas_call(
        kernel,
        out_shape=out_shape,
        in_specs=[pl.BlockSpec(memory_space=pltpu.SMEM)] + [vmem] * (len(operands) - 1),
        out_specs=jax.tree.map(lambda _: vmem, out_shape),
        compiler_params=pltpu.CompilerParams(vmem_limit_bytes=limit * 1024 * 1024),
        cost_estimate=pl.CostEstimate(flops=flops, bytes_accessed=size, transcendentals=0),
    )(*operands)


def block_kernel(info, p0, p1, out):
    odd = lax.rem(info[1], 2)
    first = jnp.where(odd == 0, p0[...], p1[...])
    second = jnp.where(odd == 0, p1[...], p0[...])
    for a, value in enumerate((first, second)):
        for half in range(2):
            row = a * 256 + half * 128
            low = half * 64
            out[row : row + 128, :] = jnp.concatenate(
                [value[:, low : low + 64], value[:, 128 + low : 192 + low]], axis=1
            )


def flat(y, c, x):
    return (y * NC + c) * NX + x


def embed_pieces(embed_w, c):
    cells = embed_w.reshape(2, 128, 64)
    packed = jnp.concatenate([cells[0], cells[1]], axis=1)
    other = swap(packed)
    both = jnp.concatenate(
        [jnp.where(c == 0, packed, other), jnp.where(c == 0, other, packed)], axis=1
    )
    pieces = []
    for k in range(2):
        perm = []
        for y, c, x in itertools.product(range(NY), range(NC), range(NX)):
            to = ((2 * c + k + x % 2) % NY, x // 2, y)
            perm.append((flat(y, c, x), flat(*to)))
        pieces.append(lax.ppermute(both, ("y", "c", "mp"), perm))
    return pieces


OFFSETS = (0, -1, 1, -2, 2, -3, 3, 4)


def hidden_kernel(info, text, p0, p1, p2, p3, own, own_x, d1, x1, d2, x2, d3, x3, d4, x4, out):
    z, y, c, x, start = info[0], info[1], info[2], info[3], info[4]
    pieces = [p0[...], p1[...], p2[...], p3[...]]
    base = (z * 8 + y * 2 + c) * TOK
    late = base - start == -64
    pos = base + lax.broadcasted_iota(jnp.int32, (TOK, 128), 0)
    is_text = (pos < start) | (pos >= start + IMG)

    def features(m):
        t = lax.rem(m - x + NX, NX)
        value = pieces[0]
        for i in range(1, NX):
            value = jnp.where(t == i, pieces[i], value)
        return jnp.where(late, jnp.concatenate([value[64:], value[:64]], axis=0), value)

    mine = jnp.concatenate([features(2 * c), features(2 * c + 1)], axis=1)
    other = jnp.concatenate([features(2 - 2 * c), features(3 - 2 * c)], axis=1)
    pairs = [
        (own[...], own_x[...]),
        (d1[:512, :], d1[512:, :]),
        (x1[512:, :], x1[:512, :]),
        (d2[:512, :], d2[512:, :]),
        (x2[512:, :], x2[:512, :]),
        (d3[:512, :], d3[512:, :]),
        (x3[512:, :], x3[:512, :]),
        (d4[...], x4[...]),
    ]
    for at, (first, second) in enumerate(pairs):
        part = jnp.dot(mine, first, preferred_element_type=F32)
        part = part + jnp.dot(other, second, preferred_element_type=F32)
        place = lax.rem(z + OFFSETS[at] * (1 - 2 * c) + NZ, NZ)
        cols = pl.ds(pl.multiple_of(place * 128, 128), 128)
        out[:, cols] = jnp.where(is_text, text[:, cols], part.astype(BF))


ARRIVALS = (0, 1, 3, 2)


def qkv_add(t, info, hidden, weights, before, out):
    z, y, c, x, start = info[0], info[1], info[2], info[3], info[4]
    base = (z * 8 + y * 2 + c) * TOK
    text_0 = (base < start) | (base >= start + IMG)
    text_1 = (base + 64 < start) | (base + 64 >= start + IMG)
    group = lax.rem(x + t, NX)

    def text(j):
        return jnp.dot(hidden[...], weights[t][j], preferred_element_type=F32)

    def image(j):
        total = 0.0
        for r, weight in enumerate(weights):
            quarter = lax.rem(x + r, NX)
            for h in range(2):
                col = pl.multiple_of((2 * quarter + h) * 128, 128)
                row = pl.multiple_of(h * 512 + group * 128, 128)
                total = total + jnp.dot(
                    hidden[:, pl.ds(col, 128)],
                    weight[j, pl.ds(row, 128), :],
                    preferred_element_type=F32,
                )
        return total

    def both(j):
        first = lax.broadcasted_iota(jnp.int32, (TOK, 512), 0) < 64
        return jnp.where(first == text_0, text(j), image(j))

    def add(product):
        for j in range(3):
            cols = slice(j * 512, (j + 1) * 512)
            value = product(j)
            out[:, cols] = value if before is None else before[:, cols] + value

    pl.when(text_0 & text_1)(lambda: add(text))
    pl.when(jnp.logical_not(text_0 | text_1))(lambda: add(image))
    pl.when(text_0 != text_1)(lambda: add(both))


def qkv_first(info, hidden, wqkv, total, w0, w1, w2, w3, sems):
    x = info[3]
    weights = (w0, w1, w2, w3)
    copies = []
    for t in range(NX):
        for j in range(3):
            for h in range(4):
                row = lax.rem(x + t, NX) * 1024 + h * 256
                copies.append(
                    pltpu.make_async_copy(
                        wqkv.at[j, pl.ds(pl.multiple_of(row, 256), 256), :],
                        weights[t].at[j, pl.ds(h * 256, 256), :],
                        sems.at[t * 12 + j * 4 + h],
                    )
                )
    for copy in copies:
        copy.start()
    for copy in copies:
        copy.wait()
    qkv_add(0, info, hidden, weights, None, total)


def qkv_next(t, info, hidden, w0, w1, w2, w3, carry, out):
    qkv_add(t, info, hidden, (w0, w1, w2, w3), carry, out)


def qkv_last(t, info, hidden, w0, w1, w2, w3, carry, o0, o1, o2, o3, total):
    qkv_add(t, info, hidden, (w0, w1, w2, w3), carry, total)
    for k, out in enumerate((o0, o1, o2, o3)):
        head = lax.rem(info[1] + k, NY)
        for j in range(3):
            value = total[:, pl.ds(pl.multiple_of(j * 512 + head * 128, 128), 128)]
            out[:, j * 128 : (j + 1) * 128] = value.astype(BF)


def project(info, hidden, wqkv):
    vmem = pl.BlockSpec(memory_space=pltpu.VMEM)
    smem = pl.BlockSpec(memory_space=pltpu.SMEM)
    weight = jax.ShapeDtypeStruct((3, 1024, 512), BF)
    total = jax.ShapeDtypeStruct((TOK, 1536), F32)
    flops = 2 * TOK * 1024 * 1536
    carry, *weights = pl.pallas_call(
        qkv_first,
        out_shape=[total] + [weight] * NX,
        in_specs=[smem, vmem, pl.BlockSpec(memory_space=pl.ANY)],
        out_specs=[vmem] * (1 + NX),
        scratch_shapes=[pltpu.SemaphoreType.DMA((48,))],
        compiler_params=pltpu.CompilerParams(vmem_limit_bytes=32 * 1024 * 1024),
        cost_estimate=pl.CostEstimate(
            flops=flops, bytes_accessed=24 << 20, transcendentals=0
        ),
    )(info, hidden, jnp.transpose(wqkv, (1, 0, 2)))
    after, before = shift(hidden, "mp", -1), shift(hidden, "mp", 1)
    after, before, carry = lax.optimization_barrier((after, before, carry))
    moves = []
    for x in range(NX):
        moves.append((x, (x - 1) % NX))
        moves.append((NX + x, NX + (x + 1) % NX))
    relayed = lax.ppermute(jnp.where(lax.axis_index("c") == 0, after, before), ("c", "mp"), moves)
    arrived = {1: after, 3: before, 2: relayed}
    for t in ARRIVALS[1:]:
        last = t == 2
        head = jax.ShapeDtypeStruct((TOK, 3 * HD), BF)
        carry = pl.pallas_call(
            functools.partial(qkv_last if last else qkv_next, t),
            out_shape=[head] * NY if last else total,
            in_specs=[smem] + [vmem] * (2 + NX),
            out_specs=[vmem] * NY if last else vmem,
            scratch_shapes=[pltpu.VMEM((TOK, 1536), F32)] if last else [],
            compiler_params=pltpu.CompilerParams(vmem_limit_bytes=24 * 1024 * 1024),
            cost_estimate=pl.CostEstimate(
                flops=flops, bytes_accessed=5 << 20, transcendentals=0
            ),
        )(info, arrived[t], *weights, carry)
    return carry


def spread_patches(pair, unit):
    def spread(low_shift, parity):
        moves = [(s, 16 + low_shift + (s + parity) // 2) for s in range(parity, 64, 2)]
        if parity:
            moves.append((0, 16 + low_shift))
        return lambda rows: lax.ppermute(rows, SEQ, moves)

    return lax.switch(unit & 7, [spread(i // 2, i % 2) for i in range(8)], pair)


def shift_patches(rows, unit):
    def moved(high):
        if high == 0:
            return lambda rows: rows
        moves = [(s, s + 4 * high) for s in range(64) if 0 <= s + 4 * high < 64]
        return lambda rows: lax.ppermute(rows, SEQ, moves)

    return lax.switch(lax.shift_right_logical(unit, 3), [moved(i - 4) for i in range(9)], rows)


FACTOR = HD**-0.5 * math.log2(math.e)


def attend_kernel(cores, offset, first_call, last_call, info, queries, *refs):
    z, y, c, start = info[0], info[1], info[2], info[4]
    kv_refs = refs[: len(cores)]
    rest = refs[len(cores) :]
    count = queries.shape[0]
    state = rest[-1]
    if first_call:
        before = None
    else:
        before, rest = rest[0], rest[1:]
    zone = lax.rem(z + offset * (1 - 2 * c) + NZ, NZ)
    no_image = (z * 1024 + 1024 <= start) | (z * 1024 >= start + IMG)
    all_image = (z * 1024 >= start) & (z * 1024 + 1024 <= start + IMG)
    full = (zone < z) | (all_image & (zone * 1024 + 1024 <= start + IMG))
    empty = (zone > z) & (no_image | (zone * 1024 >= start + IMG))

    def limits():
        lanes = lax.broadcasted_iota(jnp.int32, (1, TOK), 1)
        found = []
        for core in (c, 1 - c):
            for j in range(NY):
                pos = z * 1024 + lax.rem(y - j + NY, NY) * 256 + core * TOK + lanes
                inside = (pos >= start) & (pos < start + IMG)
                found.append(jnp.where(inside, start + (IMG - 1), pos))
        return jnp.concatenate(found, axis=1)

    def add(masked):
        if masked:
            limit = limits()
            rows = lax.broadcasted_iota(jnp.int32, (TOK, count), 0)
        found = []
        for kv_ref, own_core in zip(kv_refs, cores):
            scores = lax.dot_general(
                kv_ref[:, :HD],
                queries[...],
                (((1,), (1,)), ((), ())),
                preferred_element_type=F32,
            )
            if masked:
                core = c if own_core else 1 - c
                parts = []
                for j in range(NY):
                    base = zone * 1024 + lax.rem(y - j + NY, NY) * 256 + core * TOK
                    visible = rows <= limit - base
                    parts.append(jnp.where(visible, scores[j * TOK : (j + 1) * TOK], -1e30))
                scores = jnp.concatenate(parts, axis=0)
            found.append(scores)
        if before is None:
            top = jnp.full((1, count), -1e30, F32)
        else:
            top = before[0:1, :]
        higher = top
        for scores in found:
            higher = jnp.maximum(higher, jnp.max(scores, axis=0, keepdims=True))
        total, acc = 0.0, 0.0
        if before is not None:
            fade = jnp.exp2((top - higher) * FACTOR)
            total, acc = before[8:9, :] * fade, before[16:, :] * fade
        for kv_ref, scores in zip(kv_refs, found):
            weights = jnp.exp2((scores - higher) * FACTOR)
            total = total + jnp.sum(weights, axis=0, keepdims=True)
            acc = acc + lax.dot_general(
                kv_ref[:, HD:],
                weights.astype(BF),
                (((0,), (0,)), ((), ())),
                preferred_element_type=F32,
            )
        state[0:8, :] = jnp.broadcast_to(higher, (8, count))
        state[8:16, :] = jnp.broadcast_to(total, (8, count))
        state[16:, :] = acc

    pl.when(full)(functools.partial(add, False))
    pl.when(jnp.logical_not(full | empty))(functools.partial(add, True))
    if before is not None:

        @pl.when(empty)
        def _():
            state[...] = before[...]

    if last_call:
        rest[0][...] = state[:, : count // 2]
        rest[1][...] = state[:, count // 2 :]


def merge_kernel(info, mine, other, out):
    higher = jnp.maximum(mine[0:1, :], other[0:1, :])
    fade = jnp.exp2((mine[0:1, :] - higher) * FACTOR)
    fade_x = jnp.exp2((other[0:1, :] - higher) * FACTOR)
    total = mine[8:9, :] * fade + other[8:9, :] * fade_x
    acc = mine[16:, :] * fade + other[16:, :] * fade_x
    out[...] = (acc / total).T.astype(BF)


def attend(info, queries, group, carry, last_call):
    arrays = [array for array, _, _ in group]
    cores = [own for _, _, own in group]
    operands = [info, queries] + arrays + ([] if carry is None else [carry])
    vmem = pl.BlockSpec(memory_space=pltpu.VMEM)
    count = queries.shape[0]
    keys = sum(a.shape[0] for a in arrays)
    if last_call:
        out = [jax.ShapeDtypeStruct((HD + 16, count // 2), F32)] * 2
    else:
        out = jax.ShapeDtypeStruct((HD + 16, count), F32)
    return pl.pallas_call(
        functools.partial(attend_kernel, cores, group[0][1], carry is None, last_call),
        out_shape=out,
        in_specs=[pl.BlockSpec(memory_space=pltpu.SMEM)] + [vmem] * (len(operands) - 1),
        out_specs=[vmem] * 2 if last_call else vmem,
        scratch_shapes=[pltpu.VMEM((HD + 16, count), F32)] if last_call else [],
        compiler_params=pltpu.CompilerParams(vmem_limit_bytes=40 * 1024 * 1024),
        cost_estimate=pl.CostEstimate(
            flops=4 * count * keys * HD,
            bytes_accessed=keys * 512,
            transcendentals=count * keys,
        ),
    )(*operands)


def shards(latents, conv_w, embed_w, text_emb, wqkv, seg_ids):
    z, y, c, x = (lax.axis_index(a) for a in ("z", "y", "c", "mp"))
    place = z * 8 + y * 2 + c
    other = swap(latents)
    chip = jnp.concatenate(
        [jnp.where(c == 0, latents, other), jnp.where(c == 0, other, latents)], axis=0
    )
    moves = [(i, i - 1) for i in range(2, 64, 2)] + [(i, i + 1) for i in range(1, 62, 2)]
    payload = jnp.where(c == 0, chip[:3], chip[1:])
    beside = lax.ppermute(payload, SEQ, moves)
    seg_ids, _ = lax.optimization_barrier((seg_ids, payload))
    positions = jnp.arange(seg_ids.shape[0], dtype=jnp.int32)
    start = jnp.min(jnp.where(seg_ids == 1, positions, seg_ids.shape[0])).astype(jnp.int32)
    info = jnp.stack([z, y, c, x, start]).astype(jnp.int32)
    beside, info = lax.optimization_barrier((beside, info))
    below = swap(beside[:1])

    pieces = embed_pieces(embed_w, c)

    rows = jnp.where(
        c == 0,
        jnp.concatenate([beside[2:], chip, below], axis=0),
        jnp.concatenate([chip[1:], beside], axis=0),
    )
    conv = lax.conv_general_dilated(
        rows[None],
        conv_w,
        (1, 1),
        ((0, 0), (1, 1)),
        dimension_numbers=("NHWC", "HWIO", "NHWC"),
        preferred_element_type=F32,
    )[0]
    own = lax.dynamic_slice_in_dim(rows[1:5], x * 64, 64, 2)
    mixed = (own.astype(F32) + jax.nn.silu(conv)).astype(BF)
    pair = mixed.reshape(2, 2, 64, 2, 64).transpose(0, 2, 1, 3, 4).reshape(TOK, 256)
    unit = lax.shift_right_logical(start, 6)

    rows = spread_patches(pair, unit)
    own_w = call(
        block_kernel, jax.ShapeDtypeStruct((512, 128), BF), [tied(info, rows)] + pieces
    )
    own_x = swap(own_w)
    both = jnp.concatenate([own_w, own_x], axis=0)
    near_1, near_2 = along(both, 1), along(both, 2)
    rows, _ = lax.optimization_barrier((rows, both))
    placed = shift_patches(rows, unit)
    near_2, placed = lax.optimization_barrier((near_2, placed))
    patches = [placed] + [shift(placed, "mp", -t) for t in (1, 2, 3)]
    far_3, far_4 = along(near_2, 1), along(near_2[:512], 2)
    blocks, patches = lax.optimization_barrier(((near_1, near_2, far_3, far_4), patches))
    operands = [info, text_emb, *patches, own_w, own_x]
    for block in blocks:
        operands += [block, swap(block)]
    hidden = call(
        hidden_kernel, jax.ShapeDtypeStruct((TOK, 1024), BF), operands, 2 * TOK * 1024 * 1024
    )

    carry = project(info, hidden, wqkv)
    parts = [carry[0]] + [shift(carry[t], "y", t) for t in (1, 2, 3)]
    head = jnp.concatenate(parts, axis=0)
    other = swap(head)

    queries = jnp.concatenate([head[:, :HD], other[:, :HD]], axis=0)
    group = [(head[:, HD:], 0, True)]
    pair = (along(head[:, HD:], 1), along(other[:, HD:], 1))
    carry = None
    for step in range(1, 4):
        carry = attend(info, queries, group, carry, False)
        group, sent = [], []
        for block, own in zip(pair, (True, False)):
            block, carry = lax.optimization_barrier((block, carry))
            if own or step < 3:
                sent.append(along(block, 1))
            group.append((block, -step, own))
        pair = sent
    carry = attend(info, queries, group, carry, False)
    last, carry = lax.optimization_barrier((pair[0], carry))
    mine, other = attend(info, queries, [(last, -4, True)], carry, True)
    carry = call(
        merge_kernel, jax.ShapeDtypeStruct((NY * TOK, HD), BF), [info, mine, swap(other)]
    )
    back = [carry[:TOK]]
    for t in range(1, NY):
        back.append(shift(carry[t * TOK : (t + 1) * TOK], "y", -t))
    return ordered(back, y).transpose(1, 0, 2).reshape(TOK, 4 * HD)


def solution(mesh):
    inner = Mesh(mesh.devices.reshape(NZ, NY, NC, NX), ("z", "y", "c", "mp"))
    return jax.shard_map(
        shards,
        mesh=inner,
        in_specs=(
            P(SEQ, None, None),
            P(None, None, None, "mp"),
            P(None, "mp", SEQ),
            P(SEQ, "mp"),
            P(None, None, "mp"),
            P(),
        ),
        out_specs=P(SEQ, "mp"),
        check_vma=False,
    )
```
